32 devices in a mesh: wave: 4 (over z), lev: 8 (over y, x, core).
Axes of the slice: x: 2, y: 2, z: 4, core: 2. Of those that a mesh axis runs over, the one named last changes fastest.
Arguments:
- spec: bfloat16 [8, 8, 2, 1280], P('wave', 'lev'), may hold values from -0.59765625 to 0.59765625
- legendre: bfloat16 [8, 1280, 1200], P('wave', 'lev'), may hold values from -0.15625 to 0.15625
- gauss_w: float32 [1200], replicated, may hold values from 0.5 to 1.5
- cycle_len: int32 [1200], replicated, may hold values from 20 to 4816, as said below
- wave_map: int32 [8], replicated, may hold values from 0 to 7, as said below
Outputs:
- grid: bfloat16 [2, 600, 8, 4864], P(None, 'wave', 'lev')
- spec_out: float32 [8, 8, 2, 1280], P('wave', 'lev')
The draws below stay inside these ranges and needn't reach their ends.
Inputs may be any that keep to these rules, and one draw needn't show every extreme that they name: `wave_map`: A permutation of 0 .. 7; slot r of each index of wave (slots are numbered 2 to an index) holds a value from the r-th group of 4 consecutive values. `cycle_len`: entry 2r is the point count of the r-th cycle from the pole, entry 2r + 1 that of cycle 1200 - 1 - r; cycle j has a multiple of 4 points between max(20, 8 + 4 j) and 20 + 4 j, and cycle 1200 - 1 exactly 20 + 4 (1199); the southern cycle mirrors the northern one.
All inputs are finite; a program needn't handle non-finite values.
Results may differ from the reference program's by a relative error of at most 0.0055.
Values may be sent and summed in bfloat16 or wider, within the bound.
No kernel may reach another device: no remote copies, remote signals or barrier semaphores. Data moves between devices by JAX's collectives and lax.ppermute only.
A program may use at most 64 MiB of HBM per device.

```python
import math
import jax
import jax.numpy as jnp
from jax import lax

NN = 1280
NH = 1200
M_DEV = 2
MW = 8
FIELDS = 8
LPAD = 4864
N_WAVE = 4


def draw_wave_map(key, part):
    shuffled = jax.random.permutation(jax.random.fold_in(key, 11), N_WAVE)
    slot_ids = jnp.arange(MW, dtype=jnp.int32)
    holder = slot_ids // M_DEV
    rounds = slot_ids % M_DEV
    placed = shuffled[holder]
    within = jnp.where(rounds % 2 == 0, placed, N_WAVE - 1 - placed)
    return (rounds * N_WAVE + within).astype(jnp.int32)


def draw_cycle_len(key, part):
    packed = jnp.arange(NH, dtype=jnp.int32)
    row_ids = packed // 2
    latitude = jnp.where(packed % 2 == 0, row_ids, NH - 1 - row_ids)
    reduction = jax.random.randint(jax.random.fold_in(key, 23), (NH,), 0, 4)
    reduction = jnp.where(latitude == NH - 1, 0, reduction)
    return jnp.maximum(20, 20 + 4 * latitude - 4 * reduction).astype(jnp.int32)


def steps_of(stream_key, shape, shards, low, high):
    def one(dim, blocks):
        steps = jax.random.uniform(jax.random.fold_in(jax.random.fold_in(stream_key, 6), dim), (blocks,), jnp.float32, low / len(shards), high / len(shards))
        return jnp.repeat(jnp.exp(steps), shape[dim] // blocks).reshape((-1,) + (1,) * (len(shape) - dim - 1))

    factor_of = one(*shards[0])
    for cut in shards[1:]:
        factor_of = factor_of * one(*cut)
    return factor_of


def gaussian(rng, extent, scale, bound, shards=(), kind=jnp.bfloat16):
    level = steps_of(rng, extent, shards, -0.22, 0.18) if shards else 1.0
    result = jax.random.normal(rng, extent, jnp.float32) * scale * level
    return jnp.minimum(jnp.maximum(result, -bound), bound).astype(kind)


def setup_inputs(seed: int = 0) -> dict:
    splits = jax.random.split(jax.random.key(seed), 6)
    return {
        "spec": gaussian(splits[0], (MW, FIELDS, 2, NN), 0.1, 0.59765625, ((0, 4), (1, 8))),
        "legendre": gaussian(splits[1], (MW, NN, NH), NN ** -0.5, 0.15625, ((0, 4), (1, 8))),
        "gauss_w": jnp.clip(jax.random.uniform(splits[2], (NH,), jnp.float32, 0.5, 1.5), 0.5, 1.5),
        "cycle_len": draw_cycle_len(jax.random.fold_in(splits[5], 71), 0),
        "wave_map": draw_wave_map(jax.random.fold_in(splits[5], 71), 0),
    }


def block_rows(row_total):
    for candidate in (10, 8, 6, 5, 4, 3, 2):
        if row_total % candidate == 0:
            return candidate
    return 1


def cycle_tables(lens_pair, orders, padded):
    position = jnp.arange(padded, dtype=jnp.int32)[None, :]
    first_len = lens_pair[:, 0:1]
    second = lens_pair[:, 1:2]
    upper_half = position >= first_len
    occupied = position < first_len + second
    offset = jnp.where(upper_half, position - first_len, position)
    length = jnp.where(upper_half, second, first_len)
    turn_count = (orders[None, :, None] * offset[:, None, :]) % length[:, None, :]
    angles = (2.0 * math.pi) * turn_count.astype(jnp.float32) / length[:, None, :].astype(jnp.float32)
    cosine = jnp.where(occupied[:, None, :], jnp.cos(angles), 0.0).astype(jnp.bfloat16)
    minus_sine = jnp.where(occupied[:, None, :], -jnp.sin(angles), 0.0).astype(jnp.bfloat16)
    return jnp.concatenate([cosine, minus_sine], 1), upper_half, occupied


def cycle_block(waves, lens_pair, weights, orders, padded):
    row_count = waves.shape[0]
    fields = waves.shape[3]
    slot_count = orders.shape[0]
    tables, upper_half, occupied = cycle_tables(lens_pair, orders, padded)
    double = jnp.where(orders == 0, 1.0, 2.0)
    resolved = 2 * orders[None, None, :] < lens_pair[:, :, None]
    widening = jnp.where(resolved, double[None, None, :], 0.0)
    scaled = (waves.astype(jnp.float32) * widening[:, None, :, None, None, :]).astype(jnp.bfloat16)
    scaled = scaled.reshape(row_count, 4 * fields, 2 * slot_count)
    images = jnp.einsum("rak,rkp->rap", scaled.astype(jnp.float32), tables.astype(jnp.float32))
    images = images.reshape(row_count, 2, 2, fields, padded)
    values = jnp.where(upper_half[:, None, None, :], images[:, :, 1], images[:, :, 0])
    values = jnp.where(occupied[:, None, None, :], values, 0.0).astype(jnp.bfloat16)
    squared = (values.astype(jnp.float32) * values.astype(jnp.float32)).astype(jnp.bfloat16)
    selector = jnp.stack([jnp.logical_not(upper_half), upper_half], 1)
    by_cycle = jnp.where(selector[:, None, :, None, :], squared[:, :, None, :, :].astype(jnp.float32), 0.0)
    by_cycle = by_cycle.reshape(row_count, 4 * fields, padded)
    returned = jnp.einsum("rap,rkp->rak", by_cycle, tables.astype(jnp.float32))
    returned = returned.reshape(row_count, 2, 2, fields, 2, slot_count)
    factor = jnp.where(resolved, weights[:, :, None] / lens_pair[:, :, None].astype(jnp.float32), 0.0)
    returned = (returned * factor[:, None, :, None, None, :]).astype(jnp.bfloat16)
    return values, returned


def legendre_inverse(spec, legendre, orders):
    degrees = jnp.arange(NN, dtype=jnp.int32)

    def one_slot(operands):
        coefficients, panel, order = operands
        retained = jnp.where(degrees[None, None, :] >= order, coefficients.astype(jnp.float32), 0.0)
        parity = jnp.where((degrees + order) % 2 == 0, 1.0, -1.0)
        panel_wide = panel.astype(jnp.float32)
        north = jnp.einsum("fcn,nq->fcq", retained, panel_wide)
        south = jnp.einsum("fcn,nq->fcq", retained * parity[None, None, :], panel_wide)
        return jnp.stack([north, south], 0).astype(jnp.bfloat16)

    return lax.map(one_slot, (spec, legendre, orders))


def legendre_direct(returned, legendre, orders):
    degrees = jnp.arange(NN, dtype=jnp.int32)

    def one_slot(operands):
        fourier, panel, order = operands
        both = jnp.einsum("hfcq,nq->hfcn", fourier.astype(jnp.float32), panel.astype(jnp.float32))
        parity = jnp.where((degrees + order) % 2 == 0, 1.0, -1.0)
        total = both[0] + parity[None, None, :] * both[1]
        return jnp.where(degrees[None, None, :] >= order, total, 0.0)

    return lax.map(one_slot, (returned, legendre, orders))


def reference(spec, legendre, gauss_w, cycle_len, wave_map):
    orders = ((wave_map * NN) // MW).astype(jnp.int32)
    fourier = legendre_inverse(spec, legendre, orders)
    row_total = NH // 2
    row_block = block_rows(row_total)
    blocks = row_total // row_block
    ordered = fourier.reshape(MW, 2, FIELDS, 2, row_total, 2).transpose(4, 1, 5, 2, 3, 0)
    ordered = ordered.reshape(blocks, row_block, 2, 2, FIELDS, 2, MW)

    def run_block(operands):
        return cycle_block(operands[0], operands[1], operands[2], orders, LPAD)

    values, returned = lax.map(run_block, (ordered, cycle_len.reshape(blocks, row_block, 2), gauss_w.reshape(blocks, row_block, 2)))
    grid = values.reshape(row_total, 2, FIELDS, LPAD).transpose(1, 0, 2, 3)
    returned = returned.reshape(row_total, 2, 2, FIELDS, 2, MW).transpose(5, 1, 3, 4, 0, 2).reshape(MW, 2, FIELDS, 2, NH)
    spec_out = legendre_direct(returned, legendre, orders)
    return grid, spec_out
```

```python
import functools
import math

import jax
import jax.numpy as jnp
from jax import lax
from jax.experimental import pallas as pl
from jax.experimental.layout import Layout, with_layout_constraint
from jax.experimental.pallas import tpu as pltpu
from jax.sharding import PartitionSpec as P

LPAD = 4864


def block_rows():
    for candidate in (10, 8, 6, 5, 4, 3, 2):
        return candidate
    return 1


def cycle_tables(lens_pair, orders, padded):
    position = jnp.arange(padded, dtype=jnp.int32)[None, :]
    first_len = lens_pair[:, 0:1]
    second = lens_pair[:, 1:2]
    upper_half = position >= first_len
    occupied = position < first_len + second
    offset = jnp.where(upper_half, position - first_len, position)
    length = jnp.where(upper_half, second, first_len)
    turn_count = orders[None, :, None] * offset[:, None, :] % length[:, None, :]
    angles = 2.0 * math.pi * turn_count.astype(jnp.float32) / length[:, None, :].astype(jnp.float32)
    cosine = jnp.where(occupied[:, None, :], jnp.cos(angles), 0.0).astype(jnp.bfloat16)
    minus_sine = jnp.where(occupied[:, None, :], -jnp.sin(angles), 0.0).astype(jnp.bfloat16)
    return (jnp.concatenate([cosine, minus_sine], 1), upper_half, occupied)


def cycle_block(waves, lens_pair, weights, orders, padded):
    row_count = waves.shape[0]
    fields = waves.shape[3]
    slot_count = orders.shape[0]
    tables, upper_half, occupied = cycle_tables(lens_pair, orders, padded)
    double = jnp.where(orders == 0, 1.0, 2.0)
    resolved = 2 * orders[None, None, :] < lens_pair[:, :, None]
    widening = jnp.where(resolved, double[None, None, :], 0.0)
    scaled = (waves.astype(jnp.float32) * widening[:, None, :, None, None, :]).astype(jnp.bfloat16)
    scaled = scaled.reshape(row_count, 4 * fields, 2 * slot_count)
    images = jnp.einsum("rak,rkp->rap", scaled, tables, preferred_element_type=jnp.float32)
    images = images.reshape(row_count, 2, 2, fields, padded)
    values = jnp.where(upper_half[:, None, None, :], images[:, :, 1], images[:, :, 0])
    values = jnp.where(occupied[:, None, None, :], values, 0.0).astype(jnp.bfloat16)
    squared = (values.astype(jnp.float32) * values.astype(jnp.float32)).astype(jnp.bfloat16)
    selector = jnp.stack([jnp.logical_not(upper_half), upper_half], 1)
    by_cycle = jnp.where(
        selector[:, None, :, None, :], squared[:, :, None, :, :], jnp.zeros((), jnp.bfloat16)
    )
    by_cycle = by_cycle.reshape(row_count, 4 * fields, padded)
    returned = jnp.einsum("rap,rkp->rak", by_cycle, tables, preferred_element_type=jnp.float32)
    returned = returned.reshape(row_count, 2, 2, fields, 2, slot_count)
    factor = jnp.where(
        resolved, weights[:, :, None] / lens_pair[:, :, None].astype(jnp.float32), 0.0
    )
    returned = (returned * factor[:, None, :, None, None, :]).astype(jnp.bfloat16)
    return (values, returned)


def parity_of(degree_ids, own_orders):
    return jnp.where((degree_ids[None, :] + own_orders[:, None]) % 2 == 0, 1.0, -1.0)


def general(spec, legendre, gauss_w, cycle_len, wave_map):
    slots_dev = spec.shape[0]
    fields = spec.shape[1]
    degrees_all = spec.shape[3]
    slot_count = wave_map.shape[0]
    orders = wave_map * degrees_all // slot_count
    wave_pos = lax.axis_index("wave")
    own_orders = lax.dynamic_slice_in_dim(orders, wave_pos * slots_dev, slots_dev)
    degrees = jnp.arange(degrees_all, dtype=jnp.int32)
    retained = degrees[None, :] >= own_orders[:, None]
    coefficients = jnp.where(retained[:, None, None, :], spec, jnp.zeros((), jnp.bfloat16))
    panels = lax.all_gather(legendre, "lev", axis=1, tiled=True)
    sign_flip = parity_of(degrees, own_orders)
    flipped = (coefficients.astype(jnp.float32) * sign_flip[:, None, None, :]).astype(jnp.bfloat16)
    stacked = jnp.stack([coefficients, flipped], 1)
    fourier = jnp.einsum(
        "shfcn,snq->shfcq", stacked, panels, preferred_element_type=jnp.float32
    ).astype(jnp.bfloat16)
    cycle_waves = lax.all_to_all(fourier, "wave", split_axis=4, concat_axis=0, tiled=True)
    local_lats = cycle_waves.shape[4]
    row_total = local_lats // 2
    lat_start = wave_pos * local_lats
    lens_here = lax.dynamic_slice_in_dim(cycle_len, lat_start, local_lats)
    weights_here = lax.dynamic_slice_in_dim(gauss_w, lat_start, local_lats)
    row_block = block_rows()
    blocks = row_total // row_block
    ordered = cycle_waves.reshape(slot_count, 2, fields, 2, row_total, 2).transpose(
        4, 1, 5, 2, 3, 0
    )
    ordered = ordered.reshape(blocks, row_block, 2, 2, fields, 2, slot_count)

    def run_block(operands):
        return cycle_block(operands[0], operands[1], operands[2], orders, LPAD)

    values, returned = lax.map(
        run_block,
        (
            ordered,
            lens_here.reshape(blocks, row_block, 2),
            weights_here.reshape(blocks, row_block, 2),
        ),
    )
    grid = values.reshape(row_total, 2, fields, LPAD).transpose(1, 0, 2, 3)
    returned = returned.reshape(row_total, 2, 2, fields, 2, slot_count).transpose(5, 1, 3, 4, 0, 2)
    returned = returned.reshape(slot_count, 2, fields, 2, local_lats)
    spectral = lax.all_to_all(returned, "wave", split_axis=0, concat_axis=4, tiled=True)
    both = jnp.einsum("shfcq,snq->shfcn", spectral, panels, preferred_element_type=jnp.float32)
    total = both[:, 0] + sign_flip[:, None, None, :] * both[:, 1]
    spec_out = jnp.where(retained[:, None, None, :], total, 0.0)
    return (grid, spec_out)


LANES = 128
SUBLANES = 8
STEPS = 5
VMEM = 56 * 1024 * 1024
SINE = (6.28318516, -41.34165503, 81.60100407, -76.54978222, 39.53670553)


def cos_turns(x, period, inverse):
    turn = x - period * jnp.floor(x * inverse + 0.5)
    v = 0.25 - jnp.abs(turn * inverse)
    y = v * v
    series = SINE[4]
    for coefficient in SINE[3::-1]:
        series = series * y + coefficient
    return v * series


def params(memory=VMEM):
    return pltpu.CompilerParams(vmem_limit_bytes=memory)


def cost(flops, nbytes):
    return pl.CostEstimate(flops=flops, bytes_accessed=nbytes, transcendentals=0)


def send_spec(info, spec, levels):
    slots, parts, degrees_all = spec.shape
    own = degrees_all // levels
    rows = 2 * slots * parts

    def kernel(info_ref, x_ref, o_ref):
        degree = lax.broadcasted_iota(jnp.int32, (parts, degrees_all), 1)
        north, south = [], []
        for s in range(slots):
            order = info_ref[1 + s]
            x = jnp.where(degree >= order, x_ref[s].astype(jnp.float32), 0.0)
            sign = (1 - 2 * ((degree + order) & 1)).astype(jnp.float32)
            north.append(x)
            south.append(x * sign)
        both = jnp.concatenate(north + south, axis=0)
        slot_of = (lax.broadcasted_iota(jnp.int32, (rows, own), 0) // parts) % slots
        for j in range(levels):
            piece = both[:, j * own : (j + 1) * own]
            wide = [jnp.where(slot_of == s, piece, 0.0) for s in range(slots)]
            o_ref[j] = jnp.concatenate(wide, axis=1).astype(jnp.bfloat16)

    return pl.pallas_call(
        kernel,
        out_shape=jax.ShapeDtypeStruct((levels, rows, slots * own), jnp.bfloat16),
        in_specs=[pl.BlockSpec(memory_space=pltpu.SMEM), pl.BlockSpec(memory_space=pltpu.VMEM)],
        out_specs=pl.BlockSpec(memory_space=pltpu.VMEM),
        compiler_params=params(),
        name="send_spec",
    )(info, spec)


def partial_fourier(coefficients, panels):
    rows = coefficients.shape[0]
    chunks, depth, wide = panels.shape

    def kernel(x_ref, panel_ref, o_ref):
        for j in range(chunks):
            o_ref[j] = jnp.dot(
                x_ref[...], panel_ref[j], preferred_element_type=jnp.float32
            ).astype(jnp.bfloat16)

    return pl.pallas_call(
        kernel,
        out_shape=jax.ShapeDtypeStruct((chunks, rows, wide), jnp.bfloat16),
        compiler_params=params(),
        name="partial_fourier",
    )(coefficients, panels)


def quadratic(wave_map, parts_sum, lens, weights, waves, step):
    sources, rows, wide = parts_sum.shape
    slot_count = wave_map.shape[0]
    levels = sources // waves
    slots = slot_count // waves
    tiles = wide // LANES
    top = 2 * (slot_count - 1)
    shape = (SUBLANES, LANES)

    def kernel(map_ref, x_ref, len_ref, weight_ref, g_ref, o_ref, z_ref, r_ref, s_ref):
        z_ref[...] = jnp.zeros(z_ref.shape, jnp.float32)
        for i in range(waves):
            total = x_ref[i * levels].astype(jnp.float32)
            for j in range(1, levels):
                total = total + x_ref[i * levels + j].astype(jnp.float32)
            for row in range(rows):
                h, s, c = row // (2 * slots), row // 2 % slots, row % 2
                at = map_ref[i * slots + s] * 2 + c
                for t in range(tiles):
                    k = h * tiles + t
                    z_ref[at, k : k + 1, :] = total[row : row + 1, t * LANES : (t + 1) * LANES]
        lens_here = len_ref[...]
        kept = [
            jnp.where(lens_here > 2.0 * step * w, 1.0, 0.0) for w in range(slot_count)
        ]
        real = [z_ref[2 * w] * kept[w] for w in range(slot_count)]
        imag = [z_ref[2 * w + 1] * kept[w] for w in range(slot_count)]
        for w in range(slot_count):
            double = 1.0 if w == 0 else 2.0
            g_ref[2 * w] = real[w] * double
            g_ref[2 * w + 1] = imag[w] * double
        imag[0] = jnp.zeros(shape, jnp.float32)
        square_real, square_imag = [], []
        for n in range(top + 1):
            re, im = jnp.zeros(shape, jnp.float32), jnp.zeros(shape, jnp.float32)
            for a in range(max(0, n - slot_count + 1), (n + 1) // 2):
                b = n - a
                re = re + (real[a] * real[b] - imag[a] * imag[b])
                im = im + (real[a] * imag[b] + imag[a] * real[b])
            for b in range(1, slot_count - n):
                a = n + b
                re = re + (real[a] * real[b] + imag[a] * imag[b])
                im = im + (imag[a] * real[b] - real[a] * imag[b])
            re, im = 2.0 * re, 2.0 * im
            if n % 2 == 0:
                a = n // 2
                re = re + (real[a] * real[a] - imag[a] * imag[a])
                im = im + 2.0 * (real[a] * imag[a])
            square_real.append(re)
            square_imag.append(im)
        whole = {
            d: jnp.where(lens_here == 1.0 * step * d, 1.0, 0.0)
            for d in range(3, top + slot_count)
        }
        weights_here = weight_ref[...]
        for w in range(slot_count):
            re, im = square_real[w], square_imag[w]
            if w == 0:
                im = jnp.zeros(shape, jnp.float32)
            else:
                for n in range(w + 1, top + 1):
                    re = re + whole[w + n] * square_real[n]
                    im = im - whole[w + n] * square_imag[n]
            factor = kept[w] * weights_here
            r_ref[2 * w] = re * factor
            r_ref[2 * w + 1] = im * factor
        for i in range(waves):
            for row in range(rows):
                h, s, c = row // (2 * slots), row // 2 % slots, row % 2
                at = map_ref[i * slots + s] * 2 + c
                for t in range(tiles):
                    k = h * tiles + t
                    s_ref[row : row + 1, t * LANES : (t + 1) * LANES] = r_ref[at, k : k + 1, :]
            packed = s_ref[...].astype(jnp.bfloat16)
            for j in range(levels):
                o_ref[i * levels + j] = packed

    smem = pl.BlockSpec(memory_space=pltpu.SMEM)
    vmem = pl.BlockSpec(memory_space=pltpu.VMEM)
    return pl.pallas_call(
        kernel,
        out_shape=(
            jax.ShapeDtypeStruct((2 * slot_count,) + shape, jnp.float32),
            jax.ShapeDtypeStruct((sources, rows, wide), jnp.bfloat16),
        ),
        in_specs=[smem, vmem, vmem, vmem],
        out_specs=(vmem, vmem),
        scratch_shapes=[
            pltpu.VMEM((2 * slot_count,) + shape, jnp.float32),
            pltpu.VMEM((2 * slot_count,) + shape, jnp.float32),
            pltpu.VMEM((rows, wide), jnp.float32),
        ],
        compiler_params=params(),
        name="quadratic",
    )(wave_map, parts_sum, lens, weights)


def lane_facts(slot_count):
    lane = lax.broadcasted_iota(jnp.int32, (1, LANES), 1)
    return (
        lane % (2 * slot_count) // 2,
        lane % 2,
        lane // (2 * slot_count) % 2,
        lane // (4 * slot_count),
    )


def tile_of_row(rows, span, slot_count):
    at = lax.broadcasted_iota(jnp.int32, (rows, LANES), 0)
    at = at - lane_facts(slot_count)[3] * span % SUBLANES
    return at // 2, jnp.logical_and(at >= 0, at < span)


def phase_tables(facts, span, slot_count, step):
    groups = facts.shape[0]
    rows = -(-(span + SUBLANES // 2) // SUBLANES) * SUBLANES

    def kernel(fact_ref, p_ref, q_ref, t_ref):
        wave, part, cycle, _ = lane_facts(slot_count)
        tile, inside = tile_of_row(rows, span, slot_count)
        first = (tile * LANES).astype(jnp.float32)
        order = (step * wave).astype(jnp.float32)
        is_imag = part.astype(jnp.float32)
        point = lax.broadcasted_iota(jnp.int32, (LANES, LANES), 1).astype(jnp.float32)
        down = lax.broadcasted_iota(jnp.int32, (LANES, 1), 0)
        order_down = (step * (down % (2 * slot_count) // 2)).astype(jnp.float32)
        imag_down = (down % 2).astype(jnp.float32)
        second_down = down // (2 * slot_count) % 2 == 1

        def body(g, carry):
            fact = fact_ref[g]
            length, inverse, offset = fact[0:1], fact[1:2], fact[2:3]
            x = order * (first - offset)
            quarter = 0.25 * length
            p = cos_turns(x - is_imag * quarter, length, inverse)
            q = cos_turns(x + (1.0 - is_imag) * quarter, length, inverse)
            p_ref[g] = jnp.where(inside, p, 0.0)
            q_ref[g] = jnp.where(inside, q, 0.0)
            across = jnp.transpose(fact)
            length, inverse, split = across[:, 0:1], across[:, 1:2], across[:, 4:5]
            x = order_down * point + imag_down * (0.25 * length)
            t = cos_turns(x, length, inverse)
            t_ref[g, 0:LANES, :] = t.astype(jnp.bfloat16)
            here = jnp.logical_xor(point < split, second_down)
            t_ref[g, LANES : 2 * LANES, :] = jnp.where(here, t, 0.0).astype(jnp.bfloat16)
            return carry

        lax.fori_loop(0, groups, body, 0)

    return pl.pallas_call(
        kernel,
        out_shape=(
            jax.ShapeDtypeStruct((groups, rows, LANES), jnp.float32),
            jax.ShapeDtypeStruct((groups, rows, LANES), jnp.float32),
            jax.ShapeDtypeStruct((groups, 2 * LANES, LANES), jnp.bfloat16),
        ),
        compiler_params=params(),
        cost_estimate=cost(20 * groups * 36 * 1024, 0),
        name="phase_tables",
    )(facts)


def grid_values(ends, facts, waves, p, q, t, span, slot_count, rows_out):
    groups, rows, _ = p.shape
    per = LANES // (4 * slot_count)
    block = groups // STEPS

    def kernel(end_ref, fact_ref, wave_ref, p_ref, q_ref, t_ref, o_ref):
        _, _, cycle, _ = lane_facts(slot_count)
        tile, _ = tile_of_row(rows, span, slot_count)
        way = 1 - 2 * cycle
        tile = (tile * way).astype(jnp.float32)
        way = way.astype(jnp.float32)
        last = lax.broadcasted_iota(jnp.int32, (SUBLANES, LANES), 0) + rows - SUBLANES
        point = lax.broadcasted_iota(jnp.int32, (SUBLANES, LANES), 1)
        base = pl.program_id(0) * block

        def body(g, carry):
            fold = (rows // SUBLANES, SUBLANES, LANES)
            amplitude = wave_ref[g, 0] * p_ref[g].reshape(fold) + wave_ref[g, 1] * q_ref[g].reshape(fold)
            amplitude = amplitude.reshape(rows, LANES)
            apart = tile - way * fact_ref[g, 3:4, :]
            left = jnp.concatenate(
                [jnp.where(apart < 0.0, amplitude, 0.0), jnp.where(apart == 0.0, amplitude, 0.0)], axis=1
            ).astype(jnp.bfloat16)
            size = 4 * slot_count
            columns = []
            for r in range(per):
                before = jnp.zeros((r * size, LANES), jnp.bfloat16)
                after = jnp.zeros((LANES - (r + 1) * size, LANES), jnp.bfloat16)
                pieces = []
                for half in range(2):
                    at = half * LANES + r * size
                    pieces += [before, t_ref[g, at : at + size, :], after]
                columns.append(jnp.concatenate([x for x in pieces if x.shape[0]], axis=0))
            right = jnp.concatenate(columns, axis=1)
            product = jnp.dot(left, right, preferred_element_type=jnp.float32)
            places = {}
            for r in range(per):
                shift = r * span % SUBLANES
                values = product[:, r * LANES : (r + 1) * LANES]
                for k in range(rows // SUBLANES):
                    if k * SUBLANES >= shift + span:
                        continue
                    value = values[k * SUBLANES : (k + 1) * SUBLANES]
                    if k == rows // SUBLANES - 1:
                        position = (last - shift) // 2 * LANES + point
                        value = jnp.where(position < end_ref[(base + g) * per + r], value, 0.0)
                    places.setdefault((r * span - shift) // SUBLANES + k, []).append(value)
            whole = [functools.reduce(lambda a, b: a + b, places[k]) for k in sorted(places)]
            size_out = per * span
            o_ref[pl.ds(pl.multiple_of(g * size_out, 16), size_out), :] = jnp.concatenate(
                whole, axis=0
            ).astype(jnp.bfloat16)
            return carry

        lax.fori_loop(0, block, body, 0)

    def stepped(shape):
        return pl.BlockSpec((block,) + shape, lambda i: (i, 0, 0))

    return pl.pallas_call(
        kernel,
        grid=(STEPS,),
        out_shape=jax.ShapeDtypeStruct((rows_out * span, LANES), jnp.bfloat16),
        in_specs=[
            pl.BlockSpec(memory_space=pltpu.SMEM),
            stepped((SUBLANES, LANES)),
            pl.BlockSpec((block, 2, SUBLANES, LANES), lambda i: (i, 0, 0, 0)),
            stepped((rows, LANES)),
            stepped((rows, LANES)),
            stepped((2 * LANES, LANES)),
        ],
        out_specs=pl.BlockSpec((block * per * span, LANES), lambda i: (i, 0)),
        compiler_params=params(),
        cost_estimate=cost(20 * groups * 36 * 1024, 0),
        name="grid_values",
    )(ends, facts, waves, p, q, t)


def direct(info, returned, panels, slots, own):
    chunks, rows, _ = returned.shape
    half = slots * 2
    levels = rows // (2 * half)

    def kernel(info_ref, x_ref, panel_ref, o_ref):
        total = jnp.zeros((rows, slots * own), jnp.float32)
        for j in range(chunks):
            total = total + lax.dot_general(
                x_ref[j], panel_ref[j], (((1,), (1,)), ((), ())), preferred_element_type=jnp.float32
            )
        total = total.reshape(levels, 2 * half, slots * own)
        slot_of = lax.broadcasted_iota(jnp.int32, (levels, half, own), 1) // 2
        degree = lax.broadcasted_iota(jnp.int32, (levels, half, own), 2) + info_ref[0] * own
        result = jnp.zeros((levels, half, own), jnp.float32)
        for s in range(slots):
            order = info_ref[1 + s]
            mine = total[:, :, s * own : (s + 1) * own]
            sign = (1 - 2 * ((degree + order) & 1)).astype(jnp.float32)
            value = mine[:, :half] + sign * mine[:, half:]
            keep = jnp.logical_and(slot_of == s, degree >= order)
            result = jnp.where(keep, value, result)
        o_ref[...] = result

    return pl.pallas_call(
        kernel,
        out_shape=jax.ShapeDtypeStruct((levels, half, own), jnp.float32),
        in_specs=[pl.BlockSpec(memory_space=pltpu.SMEM)] + [pl.BlockSpec(memory_space=pltpu.VMEM)] * 2,
        out_specs=pl.BlockSpec(memory_space=pltpu.VMEM),
        compiler_params=params(),
        name="direct",
    )(info, returned, panels)


def evenly_spaced(spec, legendre, gauss_w, cycle_len, wave_map):
    slots = spec.shape[0]
    degrees_all = spec.shape[3]
    own = legendre.shape[1]
    lats = legendre.shape[2]
    slot_count = wave_map.shape[0]
    step = degrees_all // slot_count
    waves = slot_count // slots
    levels = degrees_all // own
    wave_pos = lax.axis_index("wave")
    lev_pos = lax.axis_index("lev")
    orders = lax.dynamic_slice_in_dim(wave_map * step, wave_pos * slots, slots)
    info = jnp.concatenate([lev_pos.reshape(1), orders]).astype(jnp.int32)
    rows_here = 2 * slots * 2

    sent = send_spec(info, spec.reshape(slots, 2, degrees_all), levels)
    coefficients = lax.all_to_all(sent, "lev", 0, 0, tiled=True)

    here = lats // waves
    wide = -(-here // LANES) * LANES
    tiles = wide // LANES
    panel = legendre.reshape(slots * own, lats)
    panels = jnp.stack(
        [
            jnp.pad(panel[:, i * here : (i + 1) * here], ((0, 0), (0, wide - here)))
            for i in range(waves)
        ]
    )

    lens = lax.dynamic_slice_in_dim(cycle_len, wave_pos * here, here)
    weights = lax.dynamic_slice_in_dim(gauss_w, wave_pos * here, here)
    lens = jnp.pad(lens, (0, wide - here), constant_values=4)
    weights = jnp.pad(weights, (0, wide - here))

    def both_halves(x):
        x = jnp.tile(x.reshape(tiles, LANES), (2, 1))
        return jnp.pad(x, ((0, SUBLANES - 2 * tiles), (0, 0)), constant_values=1)

    per = LANES // (4 * slot_count)
    rows_out = here // 2
    groups = -(-rows_out // (per * STEPS)) * STEPS
    span = 2 * (LPAD // LANES)
    grouped = lens[: groups * 2 * per].reshape(groups, per, 2)
    first = jnp.broadcast_to(grouped[:, :, :1], grouped.shape)
    offset = first * jnp.array([0, 1], jnp.int32)
    facts = jnp.stack(
        [
            grouped.astype(jnp.float32),
            1.0 / grouped.astype(jnp.float32),
            offset.astype(jnp.float32),
            (first // LANES).astype(jnp.float32),
            (first % LANES).astype(jnp.float32),
        ]
        + [jnp.zeros(grouped.shape, jnp.float32)] * 3,
        axis=1,
    ).reshape(groups, SUBLANES, 2 * per)
    facts = jnp.repeat(facts, 2 * slot_count, axis=2)
    ends = (grouped[:, :, 0] + grouped[:, :, 1]).reshape(groups * per)
    p, q, t = phase_tables(facts, span, slot_count, step)

    part = partial_fourier(coefficients.reshape(levels * rows_here, slots * own), panels)
    part = part.reshape(waves * levels, rows_here, wide)
    part = lax.all_to_all(part, ("wave", "lev"), 0, 0, tiled=True)
    fourier, returned = quadratic(
        wave_map,
        part,
        both_halves(lens.astype(jnp.float32)),
        both_halves(weights),
        waves,
        step,
    )
    returned = lax.all_to_all(returned, ("wave", "lev"), 0, 0, tiled=True)

    amplitudes = fourier[:, : 2 * tiles].reshape(slot_count, 2, 2, wide)[..., : groups * 2 * per]
    amplitudes = amplitudes.reshape(slot_count, 2, 2, groups, 2 * per).transpose(3, 1, 2, 4, 0)
    amplitudes = jnp.repeat(amplitudes, 2, axis=4).reshape(groups, 2, 2, LANES)
    amplitudes = jnp.tile(amplitudes, (1, 1, SUBLANES // 2, 1))
    values = grid_values(ends, facts, amplitudes, p, q, t, span, slot_count, rows_out)
    values = values.reshape(rows_out, span // 2, 2, LANES)
    values = with_layout_constraint(values, Layout(major_to_minor=(0, 1, 2, 3)))
    values = values.transpose(0, 2, 1, 3)
    values = with_layout_constraint(values, Layout(major_to_minor=(0, 2, 1, 3)))
    values = values.reshape(rows_out, 2, LPAD)
    values = with_layout_constraint(values, Layout(major_to_minor=(0, 1, 2)))
    grid = values.transpose(1, 0, 2).reshape(2, rows_out, 1, LPAD)

    returned = returned.reshape(waves, levels * rows_here, wide)
    spectral = direct(info, returned, panels, slots, own)
    spectral = lax.all_to_all(spectral, "lev", 0, 0, tiled=True)
    spec_out = spectral.transpose(1, 0, 2).reshape(slots, 1, 2, degrees_all)
    return (grid, spec_out)


def per_device(spec, legendre, gauss_w, cycle_len, wave_map):
    slot_count = wave_map.shape[0]
    fits = (
        spec.shape[3] % slot_count == 0
        and LANES % (4 * slot_count) == 0
        and spec.shape[1] == 1
        and 4 * spec.shape[0] == SUBLANES
    )
    form = evenly_spaced if fits else general
    return form(spec, legendre, gauss_w, cycle_len, wave_map)


def solution(mesh):
    placed = (P("wave", "lev", None, None), P("wave", "lev", None), P(), P(), P())
    return jax.shard_map(
        per_device,
        mesh=mesh,
        in_specs=placed,
        out_specs=(P(None, "wave", "lev", None), P("wave", "lev", None, None)),
        check_vma=False,
    )
```

```python
import functools
import math

import jax
import jax.numpy as jnp
from jax import lax
from jax.experimental import pallas as pl
from jax.experimental.layout import Layout, with_layout_constraint
from jax.experimental.pallas import tpu as pltpu
from jax.sharding import PartitionSpec as P

LPAD = 4864


def block_rows():
    for candidate in (10, 8, 6, 5, 4, 3, 2):
        return candidate
    return 1


def cycle_tables(lens_pair, orders, padded):
    position = jnp.arange(padded, dtype=jnp.int32)[None, :]
    first_len = lens_pair[:, 0:1]
    second = lens_pair[:, 1:2]
    upper_half = position >= first_len
    occupied = position < first_len + second
    offset = jnp.where(upper_half, position - first_len, position)
    length = jnp.where(upper_half, second, first_len)
    turn_count = orders[None, :, None] * offset[:, None, :] % length[:, None, :]
    angles = 2.0 * math.pi * turn_count.astype(jnp.float32) / length[:, None, :].astype(jnp.float32)
    cosine = jnp.where(occupied[:, None, :], jnp.cos(angles), 0.0).astype(jnp.bfloat16)
    minus_sine = jnp.where(occupied[:, None, :], -jnp.sin(angles), 0.0).astype(jnp.bfloat16)
    return (jnp.concatenate([cosine, minus_sine], 1), upper_half, occupied)


def cycle_block(waves, lens_pair, weights, orders, padded):
    row_count = waves.shape[0]
    fields = waves.shape[3]
    slot_count = orders.shape[0]
    tables, upper_half, occupied = cycle_tables(lens_pair, orders, padded)
    double = jnp.where(orders == 0, 1.0, 2.0)
    resolved = 2 * orders[None, None, :] < lens_pair[:, :, None]
    widening = jnp.where(resolved, double[None, None, :], 0.0)
    scaled = (waves.astype(jnp.float32) * widening[:, None, :, None, None, :]).astype(jnp.bfloat16)
    scaled = scaled.reshape(row_count, 4 * fields, 2 * slot_count)
    images = jnp.einsum("rak,rkp->rap", scaled, tables, preferred_element_type=jnp.float32)
    images = images.reshape(row_count, 2, 2, fields, padded)
    values = jnp.where(upper_half[:, None, None, :], images[:, :, 1], images[:, :, 0])
    values = jnp.where(occupied[:, None, None, :], values, 0.0).astype(jnp.bfloat16)
    squared = (values.astype(jnp.float32) * values.astype(jnp.float32)).astype(jnp.bfloat16)
    selector = jnp.stack([jnp.logical_not(upper_half), upper_half], 1)
    by_cycle = jnp.where(
        selector[:, None, :, None, :], squared[:, :, None, :, :], jnp.zeros((), jnp.bfloat16)
    )
    by_cycle = by_cycle.reshape(row_count, 4 * fields, padded)
    returned = jnp.einsum("rap,rkp->rak", by_cycle, tables, preferred_element_type=jnp.float32)
    returned = returned.reshape(row_count, 2, 2, fields, 2, slot_count)
    factor = jnp.where(
        resolved, weights[:, :, None] / lens_pair[:, :, None].astype(jnp.float32), 0.0
    )
    returned = (returned * factor[:, None, :, None, None, :]).astype(jnp.bfloat16)
    return (values, returned)


def parity_of(degree_ids, own_orders):
    return jnp.where((degree_ids[None, :] + own_orders[:, None]) % 2 == 0, 1.0, -1.0)


def general(spec, legendre, gauss_w, cycle_len, wave_map):
    slots_dev = spec.shape[0]
    fields = spec.shape[1]
    degrees_all = spec.shape[3]
    slot_count = wave_map.shape[0]
    orders = wave_map * degrees_all // slot_count
    wave_pos = lax.axis_index("wave")
    own_orders = lax.dynamic_slice_in_dim(orders, wave_pos * slots_dev, slots_dev)
    degrees = jnp.arange(degrees_all, dtype=jnp.int32)
    retained = degrees[None, :] >= own_orders[:, None]
    coefficients = jnp.where(retained[:, None, None, :], spec, jnp.zeros((), jnp.bfloat16))
    panels = lax.all_gather(legendre, "lev", axis=1, tiled=True)
    sign_flip = parity_of(degrees, own_orders)
    flipped = (coefficients.astype(jnp.float32) * sign_flip[:, None, None, :]).astype(jnp.bfloat16)
    stacked = jnp.stack([coefficients, flipped], 1)
    fourier = jnp.einsum(
        "shfcn,snq->shfcq", stacked, panels, preferred_element_type=jnp.float32
    ).astype(jnp.bfloat16)
    cycle_waves = lax.all_to_all(fourier, "wave", split_axis=4, concat_axis=0, tiled=True)
    local_lats = cycle_waves.shape[4]
    row_total = local_lats // 2
    lat_start = wave_pos * local_lats
    lens_here = lax.dynamic_slice_in_dim(cycle_len, lat_start, local_lats)
    weights_here = lax.dynamic_slice_in_dim(gauss_w, lat_start, local_lats)
    row_block = block_rows()
    blocks = row_total // row_block
    ordered = cycle_waves.reshape(slot_count, 2, fields, 2, row_total, 2).transpose(
        4, 1, 5, 2, 3, 0
    )
    ordered = ordered.reshape(blocks, row_block, 2, 2, fields, 2, slot_count)

    def run_block(operands):
        return cycle_block(operands[0], operands[1], operands[2], orders, LPAD)

    values, returned = lax.map(
        run_block,
        (
            ordered,
            lens_here.reshape(blocks, row_block, 2),
            weights_here.reshape(blocks, row_block, 2),
        ),
    )
    grid = values.reshape(row_total, 2, fields, LPAD).transpose(1, 0, 2, 3)
    returned = returned.reshape(row_total, 2, 2, fields, 2, slot_count).transpose(5, 1, 3, 4, 0, 2)
    returned = returned.reshape(slot_count, 2, fields, 2, local_lats)
    spectral = lax.all_to_all(returned, "wave", split_axis=0, concat_axis=4, tiled=True)
    both = jnp.einsum("shfcq,snq->shfcn", spectral, panels, preferred_element_type=jnp.float32)
    total = both[:, 0] + sign_flip[:, None, None, :] * both[:, 1]
    spec_out = jnp.where(retained[:, None, None, :], total, 0.0)
    return (grid, spec_out)


LANES = 128
SUBLANES = 8
STEPS = 5
VMEM = 8 * 1024 * 1024
SINE = (6.28318516, -41.34165503, 81.60100407, -76.54978222, 39.53670553)


def cos_turns(x, period, inverse):
    turn = x - period * jnp.floor(x * inverse + 0.5)
    v = 0.25 - jnp.abs(turn * inverse)
    y = v * v
    series = SINE[4]
    for coefficient in SINE[3::-1]:
        series = series * y + coefficient
    return v * series


def params(memory=VMEM):
    return pltpu.CompilerParams(vmem_limit_bytes=memory)


def cost(flops, nbytes):
    return pl.CostEstimate(flops=flops, bytes_accessed=nbytes, transcendentals=0)


def at_wave():
    return lax.axis_index("wave")


def at_level():
    return lax.axis_index("lev")


def smem():
    return pl.BlockSpec(memory_space=pltpu.SMEM)


def vmem():
    return pl.BlockSpec(memory_space=pltpu.VMEM)


def own_rows(wave_map, spec, panel, step):
    slots, parts, degrees_all = spec.shape
    rows = 2 * slots * parts

    def kernel(map_hbm, x_hbm, panel_hbm, o_ref, factor_ref, near_ref, map_ref, x_ref, sems):
        copies = [
            pltpu.make_async_copy(a, b, sems.at[i])
            for i, (a, b) in enumerate(((map_hbm, map_ref), (x_hbm, x_ref), (panel_hbm, near_ref)))
        ]
        for copy in copies:
            copy.start()
        copies[0].wait()
        row = lax.broadcasted_iota(jnp.int32, (rows, degrees_all), 0)
        degree = lax.broadcasted_iota(jnp.int32, (rows, degrees_all), 1)
        order = jnp.zeros((rows, degrees_all), jnp.int32)
        for s in range(slots):
            mine = row // parts % slots == s
            order = jnp.where(mine, map_ref[at_wave() * slots + s] * step, order)
        odd = jnp.logical_and(row >= rows // 2, ((degree + order) & 1) == 1)
        factor = jnp.where(degree >= order, jnp.where(odd, -1.0, 1.0), 0.0)
        factor_ref[...] = factor
        copies[1].wait()
        x = [x_ref[s].astype(jnp.float32) for s in range(slots)]
        o_ref[...] = jnp.concatenate(x + x, axis=0) * factor
        copies[2].wait()

    flat = jax.ShapeDtypeStruct((rows, degrees_all), jnp.float32)
    return pl.pallas_call(
        kernel,
        out_shape=(flat, flat, jax.ShapeDtypeStruct(panel.shape, panel.dtype)),
        in_specs=[pl.BlockSpec(memory_space=pltpu.HBM)] * 3,
        out_specs=(vmem(),) * 3,
        scratch_shapes=[
            pltpu.SMEM(wave_map.shape, wave_map.dtype),
            pltpu.VMEM(spec.shape, spec.dtype),
            pltpu.SemaphoreType.DMA((3,)),
        ],
        compiler_params=params(),
        cost_estimate=cost(10**9, 2 * 10**6),
        name="own_rows",
    )(wave_map, spec, panel)


def partial_fourier(first, factor, others, panels, slots, waves, wide):
    chips = len(others) + 1
    rows, degrees_all = first.shape
    parts = rows // (2 * slots)
    depth, lats = panels[0].shape
    own, here = depth // slots, lats // waves

    def kernel(first_ref, factor_ref, *refs):
        spec_refs, panel_refs = refs[: chips - 1], refs[chips - 1 : chips + 1]
        o_ref, left_ref = refs[chips + 1 :]
        factor = factor_ref[...]
        whole = [first_ref[...]]
        for ref in spec_refs:
            x = [ref[s].astype(jnp.float32) for s in range(slots)]
            whole.append(jnp.concatenate(x + x, axis=0) * factor)
        whole = jnp.concatenate(whole, axis=0)
        slot_of = lax.broadcasted_iota(jnp.int32, (chips * rows, own), 0) // parts % slots
        for level in range(2 * chips):

            @pl.when(at_level() == level)
            def _(level=level):
                for e in range(2):
                    start = (level ^ e) * own
                    piece = whole[:, start : start + own]
                    left = [jnp.where(slot_of == s, piece, 0.0) for s in range(slots)]
                    left_ref[e] = jnp.concatenate(left, axis=1).astype(jnp.bfloat16)

        total = jnp.dot(left_ref[0], panel_refs[0][...], preferred_element_type=jnp.float32)
        total += jnp.dot(left_ref[1], panel_refs[1][...], preferred_element_type=jnp.float32)
        chip = at_level() // 2
        fill = jnp.zeros((rows, wide - here), jnp.float32)
        for i in range(chips):
            mine = total[i * rows : (i + 1) * rows]
            for j in range(waves):
                value = mine[:, j * here : (j + 1) * here]
                o_ref[j, chip ^ i] = jnp.concatenate([value, fill], axis=1)

    return pl.pallas_call(
        kernel,
        out_shape=jax.ShapeDtypeStruct((waves, chips, rows, wide), jnp.float32),
        in_specs=[vmem()] * (chips + 3),
        out_specs=vmem(),
        scratch_shapes=[pltpu.VMEM((2, chips * rows, depth), jnp.bfloat16)],
        compiler_params=params(),
        cost_estimate=cost(10**9, 2 * 10**6),
        name="partial_fourier",
    )(first, factor, *others, *panels)


def quadratic(wave_map, parts_sum, lens, weights, waves, step):
    sources, rows, wide = parts_sum.shape
    slot_count = wave_map.shape[0]
    levels = sources // waves
    slots = slot_count // waves
    tiles = wide // LANES
    top = 2 * (slot_count - 1)
    shape = (SUBLANES, LANES)

    def kernel(map_ref, x_ref, len_ref, weight_ref, g_ref, o_ref, z_ref, r_ref, s_ref):
        z_ref[...] = jnp.zeros(z_ref.shape, jnp.float32)
        for i in range(waves):
            total = x_ref[i * levels].astype(jnp.float32)
            for j in range(1, levels):
                total = total + x_ref[i * levels + j].astype(jnp.float32)
            total = total.astype(jnp.bfloat16).astype(jnp.float32)
            for row in range(rows):
                h, s, c = row // (2 * slots), row // 2 % slots, row % 2
                at = map_ref[i * slots + s] * 2 + c
                for t in range(tiles):
                    k = h * tiles + t
                    z_ref[at, k : k + 1, :] = total[row : row + 1, t * LANES : (t + 1) * LANES]
        lens_here = len_ref[...]
        kept = [
            jnp.where(lens_here > 2.0 * step * w, 1.0, 0.0) for w in range(slot_count)
        ]
        real = [z_ref[2 * w] * kept[w] for w in range(slot_count)]
        imag = [z_ref[2 * w + 1] * kept[w] for w in range(slot_count)]
        for w in range(slot_count):
            double = 1.0 if w == 0 else 2.0
            g_ref[2 * w] = real[w] * double
            g_ref[2 * w + 1] = imag[w] * double
        imag[0] = jnp.zeros(shape, jnp.float32)
        square_real, square_imag = [], []
        for n in range(top + 1):
            re, im = jnp.zeros(shape, jnp.float32), jnp.zeros(shape, jnp.float32)
            for a in range(max(0, n - slot_count + 1), (n + 1) // 2):
                b = n - a
                re = re + (real[a] * real[b] - imag[a] * imag[b])
                im = im + (real[a] * imag[b] + imag[a] * real[b])
            for b in range(1, slot_count - n):
                a = n + b
                re = re + (real[a] * real[b] + imag[a] * imag[b])
                im = im + (imag[a] * real[b] - real[a] * imag[b])
            re, im = 2.0 * re, 2.0 * im
            if n % 2 == 0:
                a = n // 2
                re = re + (real[a] * real[a] - imag[a] * imag[a])
                im = im + 2.0 * (real[a] * imag[a])
            square_real.append(re)
            square_imag.append(im)
        whole = {
            d: jnp.where(lens_here == 1.0 * step * d, 1.0, 0.0)
            for d in range(3, top + slot_count)
        }
        weights_here = weight_ref[...]
        for w in range(slot_count):
            re, im = square_real[w], square_imag[w]
            if w == 0:
                im = jnp.zeros(shape, jnp.float32)
            else:
                for n in range(w + 1, top + 1):
                    re = re + whole[w + n] * square_real[n]
                    im = im - whole[w + n] * square_imag[n]
            factor = kept[w] * weights_here
            r_ref[2 * w] = re * factor
            r_ref[2 * w + 1] = im * factor
        for i in range(waves):
            for row in range(rows):
                h, s, c = row // (2 * slots), row // 2 % slots, row % 2
                at = map_ref[i * slots + s] * 2 + c
                for t in range(tiles):
                    k = h * tiles + t
                    s_ref[row : row + 1, t * LANES : (t + 1) * LANES] = r_ref[at, k : k + 1, :]
            packed = s_ref[...].astype(jnp.bfloat16)
            for j in range(levels):
                o_ref[i * levels + j] = packed

    return pl.pallas_call(
        kernel,
        out_shape=(
            jax.ShapeDtypeStruct((2 * slot_count,) + shape, jnp.float32),
            jax.ShapeDtypeStruct((sources, rows, wide), jnp.bfloat16),
        ),
        in_specs=[smem(), vmem(), vmem(), vmem()],
        out_specs=(vmem(), vmem()),
        scratch_shapes=[
            pltpu.VMEM((2 * slot_count,) + shape, jnp.float32),
            pltpu.VMEM((2 * slot_count,) + shape, jnp.float32),
            pltpu.VMEM((rows, wide), jnp.float32),
        ],
        compiler_params=params(),
        name="quadratic",
    )(wave_map, parts_sum, lens, weights)


def lane_facts(slot_count):
    lane = lax.broadcasted_iota(jnp.int32, (SUBLANES, LANES), 1)
    return (lane % (4 * slot_count) // 4, lane % 4 // 2, lane // (4 * slot_count), lane % 2)


def tile_of_row(block, span, slot_count):
    at = lax.broadcasted_iota(jnp.int32, (SUBLANES, LANES), 0) + block * SUBLANES
    at = at - lane_facts(slot_count)[2] * span % SUBLANES
    return at // 2, jnp.logical_and(at >= 0, at < span)


def prepare(cycle_len, gauss_w, span, slot_count, step, waves, groups, wide):
    here = cycle_len.shape[0] // waves
    tiles = wide // LANES
    per = SUBLANES // 2

    def kernel(len_ref, len_row_ref, weight_row_ref, o_ref, lens_ref, weights_ref):
        wave, part, row, cycle = lane_facts(slot_count)
        tile, _ = tile_of_row(0, span, slot_count)
        first = (tile * LANES).astype(jnp.float32)
        order = (step * wave).astype(jnp.float32)
        stride = order * (LANES * SUBLANES / 2.0)
        is_imag = part.astype(jnp.float32)
        way = (1 - 2 * cycle).astype(jnp.float32)
        point = lax.broadcasted_iota(jnp.int32, (SUBLANES, LANES), 1).astype(jnp.float32)
        down = lax.broadcasted_iota(jnp.int32, (SUBLANES, LANES), 0)
        start = at_wave() * here

        def body(g, carry):
            lens = [
                len_ref[start + jnp.minimum(g * SUBLANES + i, here - 1)] for i in range(SUBLANES)
            ]
            length = jnp.full((SUBLANES, LANES), lens[0], jnp.int32)
            length_down = length
            offset = jnp.zeros((SUBLANES, LANES), jnp.int32)
            split = offset
            for i in range(1, SUBLANES):
                mine = row == i // 2 if i % 2 == 0 else jnp.logical_and(row == i // 2, cycle == 1)
                length = jnp.where(mine, lens[i], length)
                length_down = jnp.where(down == i, lens[i], length_down)
            for r in range(per):
                offset = jnp.where(jnp.logical_and(row == r, cycle == 1), lens[2 * r], offset)
                split = jnp.where(row == r, lens[2 * r] // LANES, split)
            length = length.astype(jnp.float32)
            inverse = 1.0 / length
            quarter = 0.25 * length
            x = order * (first - offset.astype(jnp.float32))
            o_ref[g, 0] = cos_turns(x - is_imag * quarter, length, inverse)
            o_ref[g, 1] = cos_turns(x + (1.0 - is_imag) * quarter, length, inverse)
            turns = cos_turns(jnp.where(down == 1, stride - quarter, stride), length, inverse)
            o_ref[g, 2] = jnp.where(down < 2, turns, way * split.astype(jnp.float32))
            length = length_down.astype(jnp.float32)
            inverse = 1.0 / length
            quarter = 0.25 * length
            for i in range(2):
                turn = (i + 1.0) * step * point
                o_ref[g, 3 + 2 * i] = cos_turns(turn, length, inverse)
                o_ref[g, 4 + 2 * i] = cos_turns(turn + quarter, length, inverse)
            return carry

        lax.fori_loop(0, groups, body, 0, unroll=4)
        lens_ref[...] = jnp.full((SUBLANES, LANES), 4.0, jnp.float32)
        weights_ref[...] = jnp.zeros((SUBLANES, LANES), jnp.float32)
        for v in range(waves):

            @pl.when(at_wave() == v)
            def _(v=v):
                for t in range(tiles):
                    size = min(LANES, here - t * LANES)
                    at = v * here + t * LANES
                    lens = len_row_ref[:, at : at + size].astype(jnp.float32)
                    weights = weight_row_ref[:, at : at + size]
                    for h in range(2):
                        k = h * tiles + t
                        lens_ref[k : k + 1, 0:size] = lens
                        weights_ref[k : k + 1, 0:size] = weights

    flat = jax.ShapeDtypeStruct((SUBLANES, LANES), jnp.float32)
    return pl.pallas_call(
        kernel,
        out_shape=(jax.ShapeDtypeStruct((groups, 7, SUBLANES, LANES), jnp.float32), flat, flat),
        in_specs=[smem(), vmem(), vmem()],
        out_specs=(vmem(),) * 3,
        compiler_params=params(),
        cost_estimate=cost(3 * 10**9, 10**6),
        name="prepare",
    )(cycle_len, cycle_len.reshape(1, -1), gauss_w.reshape(1, -1))


def grid_values(cycle_len, fourier, tables, span, slot_count, rows_out, tiles):
    groups = tables.shape[0]
    per = SUBLANES // 2
    block = groups // STEPS
    blocks = -(-(span + SUBLANES // 2) // SUBLANES)
    size = 4 * slot_count
    kinds = 4 * slot_count
    around = LANES // SUBLANES

    def kernel(len_ref, fourier_ref, table_ref, o_ref, rows_ref, wave_ref):
        wave, _, row, cycle = lane_facts(slot_count)
        way = (1 - 2 * cycle).astype(jnp.float32)
        point = lax.broadcasted_iota(jnp.int32, (SUBLANES, LANES), 1)
        down = lax.broadcasted_iota(jnp.int32, (SUBLANES, LANES), 0)
        second = down % 2 == 1
        unit = jnp.where(down < 2, 1.0, 0.0)
        beside = jnp.where(down < 6, -1.0, 1.0)
        base = pl.program_id(0) * block
        start = at_wave() * 2 * rows_out

        @pl.when(pl.program_id(0) == 0)
        def _():
            for c in range(2):
                for h in range(2):
                    for w in range(slot_count):
                        for t in range(tiles):
                            at = (c * 2 + h) * slot_count + w
                            k = h * tiles + t
                            rows_ref[t, at : at + 1, :] = fourier_ref[2 * w + c, k : k + 1, :]

        pick = lax.broadcasted_iota(jnp.int32, (LANES, LANES), 0)
        lane = lax.broadcasted_iota(jnp.int32, (LANES, LANES), 1)
        pick = jnp.where(pick == lane // size * 2 + lane % 2, 1.0, 0.0).astype(jnp.bfloat16)
        turned = []
        for g in range(block):
            at = base + g
            shift = (around - at % around) % around * SUBLANES
            turned.append(pltpu.roll(rows_ref[at // around], shift, 1))
        spread = jnp.dot(
            jnp.concatenate(turned, axis=0).astype(jnp.bfloat16), pick, preferred_element_type=jnp.float32
        )
        for g in range(block):
            sums = []
            for k in range(4):
                at = g * kinds + k * slot_count
                value = jnp.where(down == wave, spread[at : at + SUBLANES], 0.0)
                sums.append(jnp.sum(value, axis=0, keepdims=True))
            for c in range(2):
                wave_ref[g, c] = jnp.where(down % 2 == 0, sums[2 * c], sums[2 * c + 1])

        def body(g, carry):
            real, imag = wave_ref[g, 0], wave_ref[g, 1]
            x = real * table_ref[g, 0] + imag * table_ref[g, 1]
            y = real * table_ref[g, 1] - imag * table_ref[g, 0]
            turn_cos, turn_sin = table_ref[g, 2, 0:1], table_ref[g, 2, 1:2]
            split = table_ref[g, 2, 2:3]
            main, mixed = [], []
            for k in range(blocks):
                if k:
                    x, y = x * turn_cos + y * turn_sin, y * turn_cos - x * turn_sin
                tile, inside = tile_of_row(k, span, slot_count)
                apart = tile.astype(jnp.float32) * way - split
                value = jnp.where(inside, x, 0.0) if k in (0, blocks - 1) else x
                main.append(jnp.where(apart < 0.0, value, 0.0))
                mixed.append(jnp.where(apart == 0.0, value, 0.0))
            main, mixed = jnp.concatenate(main, axis=0), jnp.concatenate(mixed, axis=0)
            left = jnp.concatenate([main, mixed], axis=1).astype(jnp.bfloat16)

            columns, ends = [], []
            for r in range(per):
                at = 2 * jnp.minimum((base + g) * per + r, rows_out - 1) + start
                first_end, end = len_ref[at], len_ref[at] + len_ref[at + 1]
                ends.append(end)
                cos1, sin1, cos2, sin2 = [
                    jnp.where(
                        second,
                        table_ref[g, i, 2 * r + 1 : 2 * r + 2],
                        table_ref[g, i, 2 * r : 2 * r + 1],
                    )
                    for i in range(3, 7)
                ]
                twice = 2.0 * cos2
                series = [jnp.where(down < 4, unit, jnp.where(down < 6, cos1, sin1))]
                third = series[0] * (twice + beside)
                series.append(jnp.where(down < 2, cos2, jnp.where(down < 4, sin2, third)))
                here = jnp.logical_xor(point < first_end % LANES, second)
                for _ in range(2, size // SUBLANES):
                    series.append(twice * series[-1] - series[-2])
                full = jnp.concatenate(series, axis=0).astype(jnp.bfloat16)
                part = jnp.concatenate([jnp.where(here, v, 0.0) for v in series], axis=0).astype(jnp.bfloat16)
                before = [jnp.zeros((r * size, LANES), jnp.bfloat16)] if r else []
                after = [jnp.zeros((LANES - (r + 1) * size, LANES), jnp.bfloat16)] if r < per - 1 else []
                columns.append(jnp.concatenate(before + [full] + after + before + [part] + after, axis=0))
            right = jnp.concatenate(columns, axis=1)
            product = jnp.dot(left, right, preferred_element_type=jnp.float32)
            places = {}
            for r in range(per):
                shift = r * span % SUBLANES
                for k in range(blocks):
                    if k * SUBLANES >= shift + span:
                        continue
                    value = product[k * SUBLANES : (k + 1) * SUBLANES, r * LANES : (r + 1) * LANES]
                    if k == blocks - 1:
                        position = (down + k * SUBLANES - shift) // 2 * LANES + point
                        value = jnp.where(position < ends[r], value, 0.0)
                    places.setdefault((r * span - shift) // SUBLANES + k, []).append(value)
            whole = [functools.reduce(lambda a, b: a + b, places[k]) for k in sorted(places)]
            size_out = per * span
            o_ref[pl.ds(pl.multiple_of(g * size_out, 16), size_out), :] = jnp.concatenate(
                whole, axis=0
            ).astype(jnp.bfloat16)
            return carry

        lax.fori_loop(0, block, body, 0, unroll=8)

    return pl.pallas_call(
        kernel,
        grid=(STEPS,),
        out_shape=jax.ShapeDtypeStruct((rows_out * span, LANES), jnp.bfloat16),
        in_specs=[
            smem(),
            pl.BlockSpec(fourier.shape, lambda i: (0, 0, 0)),
            pl.BlockSpec((block,) + tables.shape[1:], lambda i: (i, 0, 0, 0)),
        ],
        out_specs=pl.BlockSpec((block * per * span, LANES), lambda i: (i, 0)),
        scratch_shapes=[
            pltpu.VMEM((tiles, kinds, LANES), jnp.float32),
            pltpu.VMEM((block, 2, SUBLANES, LANES), jnp.float32),
        ],
        compiler_params=params(16 * 1024 * 1024),
        cost_estimate=cost(8 * 10**9, 3 * 10**6),
        name="grid_values",
    )(cycle_len, fourier, tables)


def direct(wave_map, returned, panels, step, slots):
    waves, tall, _ = returned.shape
    depth, lats = panels[0].shape
    own, here = depth // slots, lats // waves
    half = 2 * slots
    chips = tall // (2 * half)

    def kernel(map_ref, x_ref, own_ref, other_ref, *refs):
        o_refs, left_ref, all_ref = refs[:chips], refs[chips], refs[chips + 1]
        for j in range(waves):
            left_ref[:, j * here : (j + 1) * here] = x_ref[j, :, 0:here].astype(jnp.float32)
        left = left_ref[...].astype(jnp.bfloat16)
        shape = (chips, half, own)
        slot_of = lax.broadcasted_iota(jnp.int32, shape, 1) // 2
        lane = lax.broadcasted_iota(jnp.int32, shape, 2)
        for e, panel_ref in enumerate((own_ref, other_ref)):
            total = lax.dot_general(
                left, panel_ref[...], (((1,), (1,)), ((), ())), preferred_element_type=jnp.float32
            ).reshape(chips, 2 * half, depth)
            degree = lane + (at_level() ^ e) * own
            result = jnp.zeros(shape, jnp.float32)
            for s in range(slots):
                order = map_ref[at_wave() * slots + s] * step
                mine = total[:, :, s * own : (s + 1) * own]
                sign = (1 - 2 * ((degree + order) & 1)).astype(jnp.float32)
                value = mine[:, :half] + sign * mine[:, half:]
                keep = jnp.logical_and(slot_of == s, degree >= order)
                result = jnp.where(keep, value, result)
            all_ref[:, e * half : (e + 1) * half, :] = result
        for i in range(chips):
            o_refs[i][...] = all_ref[(at_level() // 2) ^ i]

    return pl.pallas_call(
        kernel,
        out_shape=(jax.ShapeDtypeStruct((2 * half, own), jnp.float32),) * chips,
        in_specs=[smem()] + [vmem()] * 3,
        out_specs=(vmem(),) * chips,
        scratch_shapes=[
            pltpu.VMEM((tall, lats), jnp.float32),
            pltpu.VMEM((chips, 2 * half, own), jnp.float32),
        ],
        compiler_params=params(),
        cost_estimate=cost(10**9, 2 * 10**6),
        name="direct",
    )(wave_map, returned, *panels)


def join_degrees(pieces, slots):
    chips = len(pieces)
    rows, own = pieces[0].shape
    half = rows // 2

    def kernel(*refs):
        piece_refs, o_ref, all_ref = refs[:chips], refs[chips], refs[chips + 1]
        for i in range(chips):
            for e in range(2):
                all_ref[at_level() ^ (2 * i + e)] = piece_refs[i][e * half : (e + 1) * half, :]
        whole = jnp.concatenate([all_ref[v] for v in range(2 * chips)], axis=1)
        for s in range(slots):
            o_ref[s] = whole[2 * s : 2 * s + 2]

    return pl.pallas_call(
        kernel,
        out_shape=jax.ShapeDtypeStruct((slots, 2, 2 * chips * own), jnp.float32),
        in_specs=[vmem()] * chips,
        out_specs=vmem(),
        scratch_shapes=[pltpu.VMEM((2 * chips, half, own), jnp.float32)],
        compiler_params=params(),
        name="join_degrees",
    )(*pieces)


def evenly_spaced(levels, spec, legendre, gauss_w, cycle_len, wave_map):
    slots = spec.shape[0]
    degrees_all = spec.shape[3]
    own = legendre.shape[1]
    lats = legendre.shape[2]
    slot_count = wave_map.shape[0]
    step = degrees_all // slot_count
    waves = slot_count // slots
    chips = levels // 2

    def across(x, bits):
        return lax.ppermute(x, "lev", [(j, j ^ bits) for j in range(levels)])

    def same_core(x):
        groups = [[j for j in range(waves * levels) if j % 2 == core] for core in range(2)]
        return lax.all_to_all(x, ("wave", "lev"), 0, 0, tiled=True, axis_index_groups=groups)

    mine = spec.reshape(slots, 2, degrees_all)
    others = [across(mine, 2 * i) for i in range(1, chips)]
    panel = legendre.reshape(slots * own, lats)
    first, factor, near = own_rows(wave_map, mine, panel, step)
    panels = (near, across(panel, 1))

    here = lats // waves
    wide = -(-here // LANES) * LANES
    tiles = wide // LANES
    per = SUBLANES // 2
    rows_out = here // 2
    groups = -(-rows_out // (per * STEPS)) * STEPS
    span = 2 * (LPAD // LANES)
    rows_here = 2 * slots * 2

    part = partial_fourier(first, factor, others, panels, slots, waves, wide)
    part = same_core(part.reshape(waves * chips, rows_here, wide))
    tables, lens, weights = prepare(
        cycle_len, gauss_w, span, slot_count, step, waves, groups, wide
    )
    fourier, returned = quadratic(wave_map, part, lens, weights, waves, step)
    returned = same_core(returned)

    values = grid_values(cycle_len, fourier, tables, span, slot_count, rows_out, tiles)
    returned, values = lax.optimization_barrier((returned, values))
    values = values.reshape(rows_out, span // 2, 2, LANES)
    values = with_layout_constraint(values, Layout(major_to_minor=(0, 1, 2, 3)))
    values = values.transpose(0, 2, 1, 3)
    values = with_layout_constraint(values, Layout(major_to_minor=(0, 2, 1, 3)))
    values = values.reshape(rows_out, 2, LPAD)
    values = with_layout_constraint(values, Layout(major_to_minor=(0, 1, 2)))
    grid = values.transpose(1, 0, 2).reshape(2, rows_out, 1, LPAD)

    returned = returned.reshape(waves, chips * rows_here, wide)
    pieces = direct(wave_map, returned, (panel, panels[1]), step, slots)
    pieces = [pieces[0]] + [across(pieces[i], 2 * i) for i in range(1, chips)]
    spec_out = join_degrees(pieces, slots).reshape(slots, 1, 2, degrees_all)
    return (grid, spec_out)


def per_device(levels, spec, legendre, gauss_w, cycle_len, wave_map):
    slot_count = wave_map.shape[0]
    fits = (
        spec.shape[3] % slot_count == 0
        and 2 * slot_count * SUBLANES == LANES
        and spec.shape[1] == 1
        and 4 * spec.shape[0] == SUBLANES
        and levels > 1
        and levels & (levels - 1) == 0
    )
    if fits:
        return evenly_spaced(levels, spec, legendre, gauss_w, cycle_len, wave_map)
    return general(spec, legendre, gauss_w, cycle_len, wave_map)


def solution(mesh):
    placed = (P("wave", "lev", None, None), P("wave", "lev", None), P(), P(), P())
    return jax.shard_map(
        functools.partial(per_device, mesh.shape["lev"]),
        mesh=mesh,
        in_specs=placed,
        out_specs=(P(None, "wave", "lev", None), P("wave", "lev", None, None)),
        check_vma=False,
    )
```

```python
import functools
import math

import jax
import jax.numpy as jnp
from jax import lax
from jax.experimental import pallas as pl
from jax.experimental.layout import Layout, with_layout_constraint
from jax.experimental.pallas import tpu as pltpu
from jax.sharding import PartitionSpec as P

LPAD = 4864


def block_rows():
    for candidate in (10, 8, 6, 5, 4, 3, 2):
        return candidate
    return 1


def cycle_tables(lens_pair, orders, padded):
    position = jnp.arange(padded, dtype=jnp.int32)[None, :]
    first_len = lens_pair[:, 0:1]
    second = lens_pair[:, 1:2]
    upper_half = position >= first_len
    occupied = position < first_len + second
    offset = jnp.where(upper_half, position - first_len, position)
    length = jnp.where(upper_half, second, first_len)
    turn_count = orders[None, :, None] * offset[:, None, :] % length[:, None, :]
    angles = 2.0 * math.pi * turn_count.astype(jnp.float32) / length[:, None, :].astype(jnp.float32)
    cosine = jnp.where(occupied[:, None, :], jnp.cos(angles), 0.0).astype(jnp.bfloat16)
    minus_sine = jnp.where(occupied[:, None, :], -jnp.sin(angles), 0.0).astype(jnp.bfloat16)
    return (jnp.concatenate([cosine, minus_sine], 1), upper_half, occupied)


def cycle_block(waves, lens_pair, weights, orders, padded):
    row_count = waves.shape[0]
    fields = waves.shape[3]
    slot_count = orders.shape[0]
    tables, upper_half, occupied = cycle_tables(lens_pair, orders, padded)
    double = jnp.where(orders == 0, 1.0, 2.0)
    resolved = 2 * orders[None, None, :] < lens_pair[:, :, None]
    widening = jnp.where(resolved, double[None, None, :], 0.0)
    scaled = (waves.astype(jnp.float32) * widening[:, None, :, None, None, :]).astype(jnp.bfloat16)
    scaled = scaled.reshape(row_count, 4 * fields, 2 * slot_count)
    images = jnp.einsum("rak,rkp->rap", scaled, tables, preferred_element_type=jnp.float32)
    images = images.reshape(row_count, 2, 2, fields, padded)
    values = jnp.where(upper_half[:, None, None, :], images[:, :, 1], images[:, :, 0])
    values = jnp.where(occupied[:, None, None, :], values, 0.0).astype(jnp.bfloat16)
    squared = (values.astype(jnp.float32) * values.astype(jnp.float32)).astype(jnp.bfloat16)
    selector = jnp.stack([jnp.logical_not(upper_half), upper_half], 1)
    by_cycle = jnp.where(
        selector[:, None, :, None, :], squared[:, :, None, :, :], jnp.zeros((), jnp.bfloat16)
    )
    by_cycle = by_cycle.reshape(row_count, 4 * fields, padded)
    returned = jnp.einsum("rap,rkp->rak", by_cycle, tables, preferred_element_type=jnp.float32)
    returned = returned.reshape(row_count, 2, 2, fields, 2, slot_count)
    factor = jnp.where(
        resolved, weights[:, :, None] / lens_pair[:, :, None].astype(jnp.float32), 0.0
    )
    returned = (returned * factor[:, None, :, None, None, :]).astype(jnp.bfloat16)
    return (values, returned)


def parity_of(degree_ids, own_orders):
    return jnp.where((degree_ids[None, :] + own_orders[:, None]) % 2 == 0, 1.0, -1.0)


def general(spec, legendre, gauss_w, cycle_len, wave_map):
    slots_dev = spec.shape[0]
    fields = spec.shape[1]
    degrees_all = spec.shape[3]
    slot_count = wave_map.shape[0]
    orders = wave_map * degrees_all // slot_count
    wave_pos = lax.axis_index("wave")
    own_orders = lax.dynamic_slice_in_dim(orders, wave_pos * slots_dev, slots_dev)
    degrees = jnp.arange(degrees_all, dtype=jnp.int32)
    retained = degrees[None, :] >= own_orders[:, None]
    coefficients = jnp.where(retained[:, None, None, :], spec, jnp.zeros((), jnp.bfloat16))
    panels = lax.all_gather(legendre, "lev", axis=1, tiled=True)
    sign_flip = parity_of(degrees, own_orders)
    flipped = (coefficients.astype(jnp.float32) * sign_flip[:, None, None, :]).astype(jnp.bfloat16)
    stacked = jnp.stack([coefficients, flipped], 1)
    fourier = jnp.einsum(
        "shfcn,snq->shfcq", stacked, panels, preferred_element_type=jnp.float32
    ).astype(jnp.bfloat16)
    cycle_waves = lax.all_to_all(fourier, "wave", split_axis=4, concat_axis=0, tiled=True)
    local_lats = cycle_waves.shape[4]
    row_total = local_lats // 2
    lat_start = wave_pos * local_lats
    lens_here = lax.dynamic_slice_in_dim(cycle_len, lat_start, local_lats)
    weights_here = lax.dynamic_slice_in_dim(gauss_w, lat_start, local_lats)
    row_block = block_rows()
    blocks = row_total // row_block
    ordered = cycle_waves.reshape(slot_count, 2, fields, 2, row_total, 2).transpose(
        4, 1, 5, 2, 3, 0
    )
    ordered = ordered.reshape(blocks, row_block, 2, 2, fields, 2, slot_count)

    def run_block(operands):
        return cycle_block(operands[0], operands[1], operands[2], orders, LPAD)

    values, returned = lax.map(
        run_block,
        (
            ordered,
            lens_here.reshape(blocks, row_block, 2),
            weights_here.reshape(blocks, row_block, 2),
        ),
    )
    grid = values.reshape(row_total, 2, fields, LPAD).transpose(1, 0, 2, 3)
    returned = returned.reshape(row_total, 2, 2, fields, 2, slot_count).transpose(5, 1, 3, 4, 0, 2)
    returned = returned.reshape(slot_count, 2, fields, 2, local_lats)
    spectral = lax.all_to_all(returned, "wave", split_axis=0, concat_axis=4, tiled=True)
    both = jnp.einsum("shfcq,snq->shfcn", spectral, panels, preferred_element_type=jnp.float32)
    total = both[:, 0] + sign_flip[:, None, None, :] * both[:, 1]
    spec_out = jnp.where(retained[:, None, None, :], total, 0.0)
    return (grid, spec_out)


LANES = 128
SUBLANES = 8
STEPS = 5
VMEM = 8 * 1024 * 1024
SINE = (6.28318516, -41.34165503, 81.60100407, -76.54978222, 39.53670553)


def cos_turns(x, period, inverse):
    turn = x - period * jnp.floor(x * inverse + 0.5)
    v = 0.25 - jnp.abs(turn * inverse)
    y = v * v
    series = SINE[4]
    for coefficient in SINE[3::-1]:
        series = series * y + coefficient
    return v * series


def params(memory=VMEM):
    return pltpu.CompilerParams(vmem_limit_bytes=memory)


def cost(flops, nbytes):
    return pl.CostEstimate(flops=flops, bytes_accessed=nbytes, transcendentals=0)


def at_wave():
    return lax.axis_index("wave")


def at_level():
    return lax.axis_index("lev")


def smem():
    return pl.BlockSpec(memory_space=pltpu.SMEM)


def vmem():
    return pl.BlockSpec(memory_space=pltpu.VMEM)


def parity_signs(rows, degrees_all):
    def kernel(o_ref):
        row = lax.broadcasted_iota(jnp.int32, (rows, degrees_all), 0)
        degree = lax.broadcasted_iota(jnp.int32, (rows, degrees_all), 1)
        odd = jnp.logical_and(row >= rows // 2, (degree & 1) == 1)
        o_ref[...] = jnp.where(odd, -1.0, 1.0)

    return pl.pallas_call(
        kernel,
        out_shape=jax.ShapeDtypeStruct((rows, degrees_all), jnp.float32),
        out_specs=vmem(),
        compiler_params=params(),
        cost_estimate=cost(4 * 10**9, 10**6),
        name="parity_signs",
    )()


def own_rows(wave_map, spec, panel, signs, step):
    slots, parts, degrees_all = spec.shape
    rows = 2 * slots * parts

    def kernel(map_ref, x_ref, panel_ref, sign_ref, o_ref, factor_ref, near_ref, sem):
        copy = pltpu.make_async_copy(panel_ref, near_ref, sem)
        copy.start()
        row = lax.broadcasted_iota(jnp.int32, (rows, degrees_all), 0)
        degree = lax.broadcasted_iota(jnp.int32, (rows, degrees_all), 1)
        order = jnp.zeros((rows, degrees_all), jnp.int32)
        for s in range(slots):
            mine = row // parts % slots == s
            order = jnp.where(mine, map_ref[at_wave() * slots + s] * step, order)
        turned = jnp.logical_and(row >= rows // 2, (order & 1) == 1)
        sign = sign_ref[...]
        factor = jnp.where(degree >= order, jnp.where(turned, -sign, sign), 0.0)
        factor_ref[...] = factor
        x = [x_ref[s].astype(jnp.float32) for s in range(slots)]
        o_ref[...] = jnp.concatenate(x + x, axis=0) * factor
        copy.wait()

    flat = jax.ShapeDtypeStruct((rows, degrees_all), jnp.float32)
    return pl.pallas_call(
        kernel,
        out_shape=(flat, flat, jax.ShapeDtypeStruct(panel.shape, panel.dtype)),
        in_specs=[smem(), vmem(), pl.BlockSpec(memory_space=pl.ANY), vmem()],
        out_specs=(vmem(),) * 3,
        scratch_shapes=[pltpu.SemaphoreType.DMA],
        compiler_params=params(),
        cost_estimate=cost(10**9, 2 * 10**6),
        name="own_rows",
    )(wave_map, spec, panel, signs)


def partial_fourier(first, factor, others, panels, slots, waves, wide):
    chips = len(others) + 1
    rows, degrees_all = first.shape
    parts = rows // (2 * slots)
    depth, lats = panels[0].shape
    own, here = depth // slots, lats // waves

    def kernel(first_ref, factor_ref, *refs):
        spec_refs, panel_refs = refs[: chips - 1], refs[chips - 1 : chips + 1]
        o_ref, left_ref = refs[chips + 1 :]
        factor = factor_ref[...]
        whole = [first_ref[...]]
        for ref in spec_refs:
            x = [ref[s].astype(jnp.float32) for s in range(slots)]
            whole.append(jnp.concatenate(x + x, axis=0) * factor)
        whole = jnp.concatenate(whole, axis=0)
        slot_of = lax.broadcasted_iota(jnp.int32, (chips * rows, own), 0) // parts % slots
        for level in range(2 * chips):

            @pl.when(at_level() == level)
            def _(level=level):
                for e in range(2):
                    start = (level ^ e) * own
                    piece = whole[:, start : start + own]
                    left = [jnp.where(slot_of == s, piece, 0.0) for s in range(slots)]
                    left_ref[e] = jnp.concatenate(left, axis=1).astype(jnp.bfloat16)

        total = jnp.dot(left_ref[0], panel_refs[0][...], preferred_element_type=jnp.float32)
        total += jnp.dot(left_ref[1], panel_refs[1][...], preferred_element_type=jnp.float32)
        chip = at_level() // 2
        fill = jnp.zeros((rows, wide - here), jnp.float32)
        for i in range(chips):
            mine = total[i * rows : (i + 1) * rows]
            for j in range(waves):
                value = mine[:, j * here : (j + 1) * here]
                o_ref[j, chip ^ i] = jnp.concatenate([value, fill], axis=1)

    return pl.pallas_call(
        kernel,
        out_shape=jax.ShapeDtypeStruct((waves, chips, rows, wide), jnp.float32),
        in_specs=[vmem()] * (chips + 3),
        out_specs=vmem(),
        scratch_shapes=[pltpu.VMEM((2, chips * rows, depth), jnp.bfloat16)],
        compiler_params=params(),
        cost_estimate=cost(10**9, 2 * 10**6),
        name="partial_fourier",
    )(first, factor, *others, *panels)


def quadratic(held, parts_sum, lens, weights, waves, step):
    sources, rows, wide = parts_sum.shape
    slot_count = held.shape[0]
    levels = sources // waves
    slots = slot_count // waves
    tiles = wide // LANES
    top = 2 * (slot_count - 1)
    shape = (SUBLANES, LANES)

    def kernel(held_ref, x_ref, len_ref, weight_ref, g_ref, o_ref, z_ref, r_ref, s_ref):
        half = rows // 2
        z_ref[...] = jnp.zeros(z_ref.shape, jnp.float32)
        for i in range(waves):
            total = x_ref[i * levels].astype(jnp.float32)
            for j in range(1, levels):
                total = total + x_ref[i * levels + j].astype(jnp.float32)
            total = total.astype(jnp.bfloat16).astype(jnp.float32)
            for h in range(2):
                for t in range(tiles):
                    at = i * half * SUBLANES + h * (SUBLANES // 2) + t
                    z_ref[pl.ds(at, half, stride=SUBLANES), :] = total[
                        h * half : (h + 1) * half, t * LANES : (t + 1) * LANES
                    ]
        lens_here = len_ref[...]
        kept = [
            jnp.where(lens_here > 2.0 * step * w, 1.0, 0.0) for w in range(slot_count)
        ]
        held = [
            [held_ref[w, i : i + 1, :] > 0.5 for i in range(slot_count)] for w in range(slot_count)
        ]
        real, imag = [], []
        for w in range(slot_count):
            re, im = jnp.zeros(shape, jnp.float32), jnp.zeros(shape, jnp.float32)
            for i in range(slot_count):
                at = i * 2 * SUBLANES
                re = jnp.where(held[w][i], z_ref[at : at + SUBLANES, :], re)
                im = jnp.where(held[w][i], z_ref[at + SUBLANES : at + 2 * SUBLANES, :], im)
            real.append(re * kept[w])
            imag.append(im * kept[w])
        for w in range(slot_count):
            double = 1.0 if w == 0 else 2.0
            g_ref[2 * w] = real[w] * double
            g_ref[2 * w + 1] = imag[w] * double
        imag[0] = jnp.zeros(shape, jnp.float32)
        square_real, square_imag = [], []
        for n in range(top + 1):
            re, im = jnp.zeros(shape, jnp.float32), jnp.zeros(shape, jnp.float32)
            for a in range(max(0, n - slot_count + 1), (n + 1) // 2):
                b = n - a
                re = re + (real[a] * real[b] - imag[a] * imag[b])
                im = im + (real[a] * imag[b] + imag[a] * real[b])
            for b in range(1, slot_count - n):
                a = n + b
                re = re + (real[a] * real[b] + imag[a] * imag[b])
                im = im + (imag[a] * real[b] - real[a] * imag[b])
            re, im = 2.0 * re, 2.0 * im
            if n % 2 == 0:
                a = n // 2
                re = re + (real[a] * real[a] - imag[a] * imag[a])
                im = im + 2.0 * (real[a] * imag[a])
            square_real.append(re)
            square_imag.append(im)
        whole = {
            d: jnp.where(lens_here == 1.0 * step * d, 1.0, 0.0)
            for d in range(3, top + slot_count)
        }
        weights_here = weight_ref[...]
        result = []
        for w in range(slot_count):
            re, im = square_real[w], square_imag[w]
            if w == 0:
                im = jnp.zeros(shape, jnp.float32)
            else:
                for n in range(w + 1, top + 1):
                    re = re + whole[w + n] * square_real[n]
                    im = im - whole[w + n] * square_imag[n]
            factor = kept[w] * weights_here
            result.append((re * factor, im * factor))
        for i in range(slot_count):
            re, im = result[0]
            for w in range(1, slot_count):
                re = jnp.where(held[w][i], result[w][0], re)
                im = jnp.where(held[w][i], result[w][1], im)
            at = i * 2 * SUBLANES
            r_ref[at : at + SUBLANES, :] = re
            r_ref[at + SUBLANES : at + 2 * SUBLANES, :] = im
        for i in range(waves):
            for h in range(2):
                for t in range(tiles):
                    start = i * half * SUBLANES + h * (SUBLANES // 2) + t
                    s_ref[h * half : (h + 1) * half, t * LANES : (t + 1) * LANES] = r_ref[
                        pl.ds(start, half, stride=SUBLANES), :
                    ]
            packed = s_ref[...].astype(jnp.bfloat16)
            for j in range(levels):
                o_ref[i * levels + j] = packed

    return pl.pallas_call(
        kernel,
        out_shape=(
            jax.ShapeDtypeStruct((2 * slot_count,) + shape, jnp.float32),
            jax.ShapeDtypeStruct((sources, rows, wide), jnp.bfloat16),
        ),
        in_specs=[vmem()] * 4,
        out_specs=(vmem(), vmem()),
        scratch_shapes=[
            pltpu.VMEM((2 * slot_count * SUBLANES, LANES), jnp.float32),
            pltpu.VMEM((2 * slot_count * SUBLANES, LANES), jnp.float32),
            pltpu.VMEM((rows, wide), jnp.float32),
        ],
        compiler_params=params(),
        name="quadratic",
    )(held, parts_sum, lens, weights)


def lane_facts(slot_count):
    lane = lax.broadcasted_iota(jnp.int32, (SUBLANES, LANES), 1)
    return (lane % (4 * slot_count) // 4, lane % 4 // 2, lane // (4 * slot_count), lane % 2)


def tile_of_row(block, span, slot_count):
    at = lax.broadcasted_iota(jnp.int32, (SUBLANES, LANES), 0) + block * SUBLANES
    at = at - lane_facts(slot_count)[2] * span % SUBLANES
    return at // 2, jnp.logical_and(at >= 0, at < span)


def prepare(cycle_len, gauss_w, wave_map, factor, span, step, waves, groups, wide, own):
    slot_count = wave_map.shape[0]
    slots = slot_count // waves
    rows, degrees_all = factor.shape
    levels = degrees_all // own
    here = cycle_len.shape[0] // waves
    tiles = wide // LANES
    per = SUBLANES // 2

    def kernel(
        len_ref, map_ref, len_row_ref, weight_row_ref, factor_ref, o_ref, lens_ref, weights_ref, held_ref, near_ref
    ):
        for i in range(slot_count):
            where = map_ref[i]
            for w in range(slot_count):
                held = jnp.where(where == w, 1.0, 0.0)
                held_ref[w, i : i + 1, :] = jnp.full((1, LANES), held, jnp.float32)
        for level in range(levels):

            @pl.when(at_level() == level)
            def _(level=level):
                for e in range(2):
                    start = (level ^ e) * own
                    near_ref[e] = factor_ref[:, start : start + own]

        wave, part, row, cycle = lane_facts(slot_count)
        tile, _ = tile_of_row(0, span, slot_count)
        first = (tile * LANES).astype(jnp.float32)
        order = (step * wave).astype(jnp.float32)
        stride = order * (LANES * SUBLANES / 2.0)
        is_imag = part.astype(jnp.float32)
        way = (1 - 2 * cycle).astype(jnp.float32)
        point = lax.broadcasted_iota(jnp.int32, (SUBLANES, LANES), 1).astype(jnp.float32)
        down = lax.broadcasted_iota(jnp.int32, (SUBLANES, LANES), 0)
        start = at_wave() * here

        def body(g, carry):
            lens = [
                len_ref[start + jnp.minimum(g * SUBLANES + i, here - 1)] for i in range(SUBLANES)
            ]
            length = jnp.full((SUBLANES, LANES), lens[0], jnp.int32)
            length_down = length
            offset = jnp.zeros((SUBLANES, LANES), jnp.int32)
            split = offset
            for i in range(1, SUBLANES):
                mine = row == i // 2 if i % 2 == 0 else jnp.logical_and(row == i // 2, cycle == 1)
                length = jnp.where(mine, lens[i], length)
                length_down = jnp.where(down == i, lens[i], length_down)
            for r in range(per):
                offset = jnp.where(jnp.logical_and(row == r, cycle == 1), lens[2 * r], offset)
                split = jnp.where(row == r, lens[2 * r] // LANES, split)
            length = length.astype(jnp.float32)
            inverse = 1.0 / length
            quarter = 0.25 * length
            x = order * (first - offset.astype(jnp.float32))
            o_ref[g, 0] = cos_turns(x - is_imag * quarter, length, inverse)
            o_ref[g, 1] = cos_turns(x + (1.0 - is_imag) * quarter, length, inverse)
            turns = cos_turns(jnp.where(down == 1, stride - quarter, stride), length, inverse)
            o_ref[g, 2] = jnp.where(down < 2, turns, way * split.astype(jnp.float32))
            length = length_down.astype(jnp.float32)
            inverse = 1.0 / length
            quarter = 0.25 * length
            for i in range(2):
                turn = (i + 1.0) * step * point
                o_ref[g, 3 + 2 * i] = cos_turns(turn, length, inverse)
                o_ref[g, 4 + 2 * i] = cos_turns(turn + quarter, length, inverse)
            return carry

        lax.fori_loop(0, groups, body, 0, unroll=4)
        lens_ref[...] = jnp.full((SUBLANES, LANES), 4.0, jnp.float32)
        weights_ref[...] = jnp.zeros((SUBLANES, LANES), jnp.float32)
        for v in range(waves):

            @pl.when(at_wave() == v)
            def _(v=v):
                for t in range(tiles):
                    size = min(LANES, here - t * LANES)
                    at = v * here + t * LANES
                    lens = len_row_ref[:, at : at + size].astype(jnp.float32)
                    weights = weight_row_ref[:, at : at + size]
                    for h in range(2):
                        k = h * (SUBLANES // 2) + t
                        lens_ref[k : k + 1, 0:size] = lens
                        weights_ref[k : k + 1, 0:size] = weights

    flat = jax.ShapeDtypeStruct((SUBLANES, LANES), jnp.float32)
    return pl.pallas_call(
        kernel,
        out_shape=(
            jax.ShapeDtypeStruct((groups, 7, SUBLANES, LANES), jnp.float32),
            flat,
            flat,
            jax.ShapeDtypeStruct((slot_count, slot_count, LANES), jnp.float32),
            jax.ShapeDtypeStruct((2, rows, own), jnp.float32),
        ),
        in_specs=[smem()] * 2 + [vmem()] * 3,
        out_specs=(vmem(),) * 5,
        compiler_params=params(),
        cost_estimate=cost(3 * 10**9, 10**6),
        name="prepare",
    )(cycle_len, wave_map, cycle_len.reshape(1, -1), gauss_w.reshape(1, -1), factor)


def grid_values(cycle_len, fourier, tables, span, slot_count, rows_out, tiles):
    groups = tables.shape[0]
    per = SUBLANES // 2
    block = groups // STEPS
    blocks = -(-(span + SUBLANES // 2) // SUBLANES)
    size = 4 * slot_count
    kinds = 4 * slot_count
    around = LANES // SUBLANES

    def kernel(len_ref, fourier_ref, table_ref, o_ref, rows_ref, wave_ref):
        wave, _, row, cycle = lane_facts(slot_count)
        way = (1 - 2 * cycle).astype(jnp.float32)
        point = lax.broadcasted_iota(jnp.int32, (SUBLANES, LANES), 1)
        down = lax.broadcasted_iota(jnp.int32, (SUBLANES, LANES), 0)
        second = down % 2 == 1
        unit = jnp.where(down < 2, 1.0, 0.0)
        beside = jnp.where(down < 6, -1.0, 1.0)
        base = pl.program_id(0) * block
        start = at_wave() * 2 * rows_out

        @pl.when(pl.program_id(0) == 0)
        def _():
            for c in range(2):
                for h in range(2):
                    for w in range(slot_count):
                        for t in range(tiles):
                            at = (c * 2 + h) * slot_count + w
                            k = h * (SUBLANES // 2) + t
                            rows_ref[t, at : at + 1, :] = fourier_ref[2 * w + c, k : k + 1, :]

        pick = lax.broadcasted_iota(jnp.int32, (LANES, LANES), 0)
        lane = lax.broadcasted_iota(jnp.int32, (LANES, LANES), 1)
        pick = jnp.where(pick == lane // size * 2 + lane % 2, 1.0, 0.0).astype(jnp.bfloat16)
        turned = []
        for g in range(block):
            at = base + g
            shift = (around - at % around) % around * SUBLANES
            turned.append(pltpu.roll(rows_ref[at // around], shift, 1))
        spread = jnp.dot(
            jnp.concatenate(turned, axis=0).astype(jnp.bfloat16), pick, preferred_element_type=jnp.float32
        )
        for g in range(block):
            sums = []
            for k in range(4):
                at = g * kinds + k * slot_count
                value = jnp.where(down == wave, spread[at : at + SUBLANES], 0.0)
                sums.append(jnp.sum(value, axis=0, keepdims=True))
            for c in range(2):
                wave_ref[g, c] = jnp.where(down % 2 == 0, sums[2 * c], sums[2 * c + 1])

        def body(g, carry):
            real, imag = wave_ref[g, 0], wave_ref[g, 1]
            x = real * table_ref[g, 0] + imag * table_ref[g, 1]
            y = real * table_ref[g, 1] - imag * table_ref[g, 0]
            turn_cos, turn_sin = table_ref[g, 2, 0:1], table_ref[g, 2, 1:2]
            split = table_ref[g, 2, 2:3]
            main, mixed = [], []
            for k in range(blocks):
                if k:
                    x, y = x * turn_cos + y * turn_sin, y * turn_cos - x * turn_sin
                tile, inside = tile_of_row(k, span, slot_count)
                apart = tile.astype(jnp.float32) * way - split
                value = jnp.where(inside, x, 0.0) if k in (0, blocks - 1) else x
                main.append(jnp.where(apart < 0.0, value, 0.0))
                mixed.append(jnp.where(apart == 0.0, value, 0.0))
            main, mixed = jnp.concatenate(main, axis=0), jnp.concatenate(mixed, axis=0)
            left = jnp.concatenate([main, mixed], axis=1).astype(jnp.bfloat16)

            columns, ends = [], []
            for r in range(per):
                at = 2 * jnp.minimum((base + g) * per + r, rows_out - 1) + start
                first_end, end = len_ref[at], len_ref[at] + len_ref[at + 1]
                ends.append(end)
                cos1, sin1, cos2, sin2 = [
                    jnp.where(
                        second,
                        table_ref[g, i, 2 * r + 1 : 2 * r + 2],
                        table_ref[g, i, 2 * r : 2 * r + 1],
                    )
                    for i in range(3, 7)
                ]
                twice = 2.0 * cos2
                series = [jnp.where(down < 4, unit, jnp.where(down < 6, cos1, sin1))]
                third = series[0] * (twice + beside)
                series.append(jnp.where(down < 2, cos2, jnp.where(down < 4, sin2, third)))
                here = jnp.logical_xor(point < first_end % LANES, second)
                for _ in range(2, size // SUBLANES):
                    series.append(twice * series[-1] - series[-2])
                full = jnp.concatenate(series, axis=0).astype(jnp.bfloat16)
                part = jnp.concatenate([jnp.where(here, v, 0.0) for v in series], axis=0).astype(jnp.bfloat16)
                before = [jnp.zeros((r * size, LANES), jnp.bfloat16)] if r else []
                after = [jnp.zeros((LANES - (r + 1) * size, LANES), jnp.bfloat16)] if r < per - 1 else []
                columns.append(jnp.concatenate(before + [full] + after + before + [part] + after, axis=0))
            right = jnp.concatenate(columns, axis=1)
            product = jnp.dot(left, right, preferred_element_type=jnp.float32)
            places = {}
            for r in range(per):
                shift = r * span % SUBLANES
                for k in range(blocks):
                    if k * SUBLANES >= shift + span:
                        continue
                    value = product[k * SUBLANES : (k + 1) * SUBLANES, r * LANES : (r + 1) * LANES]
                    if k == blocks - 1:
                        position = (down + k * SUBLANES - shift) // 2 * LANES + point
                        value = jnp.where(position < ends[r], value, 0.0)
                    places.setdefault((r * span - shift) // SUBLANES + k, []).append(value)
            whole = [functools.reduce(lambda a, b: a + b, places[k]) for k in sorted(places)]
            size_out = per * span
            o_ref[pl.ds(pl.multiple_of(g * size_out, 16), size_out), :] = jnp.concatenate(
                whole, axis=0
            ).astype(jnp.bfloat16)
            return carry

        lax.fori_loop(0, block, body, 0, unroll=8)

    return pl.pallas_call(
        kernel,
        grid=(STEPS,),
        out_shape=jax.ShapeDtypeStruct((rows_out * span, LANES), jnp.bfloat16),
        in_specs=[
            smem(),
            pl.BlockSpec(fourier.shape, lambda i: (0, 0, 0)),
            pl.BlockSpec((block,) + tables.shape[1:], lambda i: (i, 0, 0, 0)),
        ],
        out_specs=pl.BlockSpec((block * per * span, LANES), lambda i: (i, 0)),
        scratch_shapes=[
            pltpu.VMEM((tiles, kinds, LANES), jnp.float32),
            pltpu.VMEM((block, 2, SUBLANES, LANES), jnp.float32),
        ],
        compiler_params=params(16 * 1024 * 1024),
        cost_estimate=cost(8 * 10**9, 3 * 10**6),
        name="grid_values",
    )(cycle_len, fourier, tables)


def direct(returned, factors, panels):
    waves, tall, _ = returned.shape
    depth, lats = panels[0].shape
    own, here = factors.shape[2], lats // waves
    slots, half = depth // own, factors.shape[1] // 2
    chips = tall // (2 * half)

    def kernel(x_ref, factor_ref, own_ref, other_ref, *refs):
        o_refs, left_ref, all_ref = refs[:chips], refs[chips], refs[chips + 1]
        for j in range(waves):
            left_ref[:, j * here : (j + 1) * here] = x_ref[j, :, 0:here].astype(jnp.float32)
        left = left_ref[...].astype(jnp.bfloat16)
        shape = (chips, half, own)
        slot_of = lax.broadcasted_iota(jnp.int32, shape, 1) // 2
        for e, panel_ref in enumerate((own_ref, other_ref)):
            total = lax.dot_general(
                left, panel_ref[...], (((1,), (1,)), ((), ())), preferred_element_type=jnp.float32
            ).reshape(chips, 2 * half, depth)
            result = jnp.zeros(shape, jnp.float32)
            for s in range(slots):
                mine = total[:, :, s * own : (s + 1) * own] * factor_ref[e][None]
                result = jnp.where(slot_of == s, mine[:, :half] + mine[:, half:], result)
            all_ref[:, e * half : (e + 1) * half, :] = result
        for i in range(chips):
            o_refs[i][...] = all_ref[(at_level() // 2) ^ i]

    return pl.pallas_call(
        kernel,
        out_shape=(jax.ShapeDtypeStruct((2 * half, own), jnp.float32),) * chips,
        in_specs=[vmem()] * 4,
        out_specs=(vmem(),) * chips,
        scratch_shapes=[
            pltpu.VMEM((tall, lats), jnp.float32),
            pltpu.VMEM((chips, 2 * half, own), jnp.float32),
        ],
        compiler_params=params(),
        cost_estimate=cost(10**9, 2 * 10**6),
        name="direct",
    )(returned, factors, *panels)


def join_degrees(pieces, slots):
    chips = len(pieces)
    rows, own = pieces[0].shape
    half = rows // 2

    def kernel(*refs):
        piece_refs, o_ref, all_ref = refs[:chips], refs[chips], refs[chips + 1]
        for i in range(chips):
            for e in range(2):
                all_ref[at_level() ^ (2 * i + e)] = piece_refs[i][e * half : (e + 1) * half, :]
        whole = jnp.concatenate([all_ref[v] for v in range(2 * chips)], axis=1)
        for s in range(slots):
            o_ref[s] = whole[2 * s : 2 * s + 2]

    return pl.pallas_call(
        kernel,
        out_shape=jax.ShapeDtypeStruct((slots, 2, 2 * chips * own), jnp.float32),
        in_specs=[vmem()] * chips,
        out_specs=vmem(),
        scratch_shapes=[pltpu.VMEM((2 * chips, half, own), jnp.float32)],
        compiler_params=params(),
        name="join_degrees",
    )(*pieces)


def evenly_spaced(levels, spec, legendre, gauss_w, cycle_len, wave_map):
    slots = spec.shape[0]
    degrees_all = spec.shape[3]
    own = legendre.shape[1]
    lats = legendre.shape[2]
    slot_count = wave_map.shape[0]
    step = degrees_all // slot_count
    waves = slot_count // slots
    chips = levels // 2

    def across(x, bits):
        return lax.ppermute(x, "lev", [(j, j ^ bits) for j in range(levels)])

    def same_core(x):
        groups = [[j for j in range(waves * levels) if j % 2 == core] for core in range(2)]
        return lax.all_to_all(x, ("wave", "lev"), 0, 0, tiled=True, axis_index_groups=groups)

    mine = spec.reshape(slots, 2, degrees_all)
    others = [across(mine, 2 * i) for i in range(1, chips)]
    panel = legendre.reshape(slots * own, lats)
    signs = parity_signs(2 * slots * 2, degrees_all)
    first, factor, near = own_rows(wave_map, mine, panel, signs, step)
    panels = (near, across(panel, 1))

    here = lats // waves
    wide = -(-here // LANES) * LANES
    tiles = wide // LANES
    per = SUBLANES // 2
    rows_out = here // 2
    groups = -(-rows_out // (per * STEPS)) * STEPS
    span = 2 * (LPAD // LANES)
    rows_here = 2 * slots * 2

    part = partial_fourier(first, factor, others, panels, slots, waves, wide)
    part = same_core(part.reshape(waves * chips, rows_here, wide))
    tables, lens, weights, held, factors = prepare(
        cycle_len, gauss_w, wave_map, factor, span, step, waves, groups, wide, own
    )
    fourier, returned = quadratic(held, part, lens, weights, waves, step)
    returned = same_core(returned)

    values = grid_values(cycle_len, fourier, tables, span, slot_count, rows_out, tiles)
    returned, values = lax.optimization_barrier((returned, values))
    values = values.reshape(rows_out, span // 2, 2, LANES)
    values = with_layout_constraint(values, Layout(major_to_minor=(0, 1, 2, 3)))
    values = values.transpose(0, 2, 1, 3)
    values = with_layout_constraint(values, Layout(major_to_minor=(0, 2, 1, 3)))
    values = values.reshape(rows_out, 2, LPAD)
    values = with_layout_constraint(values, Layout(major_to_minor=(0, 1, 2)))
    grid = values.transpose(1, 0, 2).reshape(2, rows_out, 1, LPAD)

    returned = returned.reshape(waves, chips * rows_here, wide)
    pieces = direct(returned, factors, (panel, panels[1]))
    pieces = [pieces[0]] + [across(pieces[i], 2 * i) for i in range(1, chips)]
    spec_out = join_degrees(pieces, slots).reshape(slots, 1, 2, degrees_all)
    return (grid, spec_out)


def per_device(levels, spec, legendre, gauss_w, cycle_len, wave_map):
    slot_count = wave_map.shape[0]
    fits = (
        spec.shape[3] % slot_count == 0
        and 2 * slot_count * SUBLANES == LANES
        and spec.shape[1] == 1
        and 4 * spec.shape[0] == SUBLANES
        and levels > 1
        and levels & (levels - 1) == 0
    )
    if fits:
        return evenly_spaced(levels, spec, legendre, gauss_w, cycle_len, wave_map)
    return general(spec, legendre, gauss_w, cycle_len, wave_map)


def solution(mesh):
    placed = (P("wave", "lev", None, None), P("wave", "lev", None), P(), P(), P())
    return jax.shard_map(
        functools.partial(per_device, mesh.shape["lev"]),
        mesh=mesh,
        in_specs=placed,
        out_specs=(P(None, "wave", "lev", None), P("wave", "lev", None, None)),
        check_vma=False,
    )
```

```python
import functools
import math

import jax
import jax.numpy as jnp
from jax import lax
from jax.experimental import pallas as pl
from jax.experimental.layout import Layout, with_layout_constraint
from jax.experimental.pallas import tpu as pltpu
from jax.sharding import PartitionSpec as P

LPAD = 4864


def block_rows():
    for candidate in (10, 8, 6, 5, 4, 3, 2):
        return candidate
    return 1


def cycle_tables(lens_pair, orders, padded):
    position = jnp.arange(padded, dtype=jnp.int32)[None, :]
    first_len = lens_pair[:, 0:1]
    second = lens_pair[:, 1:2]
    upper_half = position >= first_len
    occupied = position < first_len + second
    offset = jnp.where(upper_half, position - first_len, position)
    length = jnp.where(upper_half, second, first_len)
    turn_count = orders[None, :, None] * offset[:, None, :] % length[:, None, :]
    angles = 2.0 * math.pi * turn_count.astype(jnp.float32) / length[:, None, :].astype(jnp.float32)
    cosine = jnp.where(occupied[:, None, :], jnp.cos(angles), 0.0).astype(jnp.bfloat16)
    minus_sine = jnp.where(occupied[:, None, :], -jnp.sin(angles), 0.0).astype(jnp.bfloat16)
    return (jnp.concatenate([cosine, minus_sine], 1), upper_half, occupied)


def cycle_block(waves, lens_pair, weights, orders, padded):
    row_count = waves.shape[0]
    fields = waves.shape[3]
    slot_count = orders.shape[0]
    tables, upper_half, occupied = cycle_tables(lens_pair, orders, padded)
    double = jnp.where(orders == 0, 1.0, 2.0)
    resolved = 2 * orders[None, None, :] < lens_pair[:, :, None]
    widening = jnp.where(resolved, double[None, None, :], 0.0)
    scaled = (waves.astype(jnp.float32) * widening[:, None, :, None, None, :]).astype(jnp.bfloat16)
    scaled = scaled.reshape(row_count, 4 * fields, 2 * slot_count)
    images = jnp.einsum("rak,rkp->rap", scaled, tables, preferred_element_type=jnp.float32)
    images = images.reshape(row_count, 2, 2, fields, padded)
    values = jnp.where(upper_half[:, None, None, :], images[:, :, 1], images[:, :, 0])
    values = jnp.where(occupied[:, None, None, :], values, 0.0).astype(jnp.bfloat16)
    squared = (values.astype(jnp.float32) * values.astype(jnp.float32)).astype(jnp.bfloat16)
    selector = jnp.stack([jnp.logical_not(upper_half), upper_half], 1)
    by_cycle = jnp.where(
        selector[:, None, :, None, :], squared[:, :, None, :, :], jnp.zeros((), jnp.bfloat16)
    )
    by_cycle = by_cycle.reshape(row_count, 4 * fields, padded)
    returned = jnp.einsum("rap,rkp->rak", by_cycle, tables, preferred_element_type=jnp.float32)
    returned = returned.reshape(row_count, 2, 2, fields, 2, slot_count)
    factor = jnp.where(
        resolved, weights[:, :, None] / lens_pair[:, :, None].astype(jnp.float32), 0.0
    )
    returned = (returned * factor[:, None, :, None, None, :]).astype(jnp.bfloat16)
    return (values, returned)


def parity_of(degree_ids, own_orders):
    return jnp.where((degree_ids[None, :] + own_orders[:, None]) % 2 == 0, 1.0, -1.0)


def general(spec, legendre, gauss_w, cycle_len, wave_map):
    slots_dev = spec.shape[0]
    fields = spec.shape[1]
    degrees_all = spec.shape[3]
    slot_count = wave_map.shape[0]
    orders = wave_map * degrees_all // slot_count
    wave_pos = lax.axis_index("wave")
    own_orders = lax.dynamic_slice_in_dim(orders, wave_pos * slots_dev, slots_dev)
    degrees = jnp.arange(degrees_all, dtype=jnp.int32)
    retained = degrees[None, :] >= own_orders[:, None]
    coefficients = jnp.where(retained[:, None, None, :], spec, jnp.zeros((), jnp.bfloat16))
    panels = lax.all_gather(legendre, "lev", axis=1, tiled=True)
    sign_flip = parity_of(degrees, own_orders)
    flipped = (coefficients.astype(jnp.float32) * sign_flip[:, None, None, :]).astype(jnp.bfloat16)
    stacked = jnp.stack([coefficients, flipped], 1)
    fourier = jnp.einsum(
        "shfcn,snq->shfcq", stacked, panels, preferred_element_type=jnp.float32
    ).astype(jnp.bfloat16)
    cycle_waves = lax.all_to_all(fourier, "wave", split_axis=4, concat_axis=0, tiled=True)
    local_lats = cycle_waves.shape[4]
    row_total = local_lats // 2
    lat_start = wave_pos * local_lats
    lens_here = lax.dynamic_slice_in_dim(cycle_len, lat_start, local_lats)
    weights_here = lax.dynamic_slice_in_dim(gauss_w, lat_start, local_lats)
    row_block = block_rows()
    blocks = row_total // row_block
    ordered = cycle_waves.reshape(slot_count, 2, fields, 2, row_total, 2).transpose(
        4, 1, 5, 2, 3, 0
    )
    ordered = ordered.reshape(blocks, row_block, 2, 2, fields, 2, slot_count)

    def run_block(operands):
        return cycle_block(operands[0], operands[1], operands[2], orders, LPAD)

    values, returned = lax.map(
        run_block,
        (
            ordered,
            lens_here.reshape(blocks, row_block, 2),
            weights_here.reshape(blocks, row_block, 2),
        ),
    )
    grid = values.reshape(row_total, 2, fields, LPAD).transpose(1, 0, 2, 3)
    returned = returned.reshape(row_total, 2, 2, fields, 2, slot_count).transpose(5, 1, 3, 4, 0, 2)
    returned = returned.reshape(slot_count, 2, fields, 2, local_lats)
    spectral = lax.all_to_all(returned, "wave", split_axis=0, concat_axis=4, tiled=True)
    both = jnp.einsum("shfcq,snq->shfcn", spectral, panels, preferred_element_type=jnp.float32)
    total = both[:, 0] + sign_flip[:, None, None, :] * both[:, 1]
    spec_out = jnp.where(retained[:, None, None, :], total, 0.0)
    return (grid, spec_out)


LANES = 128
SUBLANES = 8
STEPS = 5
VMEM = 8 * 1024 * 1024
SINE = (6.28318516, -41.34165503, 81.60100407, -76.54978222, 39.53670553)


def circle(x, period, inverse):
    turn = (x - period * jnp.floor(x * inverse + 0.5)) * inverse
    away = jnp.abs(turn)
    values = []
    for v in (0.25 - away, 0.25 - jnp.abs(away - 0.25)):
        y = v * v
        series = SINE[4]
        for coefficient in SINE[3::-1]:
            series = series * y + coefficient
        values.append(v * series)
    return values[0], jnp.where(turn < 0.0, -values[1], values[1])


def params(memory=VMEM):
    return pltpu.CompilerParams(vmem_limit_bytes=memory)


def cost(flops, nbytes):
    return pl.CostEstimate(flops=flops, bytes_accessed=nbytes, transcendentals=0)


def at_wave():
    return lax.axis_index("wave")


def at_level():
    return lax.axis_index("lev")


def smem():
    return pl.BlockSpec(memory_space=pltpu.SMEM)


def vmem():
    return pl.BlockSpec(memory_space=pltpu.VMEM)


def parity_signs(rows, degrees_all):
    def kernel(o_ref):
        row = lax.broadcasted_iota(jnp.int32, (rows, degrees_all), 0)
        degree = lax.broadcasted_iota(jnp.int32, (rows, degrees_all), 1)
        odd = jnp.logical_and(row >= rows // 2, (degree & 1) == 1)
        o_ref[...] = jnp.where(odd, -1.0, 1.0)

    return pl.pallas_call(
        kernel,
        out_shape=jax.ShapeDtypeStruct((rows, degrees_all), jnp.float32),
        out_specs=vmem(),
        compiler_params=params(),
        cost_estimate=cost(4 * 10**9, 10**6),
        name="parity_signs",
    )()


def partial_fourier(first, factor, others, panels, slots, waves, wide):
    chips = len(others) + 1
    rows, degrees_all = first.shape
    parts = rows // (2 * slots)
    depth, lats = panels[0].shape
    own, here = depth // slots, lats // waves

    def kernel(first_ref, factor_ref, *refs):
        spec_refs, panel_refs = refs[: chips - 1], refs[chips - 1 : chips + 1]
        o_ref, left_ref = refs[chips + 1 :]
        factor = factor_ref[...]
        whole = [first_ref[...]]
        for ref in spec_refs:
            x = [ref[s].astype(jnp.float32) for s in range(slots)]
            whole.append(jnp.concatenate(x + x, axis=0) * factor)
        whole = jnp.concatenate(whole, axis=0)
        slot_of = lax.broadcasted_iota(jnp.int32, (chips * rows, own), 0) // parts % slots
        for level in range(2 * chips):

            @pl.when(at_level() == level)
            def _(level=level):
                for e in range(2):
                    start = (level ^ e) * own
                    piece = whole[:, start : start + own]
                    left = [jnp.where(slot_of == s, piece, 0.0) for s in range(slots)]
                    left_ref[e] = jnp.concatenate(left, axis=1).astype(jnp.bfloat16)

        total = jnp.dot(left_ref[0], panel_refs[0][...], preferred_element_type=jnp.float32)
        total += jnp.dot(left_ref[1], panel_refs[1][...], preferred_element_type=jnp.float32)
        chip = at_level() // 2
        fill = jnp.zeros((rows, wide - here), jnp.float32)
        for i in range(chips):
            mine = total[i * rows : (i + 1) * rows]
            for j in range(waves):
                value = mine[:, j * here : (j + 1) * here]
                value = jnp.concatenate([value, fill], axis=1)
                o_ref[j, chip ^ i] = value.astype(jnp.bfloat16)

    return pl.pallas_call(
        kernel,
        out_shape=jax.ShapeDtypeStruct((waves, chips, rows, wide), jnp.bfloat16),
        in_specs=[vmem()] * (chips + 3),
        out_specs=vmem(),
        scratch_shapes=[pltpu.VMEM((2, chips * rows, depth), jnp.bfloat16)],
        compiler_params=params(),
        cost_estimate=cost(10**9, 2 * 10**6),
        name="partial_fourier",
    )(first, factor, *others, *panels)


def quadratic(held, parts_sum, lens, weights, waves, step):
    sources, rows, wide = parts_sum.shape
    slot_count = held.shape[0]
    levels = sources // waves
    slots = slot_count // waves
    tiles = wide // LANES
    top = 2 * (slot_count - 1)
    shape = (SUBLANES, LANES)

    def kernel(held_ref, x_ref, len_ref, weight_ref, g_ref, o_ref, z_ref, r_ref, s_ref):
        half = rows // 2
        z_ref[...] = jnp.zeros(z_ref.shape, jnp.float32)
        for i in range(waves):
            total = x_ref[i * levels].astype(jnp.float32)
            for j in range(1, levels):
                total = total + x_ref[i * levels + j].astype(jnp.float32)
            total = total.astype(jnp.bfloat16).astype(jnp.float32)
            for h in range(2):
                for t in range(tiles):
                    at = i * half * SUBLANES + h * (SUBLANES // 2) + t
                    z_ref[pl.ds(at, half, stride=SUBLANES), :] = total[
                        h * half : (h + 1) * half, t * LANES : (t + 1) * LANES
                    ]
        lens_here = len_ref[...]
        kept = [
            jnp.where(lens_here > 2.0 * step * w, 1.0, 0.0) for w in range(slot_count)
        ]
        held = [
            [held_ref[w, i : i + 1, :] > 0.5 for i in range(slot_count)] for w in range(slot_count)
        ]
        real, imag = [], []
        for w in range(slot_count):
            re, im = jnp.zeros(shape, jnp.float32), jnp.zeros(shape, jnp.float32)
            for i in range(slot_count):
                at = i * 2 * SUBLANES
                re = jnp.where(held[w][i], z_ref[at : at + SUBLANES, :], re)
                im = jnp.where(held[w][i], z_ref[at + SUBLANES : at + 2 * SUBLANES, :], im)
            real.append(re * kept[w])
            imag.append(im * kept[w])
        for w in range(slot_count):
            double = 1.0 if w == 0 else 2.0
            at = 2 * w * SUBLANES
            g_ref[at : at + SUBLANES, :] = real[w] * double
            g_ref[at + SUBLANES : at + 2 * SUBLANES, :] = imag[w] * double
        imag[0] = jnp.zeros(shape, jnp.float32)
        square_real, square_imag = [], []
        for n in range(top + 1):
            re, im = jnp.zeros(shape, jnp.float32), jnp.zeros(shape, jnp.float32)
            for a in range(max(0, n - slot_count + 1), (n + 1) // 2):
                b = n - a
                re = re + (real[a] * real[b] - imag[a] * imag[b])
                im = im + (real[a] * imag[b] + imag[a] * real[b])
            for b in range(1, slot_count - n):
                a = n + b
                re = re + (real[a] * real[b] + imag[a] * imag[b])
                im = im + (imag[a] * real[b] - real[a] * imag[b])
            re, im = 2.0 * re, 2.0 * im
            if n % 2 == 0:
                a = n // 2
                re = re + (real[a] * real[a] - imag[a] * imag[a])
                im = im + 2.0 * (real[a] * imag[a])
            square_real.append(re)
            square_imag.append(im)
        whole = {
            d: jnp.where(lens_here == 1.0 * step * d, 1.0, 0.0)
            for d in range(3, top + slot_count)
        }
        weights_here = weight_ref[...]
        result = []
        for w in range(slot_count):
            re, im = square_real[w], square_imag[w]
            if w == 0:
                im = jnp.zeros(shape, jnp.float32)
            else:
                for n in range(w + 1, top + 1):
                    re = re + whole[w + n] * square_real[n]
                    im = im - whole[w + n] * square_imag[n]
            factor = kept[w] * weights_here
            result.append((re * factor, im * factor))
        for i in range(slot_count):
            re, im = result[0]
            for w in range(1, slot_count):
                re = jnp.where(held[w][i], result[w][0], re)
                im = jnp.where(held[w][i], result[w][1], im)
            at = i * 2 * SUBLANES
            r_ref[at : at + SUBLANES, :] = re
            r_ref[at + SUBLANES : at + 2 * SUBLANES, :] = im
        for i in range(waves):
            for h in range(2):
                for t in range(tiles):
                    start = i * half * SUBLANES + h * (SUBLANES // 2) + t
                    s_ref[h * half : (h + 1) * half, t * LANES : (t + 1) * LANES] = r_ref[
                        pl.ds(start, half, stride=SUBLANES), :
                    ]
            packed = s_ref[...].astype(jnp.bfloat16)
            for j in range(levels):
                o_ref[i * levels + j] = packed

    return pl.pallas_call(
        kernel,
        out_shape=(
            jax.ShapeDtypeStruct((2 * slot_count * SUBLANES, LANES), jnp.float32),
            jax.ShapeDtypeStruct((sources, rows, wide), jnp.bfloat16),
        ),
        in_specs=[vmem()] * 4,
        out_specs=(vmem(), vmem()),
        scratch_shapes=[
            pltpu.VMEM((2 * slot_count * SUBLANES, LANES), jnp.float32),
            pltpu.VMEM((2 * slot_count * SUBLANES, LANES), jnp.float32),
            pltpu.VMEM((rows, wide), jnp.float32),
        ],
        compiler_params=params(),
        name="quadratic",
    )(held, parts_sum, lens, weights)


def lane_facts(slot_count):
    lane = lax.broadcasted_iota(jnp.int32, (SUBLANES, LANES), 1)
    return (lane % (4 * slot_count) // 4, lane % 4 // 2, lane // (4 * slot_count), lane % 2)


def tile_of_row(block, span, slot_count):
    at = lax.broadcasted_iota(jnp.int32, (SUBLANES, LANES), 0) + block * SUBLANES
    at = at - lane_facts(slot_count)[2] * span % SUBLANES
    return at // 2, jnp.logical_and(at >= 0, at < span)


def prepare(cycle_len, gauss_w, wave_map, spec, panel, signs, span, step, waves, groups, wide):
    slot_count = wave_map.shape[0]
    slots, parts, degrees_all = spec.shape
    own = panel.shape[0] // slots
    levels = degrees_all // own
    rows = 2 * slots * parts
    here = cycle_len.shape[0] // waves
    tiles = wide // LANES
    per = SUBLANES // 2

    def kernel(
        len_ref, map_ref, len_row_ref, weight_row_ref, x_ref, panel_ref, sign_ref,
        first_ref, factor_ref, factors_ref, near_ref, o_ref, lens_ref, weights_ref, held_ref, sem,
    ):
        copy = pltpu.make_async_copy(panel_ref, near_ref, sem)
        copy.start()
        row_of = lax.broadcasted_iota(jnp.int32, (rows, degrees_all), 0)
        degree = lax.broadcasted_iota(jnp.int32, (rows, degrees_all), 1)
        bound = jnp.zeros((rows, degrees_all), jnp.int32)
        for s in range(slots):
            mine = row_of // parts % slots == s
            bound = jnp.where(mine, map_ref[at_wave() * slots + s] * step, bound)
        turned = jnp.logical_and(row_of >= rows // 2, (bound & 1) == 1)
        sign = sign_ref[...]
        factor = jnp.where(degree >= bound, jnp.where(turned, -sign, sign), 0.0)
        factor_ref[...] = factor
        x = [x_ref[s].astype(jnp.float32) for s in range(slots)]
        first_ref[...] = jnp.concatenate(x + x, axis=0) * factor
        for level in range(levels):

            @pl.when(at_level() == level)
            def _(level=level):
                for e in range(2):
                    start = (level ^ e) * own
                    factors_ref[e] = factor[:, start : start + own]

        for i in range(slot_count):
            for w in range(slot_count):
                held = jnp.where(map_ref[i] == w, 1.0, 0.0)
                held_ref[w, i : i + 1, :] = jnp.full((1, LANES), held, jnp.float32)

        lens_ref[...] = jnp.full((SUBLANES, LANES), 4.0, jnp.float32)
        weights_ref[...] = jnp.zeros((SUBLANES, LANES), jnp.float32)
        for v in range(waves):

            @pl.when(at_wave() == v)
            def _(v=v):
                for t in range(tiles):
                    size = min(LANES, here - t * LANES)
                    at = v * here + t * LANES
                    lens = len_row_ref[at : at + size].astype(jnp.float32).reshape(1, size)
                    weights = weight_row_ref[at : at + size].reshape(1, size)
                    for h in range(2):
                        k = h * (SUBLANES // 2) + t
                        lens_ref[k : k + 1, 0:size] = lens
                        weights_ref[k : k + 1, 0:size] = weights

        wave, part, row, cycle = lane_facts(slot_count)
        tile, _ = tile_of_row(0, span, slot_count)
        first = (tile * LANES).astype(jnp.float32)
        order = (step * wave).astype(jnp.float32)
        stride = order * (LANES * SUBLANES / 2.0)
        imag = part == 1
        way = (1 - 2 * cycle).astype(jnp.float32)
        down = lax.broadcasted_iota(jnp.int32, (SUBLANES, LANES), 0)
        turn = step * lax.broadcasted_iota(jnp.int32, (SUBLANES, LANES), 1).astype(jnp.float32)
        mine = [row == i // 2 if i % 2 == 0 else jnp.logical_and(row == i // 2, cycle == 1) for i in range(SUBLANES)]
        after = [jnp.logical_and(row == r, cycle == 1) for r in range(per)]
        start = at_wave() * here

        def body(g, carry):
            lens = [
                len_ref[start + jnp.minimum(g * SUBLANES + i, here - 1)] for i in range(SUBLANES)
            ]
            length = jnp.full((SUBLANES, LANES), lens[0].astype(jnp.float32), jnp.float32)
            length_down = length
            offset = jnp.zeros((SUBLANES, LANES), jnp.float32)
            split, marks = offset, offset
            for i in range(1, SUBLANES):
                value = lens[i].astype(jnp.float32)
                length = jnp.where(mine[i], value, length)
                length_down = jnp.where(down == i, value, length_down)
            for r in range(per):
                offset = jnp.where(after[r], lens[2 * r].astype(jnp.float32), offset)
                split = jnp.where(row == r, (lens[2 * r] // LANES).astype(jnp.float32), split)
                marks = jnp.where(down == r, (lens[2 * r] % LANES).astype(jnp.float32), marks)
                marks = jnp.where(down == per + r, (lens[2 * r] + lens[2 * r + 1]).astype(jnp.float32), marks)
            inverse = 1.0 / length
            cos, sin = circle(order * (first - offset), length, inverse)
            o_ref[g, 0] = jnp.where(imag, sin, cos)
            o_ref[g, 1] = jnp.where(imag, cos, -sin)
            cos, sin = circle(stride, length, inverse)
            turns = jnp.where(down == 0, cos, sin)
            o_ref[g, 2] = jnp.where(down < 2, turns, way * split)
            cos, sin = circle(turn, length_down, 1.0 / length_down)
            o_ref[g, 3] = cos
            o_ref[g, 4] = -sin
            o_ref[g, 5] = 1.0 - 2.0 * sin * sin
            o_ref[g, 6] = -2.0 * sin * cos
            o_ref[g, 7] = marks
            return carry

        lax.fori_loop(0, groups, body, 0, unroll=4)
        copy.wait()

    flat = jax.ShapeDtypeStruct((SUBLANES, LANES), jnp.float32)
    return pl.pallas_call(
        kernel,
        out_shape=(
            jax.ShapeDtypeStruct((rows, degrees_all), jnp.float32),
            jax.ShapeDtypeStruct((rows, degrees_all), jnp.float32),
            jax.ShapeDtypeStruct((2, rows, own), jnp.float32),
            jax.ShapeDtypeStruct(panel.shape, panel.dtype),
            jax.ShapeDtypeStruct((groups, 8, SUBLANES, LANES), jnp.float32),
            flat,
            flat,
            jax.ShapeDtypeStruct((slot_count, slot_count, LANES), jnp.float32),
        ),
        in_specs=[smem()] * 2 + [vmem()] * 3 + [pl.BlockSpec(memory_space=pl.ANY), vmem()],
        out_specs=(vmem(),) * 8,
        scratch_shapes=[pltpu.SemaphoreType.DMA],
        compiler_params=params(),
        cost_estimate=cost(3 * 10**9, 10**6),
        name="prepare",
    )(cycle_len, wave_map, cycle_len, gauss_w, spec, panel, signs)


def grid_values(fourier, tables, span, slot_count, rows_out, tiles):
    groups = tables.shape[0]
    per = SUBLANES // 2
    block = groups // STEPS
    blocks = -(-(span + SUBLANES // 2) // SUBLANES)
    size = 4 * slot_count
    kinds = 4 * slot_count
    around = LANES // SUBLANES

    def kernel(fourier_ref, table_ref, o_hbm, rows_ref, wave_ref, part_ref, sems):
        wave, _, row, cycle = lane_facts(slot_count)
        way = (1 - 2 * cycle).astype(jnp.float32)
        point = lax.broadcasted_iota(jnp.int32, (SUBLANES, LANES), 1).astype(jnp.float32)
        down = lax.broadcasted_iota(jnp.int32, (SUBLANES, LANES), 0)
        second = down % 2 == 1
        unit = jnp.where(down < 2, 1.0, 0.0)
        beside = jnp.where(down < 6, -1.0, 1.0)
        for c in range(2):
            for h in range(2):
                for t in range(tiles):
                    at = (c * 2 + h) * slot_count
                    k = c * SUBLANES + h * (SUBLANES // 2) + t
                    rows_ref[t, at : at + slot_count, :] = fourier_ref[
                        pl.ds(k, slot_count, stride=2 * SUBLANES), :
                    ]
        pick = lax.broadcasted_iota(jnp.int32, (LANES, LANES), 0)
        lane = lax.broadcasted_iota(jnp.int32, (LANES, LANES), 1)
        pick = jnp.where(pick == lane // size * 2 + lane % 2, 1.0, 0.0).astype(jnp.bfloat16)

        turned = []
        for g in range(groups):
            shift = -g % around * SUBLANES
            value = rows_ref[g // around]
            turned.append(pltpu.roll(value, shift, 1) if shift else value)
        spread = jnp.dot(
            jnp.concatenate(turned, axis=0).astype(jnp.bfloat16), pick, preferred_element_type=jnp.float32
        )
        for g in range(groups):
            sums = []
            for k in range(4):
                at = g * kinds + k * slot_count
                value = jnp.where(down == wave, spread[at : at + SUBLANES], 0.0)
                sums.append(jnp.sum(value, axis=0, keepdims=True))
            for c in range(2):
                wave_ref[g, c] = jnp.where(down % 2 == 0, sums[2 * c], sums[2 * c + 1])

        def one_group(base, i, g):
            real, imag = wave_ref[g, 0], wave_ref[g, 1]
            x = real * table_ref[g, 0] + imag * table_ref[g, 1]
            y = real * table_ref[g, 1] - imag * table_ref[g, 0]
            turn_cos, turn_sin = table_ref[g, 2, 0:1], table_ref[g, 2, 1:2]
            split = table_ref[g, 2, 2:3]
            main, mixed = [], []
            for k in range(blocks):
                if k:
                    x, y = x * turn_cos + y * turn_sin, y * turn_cos - x * turn_sin
                tile, inside = tile_of_row(k, span, slot_count)
                apart = tile.astype(jnp.float32) * way - split
                value = jnp.where(inside, x, 0.0) if k in (0, blocks - 1) else x
                main.append(jnp.where(apart < 0.0, value, 0.0))
                mixed.append(jnp.where(apart == 0.0, value, 0.0))
            main, mixed = jnp.concatenate(main, axis=0), jnp.concatenate(mixed, axis=0)
            left = jnp.concatenate([main, mixed], axis=1).astype(jnp.bfloat16)

            columns, ends = [], []
            for r in range(per):
                ends.append(table_ref[g, 7, per + r : per + r + 1])
                cos1, sin1, cos2, sin2 = [
                    jnp.where(
                        second,
                        table_ref[g, i, 2 * r + 1 : 2 * r + 2],
                        table_ref[g, i, 2 * r : 2 * r + 1],
                    )
                    for i in range(3, 7)
                ]
                twice = 2.0 * cos2
                series = [jnp.where(down < 4, unit, jnp.where(down < 6, cos1, sin1))]
                third = series[0] * (twice + beside)
                series.append(jnp.where(down < 2, cos2, jnp.where(down < 4, sin2, third)))
                here = jnp.logical_xor(point < table_ref[g, 7, r : r + 1], second)
                for _ in range(2, size // SUBLANES):
                    series.append(twice * series[-1] - series[-2])
                full = jnp.concatenate(series, axis=0).astype(jnp.bfloat16)
                part = jnp.concatenate([jnp.where(here, v, 0.0) for v in series], axis=0).astype(jnp.bfloat16)
                before = [jnp.zeros((r * size, LANES), jnp.bfloat16)] if r else []
                after = [jnp.zeros((LANES - (r + 1) * size, LANES), jnp.bfloat16)] if r < per - 1 else []
                columns.append(jnp.concatenate(before + [full] + after + before + [part] + after, axis=0))
            right = jnp.concatenate(columns, axis=1)
            product = jnp.dot(left, right, preferred_element_type=jnp.float32)
            places = {}
            for r in range(per):
                shift = r * span % SUBLANES
                for k in range(blocks):
                    if k * SUBLANES >= shift + span:
                        continue
                    value = product[k * SUBLANES : (k + 1) * SUBLANES, r * LANES : (r + 1) * LANES]
                    if k == blocks - 1:
                        position = ((down + k * SUBLANES - shift) // 2 * LANES).astype(jnp.float32) + point
                        value = jnp.where(position < ends[r], value, 0.0)
                    places.setdefault((r * span - shift) // SUBLANES + k, []).append(value)
            whole = [functools.reduce(lambda a, b: a + b, places[k]) for k in sorted(places)]
            size_out = per * span
            part_ref[base, i * size_out : (i + 1) * size_out, :] = jnp.concatenate(
                whole, axis=0
            ).astype(jnp.bfloat16)

        tall = block * per * span // 2

        def copy(i, half):
            start = (2 * i + half) * tall
            size = min(tall, rows_out * span - start)
            return pltpu.make_async_copy(
                part_ref.at[i, pl.ds(half * tall, size), :],
                o_hbm.at[pl.ds(start, size), :],
                sems.at[2 * i + half],
            )

        def step(base, carry):
            for half in range(2):
                for i in range(half * block // 2, (half + 1) * block // 2):
                    one_group(base, i, base * block + i)
                for i in range(STEPS):

                    @pl.when(base == i)
                    def _(i=i, half=half):
                        copy(i, half).start()

            return carry

        lax.fori_loop(0, STEPS, step, 0)
        for i in range(STEPS):
            for half in range(2):
                copy(i, half).wait()

    return pl.pallas_call(
        kernel,
        out_shape=jax.ShapeDtypeStruct((rows_out * span, LANES), jnp.bfloat16),
        in_specs=[vmem()] * 2,
        out_specs=pl.BlockSpec(memory_space=pl.ANY),
        scratch_shapes=[
            pltpu.VMEM((tiles, kinds, LANES), jnp.float32),
            pltpu.VMEM((groups, 2, SUBLANES, LANES), jnp.float32),
            pltpu.VMEM((STEPS, block * per * span, LANES), jnp.bfloat16),
            pltpu.SemaphoreType.DMA((2 * STEPS,)),
        ],
        compiler_params=params(16 * 1024 * 1024),
        cost_estimate=cost(8 * 10**9, 3 * 10**6),
        name="grid_values",
    )(fourier, tables)


def direct(returned, factors, panels):
    waves, tall, _ = returned.shape
    depth, lats = panels[0].shape
    own, here = factors.shape[2], lats // waves
    slots, half = depth // own, factors.shape[1] // 2
    chips = tall // (2 * half)

    def kernel(x_ref, factor_ref, own_ref, other_ref, *refs):
        o_refs, left_ref, all_ref = refs[:chips], refs[chips], refs[chips + 1]
        for j in range(waves):
            left_ref[:, j * here : (j + 1) * here] = x_ref[j, :, 0:here].astype(jnp.float32)
        left = left_ref[...].astype(jnp.bfloat16)
        shape = (chips, half, own)
        slot_of = lax.broadcasted_iota(jnp.int32, shape, 1) // 2
        for e, panel_ref in enumerate((own_ref, other_ref)):
            total = lax.dot_general(
                left, panel_ref[...], (((1,), (1,)), ((), ())), preferred_element_type=jnp.float32
            ).reshape(chips, 2 * half, depth)
            result = jnp.zeros(shape, jnp.float32)
            for s in range(slots):
                mine = total[:, :, s * own : (s + 1) * own] * factor_ref[e][None]
                result = jnp.where(slot_of == s, mine[:, :half] + mine[:, half:], result)
            all_ref[:, e * half : (e + 1) * half, :] = result
        for i in range(chips):
            o_refs[i][...] = all_ref[(at_level() // 2) ^ i]

    return pl.pallas_call(
        kernel,
        out_shape=(jax.ShapeDtypeStruct((2 * half, own), jnp.float32),) * chips,
        in_specs=[vmem()] * 4,
        out_specs=(vmem(),) * chips,
        scratch_shapes=[
            pltpu.VMEM((tall, lats), jnp.float32),
            pltpu.VMEM((chips, 2 * half, own), jnp.float32),
        ],
        compiler_params=params(),
        cost_estimate=cost(10**9, 2 * 10**6),
        name="direct",
    )(returned, factors, *panels)


def join_degrees(pieces, slots):
    chips = len(pieces)
    rows, own = pieces[0].shape
    half = rows // 2

    def kernel(*refs):
        piece_refs, o_ref, all_ref = refs[:chips], refs[chips], refs[chips + 1]
        for i in range(chips):
            for e in range(2):
                all_ref[at_level() ^ (2 * i + e)] = piece_refs[i][e * half : (e + 1) * half, :]
        whole = jnp.concatenate([all_ref[v] for v in range(2 * chips)], axis=1)
        for s in range(slots):
            o_ref[s] = whole[2 * s : 2 * s + 2]

    return pl.pallas_call(
        kernel,
        out_shape=jax.ShapeDtypeStruct((slots, 2, 2 * chips * own), jnp.float32),
        in_specs=[vmem()] * chips,
        out_specs=vmem(),
        scratch_shapes=[pltpu.VMEM((2 * chips, half, own), jnp.float32)],
        compiler_params=params(),
        name="join_degrees",
    )(*pieces)


def evenly_spaced(levels, spec, legendre, gauss_w, cycle_len, wave_map):
    slots = spec.shape[0]
    degrees_all = spec.shape[3]
    own = legendre.shape[1]
    lats = legendre.shape[2]
    slot_count = wave_map.shape[0]
    step = degrees_all // slot_count
    waves = slot_count // slots
    chips = levels // 2

    def across(x, bits):
        return lax.ppermute(x, "lev", [(j, j ^ bits) for j in range(levels)])

    def same_core(x):
        groups = [[j for j in range(waves * levels) if j % 2 == core] for core in range(2)]
        return lax.all_to_all(x, ("wave", "lev"), 0, 0, tiled=True, axis_index_groups=groups)

    mine = spec.reshape(slots, 2, degrees_all)
    others = [across(mine, 2 * i) for i in range(1, chips)]
    panel = legendre.reshape(slots * own, lats)
    signs = parity_signs(2 * slots * 2, degrees_all)
    here = lats // waves
    wide = -(-here // LANES) * LANES
    tiles = wide // LANES
    per = SUBLANES // 2
    rows_out = here // 2
    groups = -(-rows_out // (per * STEPS)) * STEPS
    span = 2 * (LPAD // LANES)
    rows_here = 2 * slots * 2
    first, factor, factors, near, tables, lens, weights, held = prepare(
        cycle_len, gauss_w, wave_map, mine, panel, signs, span, step, waves, groups, wide
    )
    panels = (near, across(panel, 1))

    part = partial_fourier(first, factor, others, panels, slots, waves, wide)
    part = same_core(part.reshape(waves * chips, rows_here, wide))
    fourier, returned = quadratic(held, part, lens, weights, waves, step)
    returned = same_core(returned)

    values = grid_values(fourier, tables, span, slot_count, rows_out, tiles)
    values = values.reshape(rows_out, span // 2, 2, LANES)
    values = with_layout_constraint(values, Layout(major_to_minor=(0, 1, 2, 3)))
    values = values.transpose(0, 2, 1, 3)
    values = with_layout_constraint(values, Layout(major_to_minor=(0, 2, 1, 3)))
    values = values.reshape(rows_out, 2, LPAD)
    values = with_layout_constraint(values, Layout(major_to_minor=(0, 1, 2)))
    grid = values.transpose(1, 0, 2).reshape(2, rows_out, 1, LPAD)

    returned = returned.reshape(waves, chips * rows_here, wide)
    pieces = direct(returned, factors, (panel, panels[1]))
    pieces = [pieces[0]] + [across(pieces[i], 2 * i) for i in range(1, chips)]
    spec_out = join_degrees(pieces, slots).reshape(slots, 1, 2, degrees_all)
    return (grid, spec_out)


def per_device(levels, spec, legendre, gauss_w, cycle_len, wave_map):
    slot_count = wave_map.shape[0]
    fits = (
        spec.shape[3] % slot_count == 0
        and 2 * slot_count * SUBLANES == LANES
        and spec.shape[1] == 1
        and 4 * spec.shape[0] == SUBLANES
        and levels > 1
        and levels & (levels - 1) == 0
    )
    if fits:
        return evenly_spaced(levels, spec, legendre, gauss_w, cycle_len, wave_map)
    return general(spec, legendre, gauss_w, cycle_len, wave_map)


def solution(mesh):
    placed = (P("wave", "lev", None, None), P("wave", "lev", None), P(), P(), P())
    return jax.shard_map(
        functools.partial(per_device, mesh.shape["lev"]),
        mesh=mesh,
        in_specs=placed,
        out_specs=(P(None, "wave", "lev", None), P("wave", "lev", None, None)),
        check_vma=False,
    )
```

```python
import functools
import math

import jax
import jax.numpy as jnp
from jax import lax
from jax.experimental import pallas as pl
from jax.experimental.layout import Layout, with_layout_constraint
from jax.experimental.pallas import tpu as pltpu
from jax.sharding import PartitionSpec as P

LPAD = 4864


def block_rows():
    for candidate in (10, 8, 6, 5, 4, 3, 2):
        return candidate
    return 1


def cycle_tables(lens_pair, orders, padded):
    position = jnp.arange(padded, dtype=jnp.int32)[None, :]
    first_len = lens_pair[:, 0:1]
    second = lens_pair[:, 1:2]
    upper_half = position >= first_len
    occupied = position < first_len + second
    offset = jnp.where(upper_half, position - first_len, position)
    length = jnp.where(upper_half, second, first_len)
    turn_count = orders[None, :, None] * offset[:, None, :] % length[:, None, :]
    angles = 2.0 * math.pi * turn_count.astype(jnp.float32) / length[:, None, :].astype(jnp.float32)
    cosine = jnp.where(occupied[:, None, :], jnp.cos(angles), 0.0).astype(jnp.bfloat16)
    minus_sine = jnp.where(occupied[:, None, :], -jnp.sin(angles), 0.0).astype(jnp.bfloat16)
    return (jnp.concatenate([cosine, minus_sine], 1), upper_half, occupied)


def cycle_block(waves, lens_pair, weights, orders, padded):
    row_count = waves.shape[0]
    fields = waves.shape[3]
    slot_count = orders.shape[0]
    tables, upper_half, occupied = cycle_tables(lens_pair, orders, padded)
    double = jnp.where(orders == 0, 1.0, 2.0)
    resolved = 2 * orders[None, None, :] < lens_pair[:, :, None]
    widening = jnp.where(resolved, double[None, None, :], 0.0)
    scaled = (waves.astype(jnp.float32) * widening[:, None, :, None, None, :]).astype(jnp.bfloat16)
    scaled = scaled.reshape(row_count, 4 * fields, 2 * slot_count)
    images = jnp.einsum("rak,rkp->rap", scaled, tables, preferred_element_type=jnp.float32)
    images = images.reshape(row_count, 2, 2, fields, padded)
    values = jnp.where(upper_half[:, None, None, :], images[:, :, 1], images[:, :, 0])
    values = jnp.where(occupied[:, None, None, :], values, 0.0).astype(jnp.bfloat16)
    squared = (values.astype(jnp.float32) * values.astype(jnp.float32)).astype(jnp.bfloat16)
    selector = jnp.stack([jnp.logical_not(upper_half), upper_half], 1)
    by_cycle = jnp.where(
        selector[:, None, :, None, :], squared[:, :, None, :, :], jnp.zeros((), jnp.bfloat16)
    )
    by_cycle = by_cycle.reshape(row_count, 4 * fields, padded)
    returned = jnp.einsum("rap,rkp->rak", by_cycle, tables, preferred_element_type=jnp.float32)
    returned = returned.reshape(row_count, 2, 2, fields, 2, slot_count)
    factor = jnp.where(
        resolved, weights[:, :, None] / lens_pair[:, :, None].astype(jnp.float32), 0.0
    )
    returned = (returned * factor[:, None, :, None, None, :]).astype(jnp.bfloat16)
    return (values, returned)


def parity_of(degree_ids, own_orders):
    return jnp.where((degree_ids[None, :] + own_orders[:, None]) % 2 == 0, 1.0, -1.0)


def general(spec, legendre, gauss_w, cycle_len, wave_map):
    slots_dev = spec.shape[0]
    fields = spec.shape[1]
    degrees_all = spec.shape[3]
    slot_count = wave_map.shape[0]
    orders = wave_map * degrees_all // slot_count
    wave_pos = lax.axis_index("wave")
    own_orders = lax.dynamic_slice_in_dim(orders, wave_pos * slots_dev, slots_dev)
    degrees = jnp.arange(degrees_all, dtype=jnp.int32)
    retained = degrees[None, :] >= own_orders[:, None]
    coefficients = jnp.where(retained[:, None, None, :], spec, jnp.zeros((), jnp.bfloat16))
    panels = lax.all_gather(legendre, "lev", axis=1, tiled=True)
    sign_flip = parity_of(degrees, own_orders)
    flipped = (coefficients.astype(jnp.float32) * sign_flip[:, None, None, :]).astype(jnp.bfloat16)
    stacked = jnp.stack([coefficients, flipped], 1)
    fourier = jnp.einsum(
        "shfcn,snq->shfcq", stacked, panels, preferred_element_type=jnp.float32
    ).astype(jnp.bfloat16)
    cycle_waves = lax.all_to_all(fourier, "wave", split_axis=4, concat_axis=0, tiled=True)
    local_lats = cycle_waves.shape[4]
    row_total = local_lats // 2
    lat_start = wave_pos * local_lats
    lens_here = lax.dynamic_slice_in_dim(cycle_len, lat_start, local_lats)
    weights_here = lax.dynamic_slice_in_dim(gauss_w, lat_start, local_lats)
    row_block = block_rows()
    blocks = row_total // row_block
    ordered = cycle_waves.reshape(slot_count, 2, fields, 2, row_total, 2).transpose(
        4, 1, 5, 2, 3, 0
    )
    ordered = ordered.reshape(blocks, row_block, 2, 2, fields, 2, slot_count)

    def run_block(operands):
        return cycle_block(operands[0], operands[1], operands[2], orders, LPAD)

    values, returned = lax.map(
        run_block,
        (
            ordered,
            lens_here.reshape(blocks, row_block, 2),
            weights_here.reshape(blocks, row_block, 2),
        ),
    )
    grid = values.reshape(row_total, 2, fields, LPAD).transpose(1, 0, 2, 3)
    returned = returned.reshape(row_total, 2, 2, fields, 2, slot_count).transpose(5, 1, 3, 4, 0, 2)
    returned = returned.reshape(slot_count, 2, fields, 2, local_lats)
    spectral = lax.all_to_all(returned, "wave", split_axis=0, concat_axis=4, tiled=True)
    both = jnp.einsum("shfcq,snq->shfcn", spectral, panels, preferred_element_type=jnp.float32)
    total = both[:, 0] + sign_flip[:, None, None, :] * both[:, 1]
    spec_out = jnp.where(retained[:, None, None, :], total, 0.0)
    return (grid, spec_out)


LANES = 128
SUBLANES = 8
STEPS = 2
PIECES = 4
VMEM = 8 * 1024 * 1024
SINE = (6.28318516, -41.34165503, 81.60100407, -76.54978222, 39.53670553)


def circle(x, period, inverse):
    turn = (x - period * jnp.floor(x * inverse + 0.5)) * inverse
    away = jnp.abs(turn)
    values = []
    for v in (0.25 - away, 0.25 - jnp.abs(away - 0.25)):
        y = v * v
        series = SINE[4]
        for coefficient in SINE[3::-1]:
            series = series * y + coefficient
        values.append(v * series)
    return values[0], jnp.where(turn < 0.0, -values[1], values[1])


def params(memory=VMEM):
    return pltpu.CompilerParams(vmem_limit_bytes=memory)


def cost(flops, nbytes):
    return pl.CostEstimate(flops=flops, bytes_accessed=nbytes, transcendentals=0)


def at_wave():
    return lax.axis_index("wave")


def at_level():
    return lax.axis_index("lev")


def smem():
    return pl.BlockSpec(memory_space=pltpu.SMEM)


def vmem():
    return pl.BlockSpec(memory_space=pltpu.VMEM)


def parity_signs(rows, degrees_all):
    def kernel(o_ref):
        row = lax.broadcasted_iota(jnp.int32, (rows, degrees_all), 0)
        degree = lax.broadcasted_iota(jnp.int32, (rows, degrees_all), 1)
        odd = jnp.logical_and(row >= rows // 2, (degree & 1) == 1)
        o_ref[...] = jnp.where(odd, -1.0, 1.0)

    return pl.pallas_call(
        kernel,
        out_shape=jax.ShapeDtypeStruct((rows, degrees_all), jnp.float32),
        out_specs=vmem(),
        compiler_params=params(),
        cost_estimate=cost(4 * 10**9, 10**6),
        name="parity_signs",
    )()


def partial_fourier(first, factor, others, panels, slots, waves, wide):
    chips = len(others) + 1
    rows, degrees_all = first.shape
    parts = rows // (2 * slots)
    depth, lats = panels[0].shape
    own, here = depth // slots, lats // waves

    def kernel(first_ref, factor_ref, *refs):
        spec_refs, panel_refs = refs[: chips - 1], refs[chips - 1 : chips + 1]
        o_ref, left_ref = refs[chips + 1 :]
        factor = factor_ref[...]
        whole = [first_ref[...]]
        for ref in spec_refs:
            x = [ref[s].astype(jnp.float32) for s in range(slots)]
            whole.append(jnp.concatenate(x + x, axis=0) * factor)
        whole = jnp.concatenate(whole, axis=0)
        slot_of = lax.broadcasted_iota(jnp.int32, (chips * rows, own), 0) // parts % slots
        for level in range(2 * chips):

            @pl.when(at_level() == level)
            def _(level=level):
                for e in range(2):
                    start = (level ^ e) * own
                    piece = whole[:, start : start + own]
                    left = [jnp.where(slot_of == s, piece, 0.0) for s in range(slots)]
                    left_ref[e] = jnp.concatenate(left, axis=1).astype(jnp.bfloat16)

        total = jnp.dot(left_ref[0], panel_refs[0][...], preferred_element_type=jnp.float32)
        total += jnp.dot(left_ref[1], panel_refs[1][...], preferred_element_type=jnp.float32)
        chip = at_level() // 2
        fill = jnp.zeros((rows, wide - here), jnp.float32)
        for i in range(chips):
            mine = total[i * rows : (i + 1) * rows]
            for j in range(waves):
                value = mine[:, j * here : (j + 1) * here]
                value = jnp.concatenate([value, fill], axis=1)
                o_ref[j, chip ^ i] = value.astype(jnp.bfloat16)

    return pl.pallas_call(
        kernel,
        out_shape=jax.ShapeDtypeStruct((waves, chips, rows, wide), jnp.bfloat16),
        in_specs=[vmem()] * (chips + 3),
        out_specs=vmem(),
        scratch_shapes=[pltpu.VMEM((2, chips * rows, depth), jnp.bfloat16)],
        compiler_params=params(),
        cost_estimate=cost(10**9, 2 * 10**6),
        name="partial_fourier",
    )(first, factor, *others, *panels)


def quadratic(held, parts_sum, lens, weights, waves, step):
    sources, rows, wide = parts_sum.shape
    slot_count = held.shape[0]
    levels = sources // waves
    slots = slot_count // waves
    tiles = wide // LANES
    top = 2 * (slot_count - 1)
    shape = (SUBLANES, LANES)

    def kernel(held_ref, x_ref, len_ref, weight_ref, g_ref, o_ref, z_ref, r_ref, s_ref):
        half = rows // 2
        z_ref[...] = jnp.zeros(z_ref.shape, jnp.float32)
        for i in range(waves):
            total = x_ref[i * levels].astype(jnp.float32)
            for j in range(1, levels):
                total = total + x_ref[i * levels + j].astype(jnp.float32)
            total = total.astype(jnp.bfloat16).astype(jnp.float32)
            for h in range(2):
                for t in range(tiles):
                    at = i * half * SUBLANES + h * (SUBLANES // 2) + t
                    z_ref[pl.ds(at, half, stride=SUBLANES), :] = total[
                        h * half : (h + 1) * half, t * LANES : (t + 1) * LANES
                    ]
        lens_here = len_ref[...]
        kept = [
            jnp.where(lens_here > 2.0 * step * w, 1.0, 0.0) for w in range(slot_count)
        ]
        held = [
            [held_ref[w, i : i + 1, :] > 0.5 for i in range(slot_count)] for w in range(slot_count)
        ]
        real, imag = [], []
        for w in range(slot_count):
            re, im = jnp.zeros(shape, jnp.float32), jnp.zeros(shape, jnp.float32)
            for i in range(slot_count):
                at = i * 2 * SUBLANES
                re = jnp.where(held[w][i], z_ref[at : at + SUBLANES, :], re)
                im = jnp.where(held[w][i], z_ref[at + SUBLANES : at + 2 * SUBLANES, :], im)
            real.append(re * kept[w])
            imag.append(im * kept[w])
        for w in range(slot_count):
            double = 1.0 if w == 0 else 2.0
            at = 2 * w * SUBLANES
            g_ref[at : at + SUBLANES, :] = real[w] * double
            g_ref[at + SUBLANES : at + 2 * SUBLANES, :] = imag[w] * double
        imag[0] = jnp.zeros(shape, jnp.float32)
        square_real, square_imag = [], []
        for n in range(top + 1):
            re, im = jnp.zeros(shape, jnp.float32), jnp.zeros(shape, jnp.float32)
            for a in range(max(0, n - slot_count + 1), (n + 1) // 2):
                b = n - a
                re = re + (real[a] * real[b] - imag[a] * imag[b])
                im = im + (real[a] * imag[b] + imag[a] * real[b])
            for b in range(1, slot_count - n):
                a = n + b
                re = re + (real[a] * real[b] + imag[a] * imag[b])
                im = im + (imag[a] * real[b] - real[a] * imag[b])
            re, im = 2.0 * re, 2.0 * im
            if n % 2 == 0:
                a = n // 2
                re = re + (real[a] * real[a] - imag[a] * imag[a])
                im = im + 2.0 * (real[a] * imag[a])
            square_real.append(re)
            square_imag.append(im)
        whole = {
            d: jnp.where(lens_here == 1.0 * step * d, 1.0, 0.0)
            for d in range(3, top + slot_count)
        }
        weights_here = weight_ref[...]
        result = []
        for w in range(slot_count):
            re, im = square_real[w], square_imag[w]
            if w == 0:
                im = jnp.zeros(shape, jnp.float32)
            else:
                for n in range(w + 1, top + 1):
                    re = re + whole[w + n] * square_real[n]
                    im = im - whole[w + n] * square_imag[n]
            factor = kept[w] * weights_here
            result.append((re * factor, im * factor))
        for i in range(slot_count):
            re, im = result[0]
            for w in range(1, slot_count):
                re = jnp.where(held[w][i], result[w][0], re)
                im = jnp.where(held[w][i], result[w][1], im)
            at = i * 2 * SUBLANES
            r_ref[at : at + SUBLANES, :] = re
            r_ref[at + SUBLANES : at + 2 * SUBLANES, :] = im
        for i in range(waves):
            for h in range(2):
                for t in range(tiles):
                    start = i * half * SUBLANES + h * (SUBLANES // 2) + t
                    s_ref[h * half : (h + 1) * half, t * LANES : (t + 1) * LANES] = r_ref[
                        pl.ds(start, half, stride=SUBLANES), :
                    ]
            packed = s_ref[...].astype(jnp.bfloat16)
            for j in range(levels):
                o_ref[i * levels + j] = packed

    return pl.pallas_call(
        kernel,
        out_shape=(
            jax.ShapeDtypeStruct((2 * slot_count * SUBLANES, LANES), jnp.float32),
            jax.ShapeDtypeStruct((sources, rows, wide), jnp.bfloat16),
        ),
        in_specs=[vmem()] * 4,
        out_specs=(vmem(), vmem()),
        scratch_shapes=[
            pltpu.VMEM((2 * slot_count * SUBLANES, LANES), jnp.float32),
            pltpu.VMEM((2 * slot_count * SUBLANES, LANES), jnp.float32),
            pltpu.VMEM((rows, wide), jnp.float32),
        ],
        compiler_params=params(),
        name="quadratic",
    )(held, parts_sum, lens, weights)


def lane_facts(slot_count):
    lane = lax.broadcasted_iota(jnp.int32, (SUBLANES, LANES), 1)
    return (lane % (4 * slot_count) // 4, lane % 4 // 2, lane // (4 * slot_count), lane % 2)


def tile_of_row(block, span, slot_count):
    at = lax.broadcasted_iota(jnp.int32, (SUBLANES, LANES), 0) + block * SUBLANES
    at = at - lane_facts(slot_count)[2] * span % SUBLANES
    return at // 2, jnp.logical_and(at >= 0, at < span)


def prepare(cycle_len, gauss_w, wave_map, spec, panel, signs, span, step, waves, groups, wide):
    slot_count = wave_map.shape[0]
    slots, parts, degrees_all = spec.shape
    own = panel.shape[0] // slots
    levels = degrees_all // own
    rows = 2 * slots * parts
    here = cycle_len.shape[0] // waves
    tiles = wide // LANES
    per = SUBLANES // 2

    def kernel(
        len_ref, map_ref, len_row_ref, weight_row_ref, x_ref, panel_ref, sign_ref,
        first_ref, factor_ref, factors_ref, near_ref, o_ref, lens_ref, weights_ref, held_ref, sem,
    ):
        copy = pltpu.make_async_copy(panel_ref, near_ref, sem)
        copy.start()
        row_of = lax.broadcasted_iota(jnp.int32, (rows, degrees_all), 0)
        degree = lax.broadcasted_iota(jnp.int32, (rows, degrees_all), 1)
        bound = jnp.zeros((rows, degrees_all), jnp.int32)
        for s in range(slots):
            mine = row_of // parts % slots == s
            bound = jnp.where(mine, map_ref[at_wave() * slots + s] * step, bound)
        turned = jnp.logical_and(row_of >= rows // 2, (bound & 1) == 1)
        sign = sign_ref[...]
        factor = jnp.where(degree >= bound, jnp.where(turned, -sign, sign), 0.0)
        factor_ref[...] = factor
        x = [x_ref[s].astype(jnp.float32) for s in range(slots)]
        first_ref[...] = jnp.concatenate(x + x, axis=0) * factor
        for level in range(levels):

            @pl.when(at_level() == level)
            def _(level=level):
                for e in range(2):
                    start = (level ^ e) * own
                    factors_ref[e] = factor[:, start : start + own]

        for i in range(slot_count):
            for w in range(slot_count):
                held = jnp.where(map_ref[i] == w, 1.0, 0.0)
                held_ref[w, i : i + 1, :] = jnp.full((1, LANES), held, jnp.float32)

        lens_ref[...] = jnp.full((SUBLANES, LANES), 4.0, jnp.float32)
        weights_ref[...] = jnp.zeros((SUBLANES, LANES), jnp.float32)
        for v in range(waves):

            @pl.when(at_wave() == v)
            def _(v=v):
                for t in range(tiles):
                    size = min(LANES, here - t * LANES)
                    at = v * here + t * LANES
                    lens = len_row_ref[at : at + size].astype(jnp.float32).reshape(1, size)
                    weights = weight_row_ref[at : at + size].reshape(1, size)
                    for h in range(2):
                        k = h * (SUBLANES // 2) + t
                        lens_ref[k : k + 1, 0:size] = lens
                        weights_ref[k : k + 1, 0:size] = weights

        wave, part, row, cycle = lane_facts(slot_count)
        tile, _ = tile_of_row(0, span, slot_count)
        first = (tile * LANES).astype(jnp.float32)
        order = (step * wave).astype(jnp.float32)
        stride = order * (LANES * SUBLANES / 2.0)
        imag = part == 1
        way = (1 - 2 * cycle).astype(jnp.float32)
        down = lax.broadcasted_iota(jnp.int32, (SUBLANES, LANES), 0)
        turn = step * lax.broadcasted_iota(jnp.int32, (SUBLANES, LANES), 1).astype(jnp.float32)
        mine = [row == i // 2 if i % 2 == 0 else jnp.logical_and(row == i // 2, cycle == 1) for i in range(SUBLANES)]
        second = down % 2 == 1
        start = at_wave() * here

        def body(g, carry):
            lens = [
                len_ref[start + jnp.minimum(g * SUBLANES + i, here - 1)] for i in range(SUBLANES)
            ]
            length = jnp.full((SUBLANES, LANES), lens[0], jnp.int32)
            length_down, before, before_down = length, length, length
            for i in range(1, SUBLANES):
                length = jnp.where(mine[i], lens[i], length)
                length_down = jnp.where(down == i, lens[i], length_down)
            for r in range(1, per):
                before = jnp.where(row == r, lens[2 * r], before)
                before_down = jnp.where(down // 2 == r, lens[2 * r], before_down)
            length = length.astype(jnp.float32)
            offset = jnp.where(cycle == 1, before, 0).astype(jnp.float32)
            split = (before >> (LANES.bit_length() - 1)).astype(jnp.float32)
            marks = jnp.where(second, before_down + length_down, before_down & (LANES - 1))
            length_down = length_down.astype(jnp.float32)
            inverse = 1.0 / length
            cos, sin = circle(order * (first - offset), length, inverse)
            o_ref[g, 0] = jnp.where(imag, sin, cos)
            o_ref[g, 1] = jnp.where(imag, cos, -sin)
            cos, sin = circle(stride, length, inverse)
            turns = jnp.where(down == 0, cos, sin)
            o_ref[g, 2] = jnp.where(down < 2, turns, way * split)
            cos, sin = circle(turn, length_down, 1.0 / length_down)
            o_ref[g, 3] = cos
            o_ref[g, 4] = -sin
            o_ref[g, 5] = 1.0 - 2.0 * sin * sin
            o_ref[g, 6] = -2.0 * sin * cos
            o_ref[g, 7] = marks.astype(jnp.float32)
            return carry

        lax.fori_loop(0, groups, body, 0, unroll=19)
        copy.wait()

    flat = jax.ShapeDtypeStruct((SUBLANES, LANES), jnp.float32)
    return pl.pallas_call(
        kernel,
        out_shape=(
            jax.ShapeDtypeStruct((rows, degrees_all), jnp.float32),
            jax.ShapeDtypeStruct((rows, degrees_all), jnp.float32),
            jax.ShapeDtypeStruct((2, rows, own), jnp.float32),
            jax.ShapeDtypeStruct(panel.shape, panel.dtype),
            jax.ShapeDtypeStruct((groups, 8, SUBLANES, LANES), jnp.float32),
            flat,
            flat,
            jax.ShapeDtypeStruct((slot_count, slot_count, LANES), jnp.float32),
        ),
        in_specs=[smem()] * 2 + [vmem()] * 3 + [pl.BlockSpec(memory_space=pl.ANY), vmem()],
        out_specs=(vmem(),) * 8,
        scratch_shapes=[pltpu.SemaphoreType.DMA],
        compiler_params=params(),
        cost_estimate=cost(3 * 10**9, 10**6),
        name="prepare",
    )(cycle_len, wave_map, cycle_len, gauss_w, spec, panel, signs)


def grid_values(fourier, tables, span, slot_count, rows_out, tiles):
    groups = tables.shape[0]
    per = SUBLANES // 2
    block = groups // STEPS
    blocks = -(-(span + SUBLANES // 2) // SUBLANES)
    size = 4 * slot_count
    kinds = 4 * slot_count
    around = LANES // SUBLANES

    total = rows_out * span
    tail = total % (2 * SUBLANES)
    tail_group, tail_at = divmod(total - tail, per * span)

    def kernel(fourier_ref, table_ref, o_hbm, rows_ref, wave_ref, part_ref, tail_ref, sems):
        wave, _, row, cycle = lane_facts(slot_count)
        way = (1 - 2 * cycle).astype(jnp.float32)
        point = lax.broadcasted_iota(jnp.int32, (SUBLANES, LANES), 1).astype(jnp.float32)
        down = lax.broadcasted_iota(jnp.int32, (SUBLANES, LANES), 0)
        second = down % 2 == 1
        unit = jnp.where(down < 2, 1.0, 0.0)
        beside = jnp.where(down < 6, -1.0, 1.0)
        for c in range(2):
            for h in range(2):
                for t in range(tiles):
                    at = (c * 2 + h) * slot_count
                    k = c * SUBLANES + h * (SUBLANES // 2) + t
                    rows_ref[t, at : at + slot_count, :] = fourier_ref[
                        pl.ds(k, slot_count, stride=2 * SUBLANES), :
                    ]
        pick = lax.broadcasted_iota(jnp.int32, (LANES, LANES), 0)
        lane = lax.broadcasted_iota(jnp.int32, (LANES, LANES), 1)
        pick = jnp.where(pick == lane // size * 2 + lane % 2, 1.0, 0.0).astype(jnp.bfloat16)

        turned = []
        for g in range(groups):
            shift = -g % around * SUBLANES
            value = rows_ref[g // around]
            turned.append(pltpu.roll(value, shift, 1) if shift else value)
        spread = jnp.dot(
            jnp.concatenate(turned, axis=0).astype(jnp.bfloat16), pick, preferred_element_type=jnp.float32
        )
        for g in range(groups):
            sums = []
            for k in range(4):
                at = g * kinds + k * slot_count
                value = jnp.where(down == wave, spread[at : at + SUBLANES], 0.0)
                sums.append(jnp.sum(value, axis=0, keepdims=True))
            for c in range(2):
                wave_ref[g, c] = jnp.where(down % 2 == 0, sums[2 * c], sums[2 * c + 1])

        def one_group(base, i, g):
            real, imag = wave_ref[g, 0], wave_ref[g, 1]
            x = real * table_ref[g, 0] + imag * table_ref[g, 1]
            y = real * table_ref[g, 1] - imag * table_ref[g, 0]
            turn_cos, turn_sin = table_ref[g, 2, 0:1], table_ref[g, 2, 1:2]
            split = table_ref[g, 2, 2:3]
            main, mixed = [], []
            for k in range(blocks):
                if k:
                    x, y = x * turn_cos + y * turn_sin, y * turn_cos - x * turn_sin
                tile, inside = tile_of_row(k, span, slot_count)
                apart = tile.astype(jnp.float32) * way - split
                value = jnp.where(inside, x, 0.0) if k in (0, blocks - 1) else x
                main.append(jnp.where(apart < 0.0, value, 0.0))
                mixed.append(jnp.where(apart == 0.0, value, 0.0))
            main, mixed = jnp.concatenate(main, axis=0), jnp.concatenate(mixed, axis=0)
            left = jnp.concatenate([main, mixed], axis=1).astype(jnp.bfloat16)

            columns, ends = [], []
            for r in range(per):
                ends.append(table_ref[g, 7, 2 * r + 1 : 2 * r + 2])
                cos1, sin1, cos2, sin2 = [
                    jnp.where(
                        second,
                        table_ref[g, i, 2 * r + 1 : 2 * r + 2],
                        table_ref[g, i, 2 * r : 2 * r + 1],
                    )
                    for i in range(3, 7)
                ]
                twice = 2.0 * cos2
                series = [jnp.where(down < 4, unit, jnp.where(down < 6, cos1, sin1))]
                third = series[0] * (twice + beside)
                series.append(jnp.where(down < 2, cos2, jnp.where(down < 4, sin2, third)))
                here = jnp.logical_xor(point < table_ref[g, 7, 2 * r : 2 * r + 1], second)
                for _ in range(2, size // SUBLANES):
                    series.append(twice * series[-1] - series[-2])
                full = jnp.concatenate(series, axis=0).astype(jnp.bfloat16)
                part = jnp.concatenate([jnp.where(here, v, 0.0) for v in series], axis=0).astype(jnp.bfloat16)
                before = [jnp.zeros((r * size, LANES), jnp.bfloat16)] if r else []
                after = [jnp.zeros((LANES - (r + 1) * size, LANES), jnp.bfloat16)] if r < per - 1 else []
                columns.append(jnp.concatenate(before + [full] + after + before + [part] + after, axis=0))
            right = jnp.concatenate(columns, axis=1)
            product = jnp.dot(left, right, preferred_element_type=jnp.float32)
            places = {}
            for r in range(per):
                shift = r * span % SUBLANES
                for k in range(blocks):
                    if k * SUBLANES >= shift + span:
                        continue
                    value = product[k * SUBLANES : (k + 1) * SUBLANES, r * LANES : (r + 1) * LANES]
                    if k == blocks - 1:
                        position = ((down + k * SUBLANES - shift) // 2 * LANES).astype(jnp.float32) + point
                        value = jnp.where(position < ends[r], value, 0.0)
                    places.setdefault((r * span - shift) // SUBLANES + k, []).append(value)
            whole = [functools.reduce(lambda a, b: a + b, places[k]) for k in sorted(places)]
            size_out = per * span
            part_ref[base, i * size_out : (i + 1) * size_out, :] = jnp.concatenate(
                whole, axis=0
            ).astype(jnp.bfloat16)
            if tail and i == tail_group % block:
                tail_ref[...] = whole[tail_at // SUBLANES].astype(jnp.bfloat16)

        size_out = per * span
        cuts = [piece * block // PIECES for piece in range(PIECES + 1)]

        def copy(i, piece):
            start, end = cuts[piece] * size_out, cuts[piece + 1] * size_out
            place = i * block * size_out
            size = min(end, total - tail - place) - start
            return pltpu.make_async_copy(
                part_ref.at[i, pl.ds(start, size), :],
                o_hbm.at[pl.ds(place + start, size), :],
                sems.at[PIECES * i + piece],
            )

        def step(base, carry):
            for piece in range(PIECES):
                for i in range(cuts[piece], cuts[piece + 1]):
                    one_group(base, i, base * block + i)
                for i in range(STEPS):

                    @pl.when(base == i)
                    def _(i=i, piece=piece):
                        copy(i, piece).start()

            return carry

        lax.fori_loop(0, STEPS, step, 0)
        if tail:
            rest = pltpu.make_async_copy(
                tail_ref, o_hbm.at[pl.ds(total - tail, tail), :], sems.at[PIECES * STEPS]
            )
            rest.start()
        for i in range(STEPS):
            for piece in range(PIECES):
                copy(i, piece).wait()
        if tail:
            rest.wait()

    return pl.pallas_call(
        kernel,
        out_shape=jax.ShapeDtypeStruct((rows_out * span, LANES), jnp.bfloat16),
        in_specs=[vmem()] * 2,
        out_specs=pl.BlockSpec(memory_space=pl.ANY),
        scratch_shapes=[
            pltpu.VMEM((tiles, kinds, LANES), jnp.float32),
            pltpu.VMEM((groups, 2, SUBLANES, LANES), jnp.float32),
            pltpu.VMEM((STEPS, block * per * span, LANES), jnp.bfloat16),
            pltpu.VMEM((SUBLANES, LANES), jnp.bfloat16),
            pltpu.SemaphoreType.DMA((PIECES * STEPS + 1,)),
        ],
        compiler_params=params(16 * 1024 * 1024),
        cost_estimate=cost(8 * 10**9, 3 * 10**6),
        name="grid_values",
    )(fourier, tables)


def direct(returned, factors, panels):
    waves, tall, _ = returned.shape
    depth, lats = panels[0].shape
    own, here = factors.shape[2], lats // waves
    slots, half = depth // own, factors.shape[1] // 2
    chips = tall // (2 * half)

    def kernel(x_ref, factor_ref, own_ref, other_ref, *refs):
        o_refs, left_ref, all_ref = refs[:chips], refs[chips], refs[chips + 1]
        for j in range(waves):
            left_ref[:, j * here : (j + 1) * here] = x_ref[j, :, 0:here].astype(jnp.float32)
        left = left_ref[...].astype(jnp.bfloat16)
        shape = (chips, half, own)
        slot_of = lax.broadcasted_iota(jnp.int32, shape, 1) // 2
        for e, panel_ref in enumerate((own_ref, other_ref)):
            total = lax.dot_general(
                left, panel_ref[...], (((1,), (1,)), ((), ())), preferred_element_type=jnp.float32
            ).reshape(chips, 2 * half, depth)
            result = jnp.zeros(shape, jnp.float32)
            for s in range(slots):
                mine = total[:, :, s * own : (s + 1) * own] * factor_ref[e][None]
                result = jnp.where(slot_of == s, mine[:, :half] + mine[:, half:], result)
            all_ref[:, e * half : (e + 1) * half, :] = result
        for i in range(chips):
            o_refs[i][...] = all_ref[(at_level() // 2) ^ i]

    return pl.pallas_call(
        kernel,
        out_shape=(jax.ShapeDtypeStruct((2 * half, own), jnp.float32),) * chips,
        in_specs=[vmem()] * 4,
        out_specs=(vmem(),) * chips,
        scratch_shapes=[
            pltpu.VMEM((tall, lats), jnp.float32),
            pltpu.VMEM((chips, 2 * half, own), jnp.float32),
        ],
        compiler_params=params(),
        cost_estimate=cost(10**9, 2 * 10**6),
        name="direct",
    )(returned, factors, *panels)


def join_degrees(pieces, slots):
    chips = len(pieces)
    rows, own = pieces[0].shape
    half = rows // 2

    def kernel(*refs):
        piece_refs, o_ref, all_ref = refs[:chips], refs[chips], refs[chips + 1]
        for i in range(chips):
            for e in range(2):
                all_ref[at_level() ^ (2 * i + e)] = piece_refs[i][e * half : (e + 1) * half, :]
        whole = jnp.concatenate([all_ref[v] for v in range(2 * chips)], axis=1)
        for s in range(slots):
            o_ref[s] = whole[2 * s : 2 * s + 2]

    return pl.pallas_call(
        kernel,
        out_shape=jax.ShapeDtypeStruct((slots, 2, 2 * chips * own), jnp.float32),
        in_specs=[vmem()] * chips,
        out_specs=vmem(),
        scratch_shapes=[pltpu.VMEM((2 * chips, half, own), jnp.float32)],
        compiler_params=params(),
        name="join_degrees",
    )(*pieces)


def evenly_spaced(levels, spec, legendre, gauss_w, cycle_len, wave_map):
    slots = spec.shape[0]
    degrees_all = spec.shape[3]
    own = legendre.shape[1]
    lats = legendre.shape[2]
    slot_count = wave_map.shape[0]
    step = degrees_all // slot_count
    waves = slot_count // slots
    chips = levels // 2

    def across(x, bits):
        return lax.ppermute(x, "lev", [(j, j ^ bits) for j in range(levels)])

    def same_core(x):
        groups = [[j for j in range(waves * levels) if j % 2 == core] for core in range(2)]
        return lax.all_to_all(x, ("wave", "lev"), 0, 0, tiled=True, axis_index_groups=groups)

    mine = spec.reshape(slots, 2, degrees_all)
    others = [across(mine, 2 * i) for i in range(1, chips)]
    panel = legendre.reshape(slots * own, lats)
    signs = parity_signs(2 * slots * 2, degrees_all)
    here = lats // waves
    wide = -(-here // LANES) * LANES
    tiles = wide // LANES
    per = SUBLANES // 2
    rows_out = here // 2
    groups = -(-rows_out // (per * STEPS)) * STEPS
    span = 2 * (LPAD // LANES)
    rows_here = 2 * slots * 2
    first, factor, factors, near, tables, lens, weights, held = prepare(
        cycle_len, gauss_w, wave_map, mine, panel, signs, span, step, waves, groups, wide
    )
    panels = (near, across(panel, 1))

    part = partial_fourier(first, factor, others, panels, slots, waves, wide)
    part = same_core(part.reshape(waves * chips, rows_here, wide))
    fourier, returned = quadratic(held, part, lens, weights, waves, step)
    returned = same_core(returned)

    values = grid_values(fourier, tables, span, slot_count, rows_out, tiles)
    values = values.reshape(rows_out, span // 2, 2, LANES)
    values = with_layout_constraint(values, Layout(major_to_minor=(0, 1, 2, 3)))
    values = values.transpose(0, 2, 1, 3)
    values = with_layout_constraint(values, Layout(major_to_minor=(0, 2, 1, 3)))
    values = values.reshape(rows_out, 2, LPAD)
    values = with_layout_constraint(values, Layout(major_to_minor=(0, 1, 2)))
    grid = values.transpose(1, 0, 2).reshape(2, rows_out, 1, LPAD)

    returned = returned.reshape(waves, chips * rows_here, wide)
    pieces = direct(returned, factors, (panel, panels[1]))
    pieces = [pieces[0]] + [across(pieces[i], 2 * i) for i in range(1, chips)]
    spec_out = join_degrees(pieces, slots).reshape(slots, 1, 2, degrees_all)
    return (grid, spec_out)


def per_device(levels, spec, legendre, gauss_w, cycle_len, wave_map):
    slot_count = wave_map.shape[0]
    fits = (
        spec.shape[3] % slot_count == 0
        and 2 * slot_count * SUBLANES == LANES
        and spec.shape[1] == 1
        and 4 * spec.shape[0] == SUBLANES
        and levels > 1
        and levels & (levels - 1) == 0
    )
    if fits:
        return evenly_spaced(levels, spec, legendre, gauss_w, cycle_len, wave_map)
    return general(spec, legendre, gauss_w, cycle_len, wave_map)


def solution(mesh):
    placed = (P("wave", "lev", None, None), P("wave", "lev", None), P(), P(), P())
    return jax.shard_map(
        functools.partial(per_device, mesh.shape["lev"]),
        mesh=mesh,
        in_specs=placed,
        out_specs=(P(None, "wave", "lev", None), P("wave", "lev", None, None)),
        check_vma=False,
    )
```

```python
import functools
import math

import jax
import jax.numpy as jnp
from jax import lax
from jax.experimental import pallas as pl
from jax.experimental.layout import Layout, with_layout_constraint
from jax.experimental.pallas import tpu as pltpu
from jax.sharding import PartitionSpec as P

LPAD = 4864


def block_rows():
    for candidate in (10, 8, 6, 5, 4, 3, 2):
        return candidate
    return 1


def cycle_tables(lens_pair, orders, padded):
    position = jnp.arange(padded, dtype=jnp.int32)[None, :]
    first_len = lens_pair[:, 0:1]
    second = lens_pair[:, 1:2]
    upper_half = position >= first_len
    occupied = position < first_len + second
    offset = jnp.where(upper_half, position - first_len, position)
    length = jnp.where(upper_half, second, first_len)
    turn_count = orders[None, :, None] * offset[:, None, :] % length[:, None, :]
    angles = 2.0 * math.pi * turn_count.astype(jnp.float32) / length[:, None, :].astype(jnp.float32)
    cosine = jnp.where(occupied[:, None, :], jnp.cos(angles), 0.0).astype(jnp.bfloat16)
    minus_sine = jnp.where(occupied[:, None, :], -jnp.sin(angles), 0.0).astype(jnp.bfloat16)
    return (jnp.concatenate([cosine, minus_sine], 1), upper_half, occupied)


def cycle_block(waves, lens_pair, weights, orders, padded):
    row_count = waves.shape[0]
    fields = waves.shape[3]
    slot_count = orders.shape[0]
    tables, upper_half, occupied = cycle_tables(lens_pair, orders, padded)
    double = jnp.where(orders == 0, 1.0, 2.0)
    resolved = 2 * orders[None, None, :] < lens_pair[:, :, None]
    widening = jnp.where(resolved, double[None, None, :], 0.0)
    scaled = (waves.astype(jnp.float32) * widening[:, None, :, None, None, :]).astype(jnp.bfloat16)
    scaled = scaled.reshape(row_count, 4 * fields, 2 * slot_count)
    images = jnp.einsum("rak,rkp->rap", scaled, tables, preferred_element_type=jnp.float32)
    images = images.reshape(row_count, 2, 2, fields, padded)
    values = jnp.where(upper_half[:, None, None, :], images[:, :, 1], images[:, :, 0])
    values = jnp.where(occupied[:, None, None, :], values, 0.0).astype(jnp.bfloat16)
    squared = (values.astype(jnp.float32) * values.astype(jnp.float32)).astype(jnp.bfloat16)
    selector = jnp.stack([jnp.logical_not(upper_half), upper_half], 1)
    by_cycle = jnp.where(
        selector[:, None, :, None, :], squared[:, :, None, :, :], jnp.zeros((), jnp.bfloat16)
    )
    by_cycle = by_cycle.reshape(row_count, 4 * fields, padded)
    returned = jnp.einsum("rap,rkp->rak", by_cycle, tables, preferred_element_type=jnp.float32)
    returned = returned.reshape(row_count, 2, 2, fields, 2, slot_count)
    factor = jnp.where(
        resolved, weights[:, :, None] / lens_pair[:, :, None].astype(jnp.float32), 0.0
    )
    returned = (returned * factor[:, None, :, None, None, :]).astype(jnp.bfloat16)
    return (values, returned)


def parity_of(degree_ids, own_orders):
    return jnp.where((degree_ids[None, :] + own_orders[:, None]) % 2 == 0, 1.0, -1.0)


def general(spec, legendre, gauss_w, cycle_len, wave_map):
    slots_dev = spec.shape[0]
    fields = spec.shape[1]
    degrees_all = spec.shape[3]
    slot_count = wave_map.shape[0]
    orders = wave_map * degrees_all // slot_count
    wave_pos = lax.axis_index("wave")
    own_orders = lax.dynamic_slice_in_dim(orders, wave_pos * slots_dev, slots_dev)
    degrees = jnp.arange(degrees_all, dtype=jnp.int32)
    retained = degrees[None, :] >= own_orders[:, None]
    coefficients = jnp.where(retained[:, None, None, :], spec, jnp.zeros((), jnp.bfloat16))
    panels = lax.all_gather(legendre, "lev", axis=1, tiled=True)
    sign_flip = parity_of(degrees, own_orders)
    flipped = (coefficients.astype(jnp.float32) * sign_flip[:, None, None, :]).astype(jnp.bfloat16)
    stacked = jnp.stack([coefficients, flipped], 1)
    fourier = jnp.einsum(
        "shfcn,snq->shfcq", stacked, panels, preferred_element_type=jnp.float32
    ).astype(jnp.bfloat16)
    cycle_waves = lax.all_to_all(fourier, "wave", split_axis=4, concat_axis=0, tiled=True)
    local_lats = cycle_waves.shape[4]
    row_total = local_lats // 2
    lat_start = wave_pos * local_lats
    lens_here = lax.dynamic_slice_in_dim(cycle_len, lat_start, local_lats)
    weights_here = lax.dynamic_slice_in_dim(gauss_w, lat_start, local_lats)
    row_block = block_rows()
    blocks = row_total // row_block
    ordered = cycle_waves.reshape(slot_count, 2, fields, 2, row_total, 2).transpose(
        4, 1, 5, 2, 3, 0
    )
    ordered = ordered.reshape(blocks, row_block, 2, 2, fields, 2, slot_count)

    def run_block(operands):
        return cycle_block(operands[0], operands[1], operands[2], orders, LPAD)

    values, returned = lax.map(
        run_block,
        (
            ordered,
            lens_here.reshape(blocks, row_block, 2),
            weights_here.reshape(blocks, row_block, 2),
        ),
    )
    grid = values.reshape(row_total, 2, fields, LPAD).transpose(1, 0, 2, 3)
    returned = returned.reshape(row_total, 2, 2, fields, 2, slot_count).transpose(5, 1, 3, 4, 0, 2)
    returned = returned.reshape(slot_count, 2, fields, 2, local_lats)
    spectral = lax.all_to_all(returned, "wave", split_axis=0, concat_axis=4, tiled=True)
    both = jnp.einsum("shfcq,snq->shfcn", spectral, panels, preferred_element_type=jnp.float32)
    total = both[:, 0] + sign_flip[:, None, None, :] * both[:, 1]
    spec_out = jnp.where(retained[:, None, None, :], total, 0.0)
    return (grid, spec_out)


LANES = 128
SUBLANES = 8
STEPS = 2
PIECES = 4
VMEM = 8 * 1024 * 1024
SINE = (6.28318516, -41.34165503, 81.60100407, -76.54978222, 39.53670553)


def circle(x, period, inverse):
    turn = (x - period * jnp.floor(x * inverse + 0.5)) * inverse
    away = jnp.abs(turn)
    values = []
    for v in (0.25 - away, 0.25 - jnp.abs(away - 0.25)):
        y = v * v
        series = SINE[4]
        for coefficient in SINE[3::-1]:
            series = series * y + coefficient
        values.append(v * series)
    return values[0], jnp.where(turn < 0.0, -values[1], values[1])


def params(memory=VMEM):
    return pltpu.CompilerParams(vmem_limit_bytes=memory)


def cost(flops, nbytes):
    return pl.CostEstimate(flops=flops, bytes_accessed=nbytes, transcendentals=0)


def at_wave():
    return lax.axis_index("wave")


def at_level():
    return lax.axis_index("lev")


def from_middle(count):
    return sorted(range(count), key=lambda i: (abs(2 * i - count + 1), -i))


def smem():
    return pl.BlockSpec(memory_space=pltpu.SMEM)


def vmem():
    return pl.BlockSpec(memory_space=pltpu.VMEM)


def parity_signs(rows, degrees_all):
    def kernel(o_ref):
        row = lax.broadcasted_iota(jnp.int32, (rows, degrees_all), 0)
        degree = lax.broadcasted_iota(jnp.int32, (rows, degrees_all), 1)
        odd = jnp.logical_and(row >= rows // 2, (degree & 1) == 1)
        o_ref[...] = jnp.where(odd, -1.0, 1.0)

    return pl.pallas_call(
        kernel,
        out_shape=jax.ShapeDtypeStruct((rows, degrees_all), jnp.float32),
        out_specs=vmem(),
        compiler_params=params(),
        cost_estimate=cost(4 * 10**9, 10**6),
        name="parity_signs",
    )()


def partial_fourier(first, factor, others, panels, slots, waves, wide):
    chips = len(others) + 1
    rows, degrees_all = first.shape
    parts = rows // (2 * slots)
    depth, lats = panels[0].shape
    own, here = depth // slots, lats // waves

    def kernel(first_ref, factor_ref, *refs):
        spec_refs, panel_refs = refs[: chips - 1], refs[chips - 1 : chips + 1]
        o_ref, left_ref = refs[chips + 1 :]
        factor = factor_ref[...]
        whole = [first_ref[...]]
        for ref in spec_refs:
            x = [ref[s].astype(jnp.float32) for s in range(slots)]
            whole.append(jnp.concatenate(x + x, axis=0) * factor)
        whole = jnp.concatenate(whole, axis=0)
        slot_of = lax.broadcasted_iota(jnp.int32, (chips * rows, own), 0) // parts % slots
        for level in range(2 * chips):

            @pl.when(at_level() == level)
            def _(level=level):
                for e in range(2):
                    start = (level ^ e) * own
                    piece = whole[:, start : start + own]
                    left = [jnp.where(slot_of == s, piece, 0.0) for s in range(slots)]
                    left_ref[e] = jnp.concatenate(left, axis=1).astype(jnp.bfloat16)

        total = jnp.dot(left_ref[0], panel_refs[0][...], preferred_element_type=jnp.float32)
        total += jnp.dot(left_ref[1], panel_refs[1][...], preferred_element_type=jnp.float32)
        chip = at_level() // 2
        places = [from_middle(waves).index(j) for j in range(waves)]
        fill = jnp.zeros((rows, wide - here), jnp.float32)
        for i in range(chips):
            mine = total[i * rows : (i + 1) * rows]
            for j in range(waves):
                value = mine[:, j * here : (j + 1) * here]
                value = jnp.concatenate([value, fill], axis=1)
                o_ref[places[j], chip ^ i] = value.astype(jnp.bfloat16)

    return pl.pallas_call(
        kernel,
        out_shape=jax.ShapeDtypeStruct((waves, chips, rows, wide), jnp.bfloat16),
        in_specs=[vmem()] * (chips + 3),
        out_specs=vmem(),
        scratch_shapes=[pltpu.VMEM((2, chips * rows, depth), jnp.bfloat16)],
        compiler_params=params(),
        cost_estimate=cost(10**9, 2 * 10**6),
        name="partial_fourier",
    )(first, factor, *others, *panels)


def quadratic(held, parts_sum, lens, weights, waves, step):
    sources, rows, wide = parts_sum.shape
    slot_count = held.shape[0]
    levels = sources // waves
    slots = slot_count // waves
    tiles = wide // LANES
    top = 2 * (slot_count - 1)
    shape = (SUBLANES, LANES)

    def kernel(held_ref, x_ref, len_ref, weight_ref, g_ref, o_ref, z_ref, r_ref, s_ref):
        half = rows // 2
        z_ref[...] = jnp.zeros(z_ref.shape, jnp.float32)
        for place, i in enumerate(from_middle(waves)):
            total = x_ref[place * levels].astype(jnp.float32)
            for j in range(1, levels):
                total = total + x_ref[place * levels + j].astype(jnp.float32)
            total = total.astype(jnp.bfloat16).astype(jnp.float32)
            for h in range(2):
                for t in range(tiles):
                    at = i * half * SUBLANES + h * (SUBLANES // 2) + t
                    z_ref[pl.ds(at, half, stride=SUBLANES), :] = total[
                        h * half : (h + 1) * half, t * LANES : (t + 1) * LANES
                    ]
        lens_here = len_ref[...]
        kept = [
            jnp.where(lens_here > 2.0 * step * w, 1.0, 0.0) for w in range(slot_count)
        ]
        held = [
            [held_ref[w, i : i + 1, :] > 0.5 for i in range(slot_count)] for w in range(slot_count)
        ]
        real, imag = [], []
        for w in range(slot_count):
            re, im = jnp.zeros(shape, jnp.float32), jnp.zeros(shape, jnp.float32)
            for i in range(slot_count):
                at = i * 2 * SUBLANES
                re = jnp.where(held[w][i], z_ref[at : at + SUBLANES, :], re)
                im = jnp.where(held[w][i], z_ref[at + SUBLANES : at + 2 * SUBLANES, :], im)
            real.append(re * kept[w])
            imag.append(im * kept[w])
        for w in range(slot_count):
            double = 1.0 if w == 0 else 2.0
            at = 2 * w * SUBLANES
            g_ref[at : at + SUBLANES, :] = real[w] * double
            g_ref[at + SUBLANES : at + 2 * SUBLANES, :] = imag[w] * double
        imag[0] = jnp.zeros(shape, jnp.float32)
        square_real, square_imag = [], []
        for n in range(top + 1):
            re, im = jnp.zeros(shape, jnp.float32), jnp.zeros(shape, jnp.float32)
            for a in range(max(0, n - slot_count + 1), (n + 1) // 2):
                b = n - a
                re = re + (real[a] * real[b] - imag[a] * imag[b])
                im = im + (real[a] * imag[b] + imag[a] * real[b])
            for b in range(1, slot_count - n):
                a = n + b
                re = re + (real[a] * real[b] + imag[a] * imag[b])
                im = im + (imag[a] * real[b] - real[a] * imag[b])
            re, im = 2.0 * re, 2.0 * im
            if n % 2 == 0:
                a = n // 2
                re = re + (real[a] * real[a] - imag[a] * imag[a])
                im = im + 2.0 * (real[a] * imag[a])
            square_real.append(re)
            square_imag.append(im)
        whole = {
            d: jnp.where(lens_here == 1.0 * step * d, 1.0, 0.0)
            for d in range(3, top + slot_count)
        }
        weights_here = weight_ref[...]
        result = []
        for w in range(slot_count):
            re, im = square_real[w], square_imag[w]
            if w == 0:
                im = jnp.zeros(shape, jnp.float32)
            else:
                for n in range(w + 1, top + 1):
                    re = re + whole[w + n] * square_real[n]
                    im = im - whole[w + n] * square_imag[n]
            factor = kept[w] * weights_here
            result.append((re * factor, im * factor))
        for i in range(slot_count):
            re, im = result[0]
            for w in range(1, slot_count):
                re = jnp.where(held[w][i], result[w][0], re)
                im = jnp.where(held[w][i], result[w][1], im)
            at = i * 2 * SUBLANES
            r_ref[at : at + SUBLANES, :] = re
            r_ref[at + SUBLANES : at + 2 * SUBLANES, :] = im
        for place, i in enumerate(from_middle(waves)):
            for h in range(2):
                for t in range(tiles):
                    start = i * half * SUBLANES + h * (SUBLANES // 2) + t
                    s_ref[h * half : (h + 1) * half, t * LANES : (t + 1) * LANES] = r_ref[
                        pl.ds(start, half, stride=SUBLANES), :
                    ]
            packed = s_ref[...].astype(jnp.bfloat16)
            for j in range(levels):
                o_ref[place * levels + j] = packed

    return pl.pallas_call(
        kernel,
        out_shape=(
            jax.ShapeDtypeStruct((2 * slot_count * SUBLANES, LANES), jnp.float32),
            jax.ShapeDtypeStruct((sources, rows, wide), jnp.bfloat16),
        ),
        in_specs=[vmem()] * 4,
        out_specs=(vmem(), vmem()),
        scratch_shapes=[
            pltpu.VMEM((2 * slot_count * SUBLANES, LANES), jnp.float32),
            pltpu.VMEM((2 * slot_count * SUBLANES, LANES), jnp.float32),
            pltpu.VMEM((rows, wide), jnp.float32),
        ],
        compiler_params=params(),
        name="quadratic",
    )(held, parts_sum, lens, weights)


def lane_facts(slot_count):
    lane = lax.broadcasted_iota(jnp.int32, (SUBLANES, LANES), 1)
    return (lane % (4 * slot_count) // 4, lane % 4 // 2, lane // (4 * slot_count), lane % 2)


def tile_of_row(block, span, slot_count):
    at = lax.broadcasted_iota(jnp.int32, (SUBLANES, LANES), 0) + block * SUBLANES
    at = at - lane_facts(slot_count)[2] * span % SUBLANES
    return at // 2, jnp.logical_and(at >= 0, at < span)


def prepare(cycle_len, gauss_w, wave_map, spec, panel, signs, span, step, waves, groups, wide):
    slot_count = wave_map.shape[0]
    slots, parts, degrees_all = spec.shape
    own = panel.shape[0] // slots
    levels = degrees_all // own
    rows = 2 * slots * parts
    here = cycle_len.shape[0] // waves
    tiles = wide // LANES
    per = SUBLANES // 2

    def kernel(
        len_ref, map_ref, len_row_ref, weight_row_ref, x_ref, panel_ref, sign_ref,
        first_ref, factor_ref, factors_ref, near_ref, o_ref, lens_ref, weights_ref, held_ref, sem,
    ):
        copy = pltpu.make_async_copy(panel_ref, near_ref, sem)
        copy.start()
        row_of = lax.broadcasted_iota(jnp.int32, (rows, degrees_all), 0)
        degree = lax.broadcasted_iota(jnp.int32, (rows, degrees_all), 1)
        bound = jnp.zeros((rows, degrees_all), jnp.int32)
        for s in range(slots):
            mine = row_of // parts % slots == s
            bound = jnp.where(mine, map_ref[at_wave() * slots + s] * step, bound)
        turned = jnp.logical_and(row_of >= rows // 2, (bound & 1) == 1)
        sign = sign_ref[...]
        factor = jnp.where(degree >= bound, jnp.where(turned, -sign, sign), 0.0)
        factor_ref[...] = factor
        x = [x_ref[s].astype(jnp.float32) for s in range(slots)]
        first_ref[...] = jnp.concatenate(x + x, axis=0) * factor
        for level in range(levels):

            @pl.when(at_level() == level)
            def _(level=level):
                for e in range(2):
                    start = (level ^ e) * own
                    factors_ref[e] = factor[:, start : start + own]

        for i in range(slot_count):
            for w in range(slot_count):
                held = jnp.where(map_ref[i] == w, 1.0, 0.0)
                held_ref[w, i : i + 1, :] = jnp.full((1, LANES), held, jnp.float32)

        lens_ref[...] = jnp.full((SUBLANES, LANES), 4.0, jnp.float32)
        weights_ref[...] = jnp.zeros((SUBLANES, LANES), jnp.float32)
        for v in range(waves):

            @pl.when(at_wave() == v)
            def _(v=v):
                for t in range(tiles):
                    size = min(LANES, here - t * LANES)
                    at = v * here + t * LANES
                    lens = len_row_ref[at : at + size].astype(jnp.float32).reshape(1, size)
                    weights = weight_row_ref[at : at + size].reshape(1, size)
                    for h in range(2):
                        k = h * (SUBLANES // 2) + t
                        lens_ref[k : k + 1, 0:size] = lens
                        weights_ref[k : k + 1, 0:size] = weights

        wave, part, row, cycle = lane_facts(slot_count)
        tile, _ = tile_of_row(0, span, slot_count)
        first = (tile * LANES).astype(jnp.float32)
        order = (step * wave).astype(jnp.float32)
        stride = order * (LANES * SUBLANES / 2.0)
        imag = part == 1
        way = (1 - 2 * cycle).astype(jnp.float32)
        down = lax.broadcasted_iota(jnp.int32, (SUBLANES, LANES), 0)
        turn = step * lax.broadcasted_iota(jnp.int32, (SUBLANES, LANES), 1).astype(jnp.float32)
        mine = [row == i // 2 if i % 2 == 0 else jnp.logical_and(row == i // 2, cycle == 1) for i in range(SUBLANES)]
        second = down % 2 == 1
        start = at_wave() * here

        def body(g, carry):
            lens = [
                len_ref[start + jnp.minimum(g * SUBLANES + i, here - 1)] for i in range(SUBLANES)
            ]
            length = jnp.full((SUBLANES, LANES), lens[0], jnp.int32)
            length_down, before, before_down = length, length, length
            for i in range(1, SUBLANES):
                length = jnp.where(mine[i], lens[i], length)
                length_down = jnp.where(down == i, lens[i], length_down)
            for r in range(1, per):
                before = jnp.where(row == r, lens[2 * r], before)
                before_down = jnp.where(down // 2 == r, lens[2 * r], before_down)
            length = length.astype(jnp.float32)
            offset = jnp.where(cycle == 1, before, 0).astype(jnp.float32)
            split = (before >> (LANES.bit_length() - 1)).astype(jnp.float32)
            marks = jnp.where(second, before_down + length_down, before_down & (LANES - 1))
            length_down = length_down.astype(jnp.float32)
            inverse = 1.0 / length
            cos, sin = circle(order * (first - offset), length, inverse)
            o_ref[g, 0] = jnp.where(imag, sin, cos)
            o_ref[g, 1] = jnp.where(imag, cos, -sin)
            cos, sin = circle(stride, length, inverse)
            turns = jnp.where(down == 0, cos, sin)
            o_ref[g, 2] = jnp.where(down < 2, turns, way * split)
            cos, sin = circle(turn, length_down, 1.0 / length_down)
            o_ref[g, 3] = cos
            o_ref[g, 4] = -sin
            o_ref[g, 5] = 1.0 - 2.0 * sin * sin
            o_ref[g, 6] = -2.0 * sin * cos
            o_ref[g, 7] = marks.astype(jnp.float32)
            return carry

        lax.fori_loop(0, groups, body, 0, unroll=19)
        copy.wait()

    flat = jax.ShapeDtypeStruct((SUBLANES, LANES), jnp.float32)
    return pl.pallas_call(
        kernel,
        out_shape=(
            jax.ShapeDtypeStruct((rows, degrees_all), jnp.float32),
            jax.ShapeDtypeStruct((rows, degrees_all), jnp.float32),
            jax.ShapeDtypeStruct((2, rows, own), jnp.float32),
            jax.ShapeDtypeStruct(panel.shape, panel.dtype),
            jax.ShapeDtypeStruct((groups, 8, SUBLANES, LANES), jnp.float32),
            flat,
            flat,
            jax.ShapeDtypeStruct((slot_count, slot_count, LANES), jnp.float32),
        ),
        in_specs=[smem()] * 2 + [vmem()] * 3 + [pl.BlockSpec(memory_space=pl.ANY), vmem()],
        out_specs=(vmem(),) * 8,
        scratch_shapes=[pltpu.SemaphoreType.DMA],
        compiler_params=params(),
        cost_estimate=cost(3 * 10**9, 10**6),
        name="prepare",
    )(cycle_len, wave_map, cycle_len, gauss_w, spec, panel, signs)


def grid_values(fourier, tables, span, slot_count, rows_out, tiles):
    groups = tables.shape[0]
    per = SUBLANES // 2
    block = groups // STEPS
    blocks = -(-(span + SUBLANES // 2) // SUBLANES)
    size = 4 * slot_count
    kinds = 4 * slot_count
    around = LANES // SUBLANES

    total = rows_out * span
    tail = total % (2 * SUBLANES)
    tail_group, tail_at = divmod(total - tail, per * span)

    def kernel(fourier_ref, table_ref, o_hbm, rows_ref, wave_ref, part_ref, tail_ref, sems):
        wave, _, row, cycle = lane_facts(slot_count)
        way = (1 - 2 * cycle).astype(jnp.float32)
        point = lax.broadcasted_iota(jnp.int32, (SUBLANES, LANES), 1).astype(jnp.float32)
        down = lax.broadcasted_iota(jnp.int32, (SUBLANES, LANES), 0)
        second = down % 2 == 1
        unit = jnp.where(down < 2, 1.0, 0.0)
        beside = jnp.where(down < 6, -1.0, 1.0)
        for c in range(2):
            for h in range(2):
                for t in range(tiles):
                    at = (c * 2 + h) * slot_count
                    k = c * SUBLANES + h * (SUBLANES // 2) + t
                    rows_ref[t, at : at + slot_count, :] = fourier_ref[
                        pl.ds(k, slot_count, stride=2 * SUBLANES), :
                    ]
        pick = lax.broadcasted_iota(jnp.int32, (LANES, LANES), 0)
        lane = lax.broadcasted_iota(jnp.int32, (LANES, LANES), 1)
        pick = jnp.where(pick == lane // size * 2 + lane % 2, 1.0, 0.0).astype(jnp.bfloat16)

        turned = []
        for g in range(groups):
            shift = -g % around * SUBLANES
            value = rows_ref[g // around]
            turned.append(pltpu.roll(value, shift, 1) if shift else value)
        spread = jnp.dot(
            jnp.concatenate(turned, axis=0).astype(jnp.bfloat16), pick, preferred_element_type=jnp.float32
        )
        for g in range(groups):
            sums = []
            for k in range(4):
                at = g * kinds + k * slot_count
                value = jnp.where(down == wave, spread[at : at + SUBLANES], 0.0)
                sums.append(jnp.sum(value, axis=0, keepdims=True))
            for c in range(2):
                wave_ref[g, c] = jnp.where(down % 2 == 0, sums[2 * c], sums[2 * c + 1])

        def one_group(base, i, g):
            real, imag = wave_ref[g, 0], wave_ref[g, 1]
            x = real * table_ref[g, 0] + imag * table_ref[g, 1]
            y = real * table_ref[g, 1] - imag * table_ref[g, 0]
            turn_cos, turn_sin = table_ref[g, 2, 0:1], table_ref[g, 2, 1:2]
            split = table_ref[g, 2, 2:3]
            main, mixed = [], []
            for k in range(blocks):
                if k:
                    x, y = x * turn_cos + y * turn_sin, y * turn_cos - x * turn_sin
                tile, inside = tile_of_row(k, span, slot_count)
                apart = tile.astype(jnp.float32) * way - split
                value = jnp.where(inside, x, 0.0) if k in (0, blocks - 1) else x
                main.append(jnp.where(apart < 0.0, value, 0.0))
                mixed.append(jnp.where(apart == 0.0, value, 0.0))
            main, mixed = jnp.concatenate(main, axis=0), jnp.concatenate(mixed, axis=0)
            left = jnp.concatenate([main, mixed], axis=1).astype(jnp.bfloat16)

            columns, ends = [], []
            for r in range(per):
                ends.append(table_ref[g, 7, 2 * r + 1 : 2 * r + 2])
                cos1, sin1, cos2, sin2 = [
                    jnp.where(
                        second,
                        table_ref[g, i, 2 * r + 1 : 2 * r + 2],
                        table_ref[g, i, 2 * r : 2 * r + 1],
                    )
                    for i in range(3, 7)
                ]
                twice = 2.0 * cos2
                series = [jnp.where(down < 4, unit, jnp.where(down < 6, cos1, sin1))]
                third = series[0] * (twice + beside)
                series.append(jnp.where(down < 2, cos2, jnp.where(down < 4, sin2, third)))
                here = jnp.logical_xor(point < table_ref[g, 7, 2 * r : 2 * r + 1], second)
                for _ in range(2, size // SUBLANES):
                    series.append(twice * series[-1] - series[-2])
                full = jnp.concatenate(series, axis=0).astype(jnp.bfloat16)
                part = jnp.concatenate([jnp.where(here, v, 0.0) for v in series], axis=0).astype(jnp.bfloat16)
                before = [jnp.zeros((r * size, LANES), jnp.bfloat16)] if r else []
                after = [jnp.zeros((LANES - (r + 1) * size, LANES), jnp.bfloat16)] if r < per - 1 else []
                columns.append(jnp.concatenate(before + [full] + after + before + [part] + after, axis=0))
            right = jnp.concatenate(columns, axis=1)
            product = jnp.dot(left, right, preferred_element_type=jnp.float32)
            places = {}
            for r in range(per):
                shift = r * span % SUBLANES
                for k in range(blocks):
                    if k * SUBLANES >= shift + span:
                        continue
                    value = product[k * SUBLANES : (k + 1) * SUBLANES, r * LANES : (r + 1) * LANES]
                    if k == blocks - 1:
                        position = ((down + k * SUBLANES - shift) // 2 * LANES).astype(jnp.float32) + point
                        value = jnp.where(position < ends[r], value, 0.0)
                    places.setdefault((r * span - shift) // SUBLANES + k, []).append(value)
            whole = [functools.reduce(lambda a, b: a + b, places[k]) for k in sorted(places)]
            size_out = per * span
            part_ref[base, i * size_out : (i + 1) * size_out, :] = jnp.concatenate(
                whole, axis=0
            ).astype(jnp.bfloat16)
            if tail and i == tail_group % block:
                tail_ref[...] = whole[tail_at // SUBLANES].astype(jnp.bfloat16)

        size_out = per * span
        cuts = [piece * block // PIECES for piece in range(PIECES + 1)]

        def copy(i, piece):
            start, end = cuts[piece] * size_out, cuts[piece + 1] * size_out
            place = i * block * size_out
            size = min(end, total - tail - place) - start
            return pltpu.make_async_copy(
                part_ref.at[i, pl.ds(start, size), :],
                o_hbm.at[pl.ds(place + start, size), :],
                sems.at[PIECES * i + piece],
            )

        def step(base, carry):
            for piece in range(PIECES):
                for i in range(cuts[piece], cuts[piece + 1]):
                    one_group(base, i, base * block + i)
                for i in range(STEPS):

                    @pl.when(base == i)
                    def _(i=i, piece=piece):
                        copy(i, piece).start()

            return carry

        lax.fori_loop(0, STEPS, step, 0)
        if tail:
            rest = pltpu.make_async_copy(
                tail_ref, o_hbm.at[pl.ds(total - tail, tail), :], sems.at[PIECES * STEPS]
            )
            rest.start()
        for i in range(STEPS):
            for piece in range(PIECES):
                copy(i, piece).wait()
        if tail:
            rest.wait()

    return pl.pallas_call(
        kernel,
        out_shape=jax.ShapeDtypeStruct((rows_out * span, LANES), jnp.bfloat16),
        in_specs=[vmem()] * 2,
        out_specs=pl.BlockSpec(memory_space=pl.ANY),
        scratch_shapes=[
            pltpu.VMEM((tiles, kinds, LANES), jnp.float32),
            pltpu.VMEM((groups, 2, SUBLANES, LANES), jnp.float32),
            pltpu.VMEM((STEPS, block * per * span, LANES), jnp.bfloat16),
            pltpu.VMEM((SUBLANES, LANES), jnp.bfloat16),
            pltpu.SemaphoreType.DMA((PIECES * STEPS + 1,)),
        ],
        compiler_params=params(16 * 1024 * 1024),
        cost_estimate=cost(8 * 10**9, 3 * 10**6),
        name="grid_values",
    )(fourier, tables)


def direct(returned, factors, panels):
    waves, tall, _ = returned.shape
    depth, lats = panels[0].shape
    own, here = factors.shape[2], lats // waves
    slots, half = depth // own, factors.shape[1] // 2
    chips = tall // (2 * half)

    def kernel(x_ref, factor_ref, own_ref, other_ref, *refs):
        o_refs, left_ref, all_ref = refs[:chips], refs[chips], refs[chips + 1]
        for place, j in enumerate(from_middle(waves)):
            left_ref[:, j * here : (j + 1) * here] = x_ref[place, :, 0:here].astype(jnp.float32)
        left = left_ref[...].astype(jnp.bfloat16)
        shape = (chips, half, own)
        slot_of = lax.broadcasted_iota(jnp.int32, shape, 1) // 2
        for e, panel_ref in enumerate((own_ref, other_ref)):
            total = lax.dot_general(
                left, panel_ref[...], (((1,), (1,)), ((), ())), preferred_element_type=jnp.float32
            ).reshape(chips, 2 * half, depth)
            result = jnp.zeros(shape, jnp.float32)
            for s in range(slots):
                mine = total[:, :, s * own : (s + 1) * own] * factor_ref[e][None]
                result = jnp.where(slot_of == s, mine[:, :half] + mine[:, half:], result)
            all_ref[:, e * half : (e + 1) * half, :] = result
        for i in range(chips):
            o_refs[i][...] = all_ref[(at_level() // 2) ^ i]

    return pl.pallas_call(
        kernel,
        out_shape=(jax.ShapeDtypeStruct((2 * half, own), jnp.float32),) * chips,
        in_specs=[vmem()] * 4,
        out_specs=(vmem(),) * chips,
        scratch_shapes=[
            pltpu.VMEM((tall, lats), jnp.float32),
            pltpu.VMEM((chips, 2 * half, own), jnp.float32),
        ],
        compiler_params=params(),
        cost_estimate=cost(10**9, 2 * 10**6),
        name="direct",
    )(returned, factors, *panels)


def join_degrees(pieces, slots):
    chips = len(pieces)
    rows, own = pieces[0].shape
    half = rows // 2

    def kernel(*refs):
        piece_refs, o_ref, all_ref = refs[:chips], refs[chips], refs[chips + 1]
        for i in range(chips):
            for e in range(2):
                all_ref[at_level() ^ (2 * i + e)] = piece_refs[i][e * half : (e + 1) * half, :]
        whole = jnp.concatenate([all_ref[v] for v in range(2 * chips)], axis=1)
        for s in range(slots):
            o_ref[s] = whole[2 * s : 2 * s + 2]

    return pl.pallas_call(
        kernel,
        out_shape=jax.ShapeDtypeStruct((slots, 2, 2 * chips * own), jnp.float32),
        in_specs=[vmem()] * chips,
        out_specs=vmem(),
        scratch_shapes=[pltpu.VMEM((2 * chips, half, own), jnp.float32)],
        compiler_params=params(),
        name="join_degrees",
    )(*pieces)


def evenly_spaced(levels, spec, legendre, gauss_w, cycle_len, wave_map):
    slots = spec.shape[0]
    degrees_all = spec.shape[3]
    own = legendre.shape[1]
    lats = legendre.shape[2]
    slot_count = wave_map.shape[0]
    step = degrees_all // slot_count
    waves = slot_count // slots
    chips = levels // 2

    def across(x, bits):
        return lax.ppermute(x, "lev", [(j, j ^ bits) for j in range(levels)])

    def same_core(x):
        groups = [
            [wave * levels + 2 * chip + core for wave in from_middle(waves) for chip in range(chips)]
            for core in range(2)
        ]
        return lax.all_to_all(x, ("wave", "lev"), 0, 0, tiled=True, axis_index_groups=groups)

    mine = spec.reshape(slots, 2, degrees_all)
    others = [across(mine, 2 * i) for i in range(1, chips)]
    panel = legendre.reshape(slots * own, lats)
    signs = parity_signs(2 * slots * 2, degrees_all)
    here = lats // waves
    wide = -(-here // LANES) * LANES
    tiles = wide // LANES
    per = SUBLANES // 2
    rows_out = here // 2
    groups = -(-rows_out // (per * STEPS)) * STEPS
    span = 2 * (LPAD // LANES)
    rows_here = 2 * slots * 2
    first, factor, factors, near, tables, lens, weights, held = prepare(
        cycle_len, gauss_w, wave_map, mine, panel, signs, span, step, waves, groups, wide
    )
    panels = (near, across(panel, 1))

    part = partial_fourier(first, factor, others, panels, slots, waves, wide)
    part = same_core(part.reshape(waves * chips, rows_here, wide))
    fourier, returned = quadratic(held, part, lens, weights, waves, step)
    returned = same_core(returned)

    values = grid_values(fourier, tables, span, slot_count, rows_out, tiles)
    values = values.reshape(rows_out, span // 2, 2, LANES)
    values = with_layout_constraint(values, Layout(major_to_minor=(0, 1, 2, 3)))
    values = values.transpose(0, 2, 1, 3)
    values = with_layout_constraint(values, Layout(major_to_minor=(0, 2, 1, 3)))
    values = values.reshape(rows_out, 2, LPAD)
    values = with_layout_constraint(values, Layout(major_to_minor=(0, 1, 2)))
    grid = values.transpose(1, 0, 2).reshape(2, rows_out, 1, LPAD)

    returned = returned.reshape(waves, chips * rows_here, wide)
    pieces = direct(returned, factors, (panel, panels[1]))
    pieces = [pieces[0]] + [across(pieces[i], 2 * i) for i in range(1, chips)]
    spec_out = join_degrees(pieces, slots).reshape(slots, 1, 2, degrees_all)
    return (grid, spec_out)


def per_device(levels, spec, legendre, gauss_w, cycle_len, wave_map):
    slot_count = wave_map.shape[0]
    fits = (
        spec.shape[3] % slot_count == 0
        and 2 * slot_count * SUBLANES == LANES
        and spec.shape[1] == 1
        and 4 * spec.shape[0] == SUBLANES
        and levels > 1
        and levels & (levels - 1) == 0
    )
    if fits:
        return evenly_spaced(levels, spec, legendre, gauss_w, cycle_len, wave_map)
    return general(spec, legendre, gauss_w, cycle_len, wave_map)


def solution(mesh):
    placed = (P("wave", "lev", None, None), P("wave", "lev", None), P(), P(), P())
    return jax.shard_map(
        functools.partial(per_device, mesh.shape["lev"]),
        mesh=mesh,
        in_specs=placed,
        out_specs=(P(None, "wave", "lev", None), P("wave", "lev", None, None)),
        check_vma=False,
    )
```

```python
import functools
import math

import jax
import jax.numpy as jnp
from jax import lax
from jax.experimental import pallas as pl
from jax.experimental.layout import Layout, with_layout_constraint
from jax.experimental.pallas import tpu as pltpu
from jax.sharding import PartitionSpec as P

LPAD = 4864


def block_rows():
    for candidate in (10, 8, 6, 5, 4, 3, 2):
        return candidate
    return 1


def cycle_tables(lens_pair, orders, padded):
    position = jnp.arange(padded, dtype=jnp.int32)[None, :]
    first_len = lens_pair[:, 0:1]
    second = lens_pair[:, 1:2]
    upper_half = position >= first_len
    occupied = position < first_len + second
    offset = jnp.where(upper_half, position - first_len, position)
    length = jnp.where(upper_half, second, first_len)
    turn_count = orders[None, :, None] * offset[:, None, :] % length[:, None, :]
    angles = 2.0 * math.pi * turn_count.astype(jnp.float32) / length[:, None, :].astype(jnp.float32)
    cosine = jnp.where(occupied[:, None, :], jnp.cos(angles), 0.0).astype(jnp.bfloat16)
    minus_sine = jnp.where(occupied[:, None, :], -jnp.sin(angles), 0.0).astype(jnp.bfloat16)
    return (jnp.concatenate([cosine, minus_sine], 1), upper_half, occupied)


def cycle_block(waves, lens_pair, weights, orders, padded):
    row_count = waves.shape[0]
    fields = waves.shape[3]
    slot_count = orders.shape[0]
    tables, upper_half, occupied = cycle_tables(lens_pair, orders, padded)
    double = jnp.where(orders == 0, 1.0, 2.0)
    resolved = 2 * orders[None, None, :] < lens_pair[:, :, None]
    widening = jnp.where(resolved, double[None, None, :], 0.0)
    scaled = (waves.astype(jnp.float32) * widening[:, None, :, None, None, :]).astype(jnp.bfloat16)
    scaled = scaled.reshape(row_count, 4 * fields, 2 * slot_count)
    images = jnp.einsum("rak,rkp->rap", scaled, tables, preferred_element_type=jnp.float32)
    images = images.reshape(row_count, 2, 2, fields, padded)
    values = jnp.where(upper_half[:, None, None, :], images[:, :, 1], images[:, :, 0])
    values = jnp.where(occupied[:, None, None, :], values, 0.0).astype(jnp.bfloat16)
    squared = (values.astype(jnp.float32) * values.astype(jnp.float32)).astype(jnp.bfloat16)
    selector = jnp.stack([jnp.logical_not(upper_half), upper_half], 1)
    by_cycle = jnp.where(
        selector[:, None, :, None, :], squared[:, :, None, :, :], jnp.zeros((), jnp.bfloat16)
    )
    by_cycle = by_cycle.reshape(row_count, 4 * fields, padded)
    returned = jnp.einsum("rap,rkp->rak", by_cycle, tables, preferred_element_type=jnp.float32)
    returned = returned.reshape(row_count, 2, 2, fields, 2, slot_count)
    factor = jnp.where(
        resolved, weights[:, :, None] / lens_pair[:, :, None].astype(jnp.float32), 0.0
    )
    returned = (returned * factor[:, None, :, None, None, :]).astype(jnp.bfloat16)
    return (values, returned)


def parity_of(degree_ids, own_orders):
    return jnp.where((degree_ids[None, :] + own_orders[:, None]) % 2 == 0, 1.0, -1.0)


def general(spec, legendre, gauss_w, cycle_len, wave_map):
    slots_dev = spec.shape[0]
    fields = spec.shape[1]
    degrees_all = spec.shape[3]
    slot_count = wave_map.shape[0]
    orders = wave_map * degrees_all // slot_count
    wave_pos = lax.axis_index("wave")
    own_orders = lax.dynamic_slice_in_dim(orders, wave_pos * slots_dev, slots_dev)
    degrees = jnp.arange(degrees_all, dtype=jnp.int32)
    retained = degrees[None, :] >= own_orders[:, None]
    coefficients = jnp.where(retained[:, None, None, :], spec, jnp.zeros((), jnp.bfloat16))
    panels = lax.all_gather(legendre, "lev", axis=1, tiled=True)
    sign_flip = parity_of(degrees, own_orders)
    flipped = (coefficients.astype(jnp.float32) * sign_flip[:, None, None, :]).astype(jnp.bfloat16)
    stacked = jnp.stack([coefficients, flipped], 1)
    fourier = jnp.einsum(
        "shfcn,snq->shfcq", stacked, panels, preferred_element_type=jnp.float32
    ).astype(jnp.bfloat16)
    cycle_waves = lax.all_to_all(fourier, "wave", split_axis=4, concat_axis=0, tiled=True)
    local_lats = cycle_waves.shape[4]
    row_total = local_lats // 2
    lat_start = wave_pos * local_lats
    lens_here = lax.dynamic_slice_in_dim(cycle_len, lat_start, local_lats)
    weights_here = lax.dynamic_slice_in_dim(gauss_w, lat_start, local_lats)
    row_block = block_rows()
    blocks = row_total // row_block
    ordered = cycle_waves.reshape(slot_count, 2, fields, 2, row_total, 2).transpose(
        4, 1, 5, 2, 3, 0
    )
    ordered = ordered.reshape(blocks, row_block, 2, 2, fields, 2, slot_count)

    def run_block(operands):
        return cycle_block(operands[0], operands[1], operands[2], orders, LPAD)

    values, returned = lax.map(
        run_block,
        (
            ordered,
            lens_here.reshape(blocks, row_block, 2),
            weights_here.reshape(blocks, row_block, 2),
        ),
    )
    grid = values.reshape(row_total, 2, fields, LPAD).transpose(1, 0, 2, 3)
    returned = returned.reshape(row_total, 2, 2, fields, 2, slot_count).transpose(5, 1, 3, 4, 0, 2)
    returned = returned.reshape(slot_count, 2, fields, 2, local_lats)
    spectral = lax.all_to_all(returned, "wave", split_axis=0, concat_axis=4, tiled=True)
    both = jnp.einsum("shfcq,snq->shfcn", spectral, panels, preferred_element_type=jnp.float32)
    total = both[:, 0] + sign_flip[:, None, None, :] * both[:, 1]
    spec_out = jnp.where(retained[:, None, None, :], total, 0.0)
    return (grid, spec_out)


LANES = 128
SUBLANES = 8
STEPS = 2
PIECES = 4
VMEM = 8 * 1024 * 1024
SINE = (6.28318516, -41.34165503, 81.60100407, -76.54978222, 39.53670553)


def circle(x, period, inverse):
    turn = (x - period * jnp.floor(x * inverse + 0.5)) * inverse
    away = jnp.abs(turn)
    values = []
    for v in (0.25 - away, 0.25 - jnp.abs(away - 0.25)):
        y = v * v
        series = SINE[4]
        for coefficient in SINE[3::-1]:
            series = series * y + coefficient
        values.append(v * series)
    return values[0], jnp.where(turn < 0.0, -values[1], values[1])


def params(memory=VMEM):
    return pltpu.CompilerParams(vmem_limit_bytes=memory)


def cost(flops, nbytes):
    return pl.CostEstimate(flops=flops, bytes_accessed=nbytes, transcendentals=0)


def at_wave():
    return lax.axis_index("wave")


def at_level():
    return lax.axis_index("lev")


def from_middle(count):
    return sorted(range(count), key=lambda i: (abs(2 * i - count + 1), -i))


def turned(chips):
    return chips // 2


def smem():
    return pl.BlockSpec(memory_space=pltpu.SMEM)


def vmem():
    return pl.BlockSpec(memory_space=pltpu.VMEM)


def parity_signs(rows, degrees_all):
    def kernel(o_ref):
        row = lax.broadcasted_iota(jnp.int32, (rows, degrees_all), 0)
        degree = lax.broadcasted_iota(jnp.int32, (rows, degrees_all), 1)
        odd = jnp.logical_and(row >= rows // 2, (degree & 1) == 1)
        o_ref[...] = jnp.where(odd, -1.0, 1.0)

    return pl.pallas_call(
        kernel,
        out_shape=jax.ShapeDtypeStruct((rows, degrees_all), jnp.float32),
        out_specs=vmem(),
        compiler_params=params(),
        cost_estimate=cost(4 * 10**9, 10**6),
        name="parity_signs",
    )()


def partial_fourier(first, factor, others, panels, slots, waves, wide):
    chips = len(others) + 1
    rows, degrees_all = first.shape
    parts = rows // (2 * slots)
    depth, lats = panels[0].shape
    own, here = depth // slots, lats // waves

    def kernel(first_ref, factor_ref, *refs):
        spec_refs, panel_refs = refs[: chips - 1], refs[chips - 1 : chips + 1]
        o_ref, left_ref = refs[chips + 1 :]
        factor = factor_ref[...]
        whole = [first_ref[...]]
        for ref in spec_refs:
            x = [ref[s].astype(jnp.float32) for s in range(slots)]
            whole.append(jnp.concatenate(x + x, axis=0) * factor)
        whole = jnp.concatenate(whole, axis=0)
        slot_of = lax.broadcasted_iota(jnp.int32, (chips * rows, own), 0) // parts % slots
        for level in range(2 * chips):

            @pl.when(at_level() == level)
            def _(level=level):
                for e in range(2):
                    start = (level ^ e) * own
                    piece = whole[:, start : start + own]
                    left = [jnp.where(slot_of == s, piece, 0.0) for s in range(slots)]
                    left_ref[e] = jnp.concatenate(left, axis=1).astype(jnp.bfloat16)

        total = jnp.dot(left_ref[0], panel_refs[0][...], preferred_element_type=jnp.float32)
        total += jnp.dot(left_ref[1], panel_refs[1][...], preferred_element_type=jnp.float32)
        chip = at_level() // 2
        places = [from_middle(waves).index(j) for j in range(waves)]
        fill = jnp.zeros((rows, wide - here), jnp.float32)
        for i in range(chips):
            mine = total[i * rows : (i + 1) * rows]
            for j in range(waves):
                value = mine[:, j * here : (j + 1) * here]
                value = jnp.concatenate([value, fill], axis=1)
                o_ref[places[j], chip ^ i ^ turned(chips)] = value.astype(jnp.bfloat16)

    return pl.pallas_call(
        kernel,
        out_shape=jax.ShapeDtypeStruct((waves, chips, rows, wide), jnp.bfloat16),
        in_specs=[vmem()] * (chips + 3),
        out_specs=vmem(),
        scratch_shapes=[pltpu.VMEM((2, chips * rows, depth), jnp.bfloat16)],
        compiler_params=params(),
        cost_estimate=cost(10**9, 2 * 10**6),
        name="partial_fourier",
    )(first, factor, *others, *panels)


def quadratic(held, parts_sum, lens, weights, waves, step):
    sources, rows, wide = parts_sum.shape
    slot_count = held.shape[0]
    levels = sources // waves
    slots = slot_count // waves
    tiles = wide // LANES
    top = 2 * (slot_count - 1)
    shape = (SUBLANES, LANES)

    def kernel(held_ref, x_ref, len_ref, weight_ref, g_ref, o_ref, z_ref, r_ref, s_ref):
        half = rows // 2
        z_ref[...] = jnp.zeros(z_ref.shape, jnp.float32)
        for place, i in enumerate(from_middle(waves)):
            total = x_ref[place * levels].astype(jnp.float32)
            for j in range(1, levels):
                total = total + x_ref[place * levels + j].astype(jnp.float32)
            total = total.astype(jnp.bfloat16).astype(jnp.float32)
            for h in range(2):
                for t in range(tiles):
                    at = i * half * SUBLANES + h * (SUBLANES // 2) + t
                    z_ref[pl.ds(at, half, stride=SUBLANES), :] = total[
                        h * half : (h + 1) * half, t * LANES : (t + 1) * LANES
                    ]
        lens_here = len_ref[...]
        kept = [
            jnp.where(lens_here > 2.0 * step * w, 1.0, 0.0) for w in range(slot_count)
        ]
        held = [
            [held_ref[w, i : i + 1, :] > 0.5 for i in range(slot_count)] for w in range(slot_count)
        ]
        real, imag = [], []
        for w in range(slot_count):
            re, im = jnp.zeros(shape, jnp.float32), jnp.zeros(shape, jnp.float32)
            for i in range(slot_count):
                at = i * 2 * SUBLANES
                re = jnp.where(held[w][i], z_ref[at : at + SUBLANES, :], re)
                im = jnp.where(held[w][i], z_ref[at + SUBLANES : at + 2 * SUBLANES, :], im)
            real.append(re * kept[w])
            imag.append(im * kept[w])
        for w in range(slot_count):
            double = 1.0 if w == 0 else 2.0
            at = 2 * w * SUBLANES
            g_ref[at : at + SUBLANES, :] = real[w] * double
            g_ref[at + SUBLANES : at + 2 * SUBLANES, :] = imag[w] * double
        imag[0] = jnp.zeros(shape, jnp.float32)
        square_real, square_imag = [], []
        for n in range(top + 1):
            re, im = jnp.zeros(shape, jnp.float32), jnp.zeros(shape, jnp.float32)
            for a in range(max(0, n - slot_count + 1), (n + 1) // 2):
                b = n - a
                re = re + (real[a] * real[b] - imag[a] * imag[b])
                im = im + (real[a] * imag[b] + imag[a] * real[b])
            for b in range(1, slot_count - n):
                a = n + b
                re = re + (real[a] * real[b] + imag[a] * imag[b])
                im = im + (imag[a] * real[b] - real[a] * imag[b])
            re, im = 2.0 * re, 2.0 * im
            if n % 2 == 0:
                a = n // 2
                re = re + (real[a] * real[a] - imag[a] * imag[a])
                im = im + 2.0 * (real[a] * imag[a])
            square_real.append(re)
            square_imag.append(im)
        whole = {
            d: jnp.where(lens_here == 1.0 * step * d, 1.0, 0.0)
            for d in range(3, top + slot_count)
        }
        weights_here = weight_ref[...]
        result = []
        for w in range(slot_count):
            re, im = square_real[w], square_imag[w]
            if w == 0:
                im = jnp.zeros(shape, jnp.float32)
            else:
                for n in range(w + 1, top + 1):
                    re = re + whole[w + n] * square_real[n]
                    im = im - whole[w + n] * square_imag[n]
            factor = kept[w] * weights_here
            result.append((re * factor, im * factor))
        for i in range(slot_count):
            re, im = result[0]
            for w in range(1, slot_count):
                re = jnp.where(held[w][i], result[w][0], re)
                im = jnp.where(held[w][i], result[w][1], im)
            at = i * 2 * SUBLANES
            r_ref[at : at + SUBLANES, :] = re
            r_ref[at + SUBLANES : at + 2 * SUBLANES, :] = im
        for place, i in enumerate(from_middle(waves)):
            for h in range(2):
                for t in range(tiles):
                    start = i * half * SUBLANES + h * (SUBLANES // 2) + t
                    s_ref[h * half : (h + 1) * half, t * LANES : (t + 1) * LANES] = r_ref[
                        pl.ds(start, half, stride=SUBLANES), :
                    ]
            packed = s_ref[...].astype(jnp.bfloat16)
            for j in range(levels):
                o_ref[place * levels + j] = packed

    return pl.pallas_call(
        kernel,
        out_shape=(
            jax.ShapeDtypeStruct((2 * slot_count * SUBLANES, LANES), jnp.float32),
            jax.ShapeDtypeStruct((sources, rows, wide), jnp.bfloat16),
        ),
        in_specs=[vmem()] * 4,
        out_specs=(vmem(), vmem()),
        scratch_shapes=[
            pltpu.VMEM((2 * slot_count * SUBLANES, LANES), jnp.float32),
            pltpu.VMEM((2 * slot_count * SUBLANES, LANES), jnp.float32),
            pltpu.VMEM((rows, wide), jnp.float32),
        ],
        compiler_params=params(),
        name="quadratic",
    )(held, parts_sum, lens, weights)


def lane_facts(slot_count):
    lane = lax.broadcasted_iota(jnp.int32, (SUBLANES, LANES), 1)
    return (lane % (4 * slot_count) // 4, lane % 4 // 2, lane // (4 * slot_count), lane % 2)


def tile_of_row(block, span, slot_count):
    at = lax.broadcasted_iota(jnp.int32, (SUBLANES, LANES), 0) + block * SUBLANES
    at = at - lane_facts(slot_count)[2] * span % SUBLANES
    return at // 2, jnp.logical_and(at >= 0, at < span)


def prepare(cycle_len, gauss_w, wave_map, spec, panel, signs, span, step, waves, groups, wide):
    slot_count = wave_map.shape[0]
    slots, parts, degrees_all = spec.shape
    own = panel.shape[0] // slots
    levels = degrees_all // own
    rows = 2 * slots * parts
    here = cycle_len.shape[0] // waves
    tiles = wide // LANES
    per = SUBLANES // 2

    def kernel(
        len_ref, map_ref, len_row_ref, weight_row_ref, x_ref, panel_ref, sign_ref,
        first_ref, factor_ref, factors_ref, near_ref, o_ref, lens_ref, weights_ref, held_ref, sem,
    ):
        copy = pltpu.make_async_copy(panel_ref, near_ref, sem)
        copy.start()
        row_of = lax.broadcasted_iota(jnp.int32, (rows, degrees_all), 0)
        degree = lax.broadcasted_iota(jnp.int32, (rows, degrees_all), 1)
        bound = jnp.zeros((rows, degrees_all), jnp.int32)
        for s in range(slots):
            mine = row_of // parts % slots == s
            bound = jnp.where(mine, map_ref[at_wave() * slots + s] * step, bound)
        turned = jnp.logical_and(row_of >= rows // 2, (bound & 1) == 1)
        sign = sign_ref[...]
        factor = jnp.where(degree >= bound, jnp.where(turned, -sign, sign), 0.0)
        factor_ref[...] = factor
        x = [x_ref[s].astype(jnp.float32) for s in range(slots)]
        first_ref[...] = jnp.concatenate(x + x, axis=0) * factor
        for level in range(levels):

            @pl.when(at_level() == level)
            def _(level=level):
                for e in range(2):
                    start = (level ^ e) * own
                    factors_ref[e] = factor[:, start : start + own]

        for i in range(slot_count):
            for w in range(slot_count):
                held = jnp.where(map_ref[i] == w, 1.0, 0.0)
                held_ref[w, i : i + 1, :] = jnp.full((1, LANES), held, jnp.float32)

        lens_ref[...] = jnp.full((SUBLANES, LANES), 4.0, jnp.float32)
        weights_ref[...] = jnp.zeros((SUBLANES, LANES), jnp.float32)
        for v in range(waves):

            @pl.when(at_wave() == v)
            def _(v=v):
                for t in range(tiles):
                    size = min(LANES, here - t * LANES)
                    at = v * here + t * LANES
                    lens = len_row_ref[at : at + size].astype(jnp.float32).reshape(1, size)
                    weights = weight_row_ref[at : at + size].reshape(1, size)
                    for h in range(2):
                        k = h * (SUBLANES // 2) + t
                        lens_ref[k : k + 1, 0:size] = lens
                        weights_ref[k : k + 1, 0:size] = weights

        wave, part, row, cycle = lane_facts(slot_count)
        tile, _ = tile_of_row(0, span, slot_count)
        first = (tile * LANES).astype(jnp.float32)
        order = (step * wave).astype(jnp.float32)
        stride = order * (LANES * SUBLANES / 2.0)
        imag = part == 1
        way = (1 - 2 * cycle).astype(jnp.float32)
        down = lax.broadcasted_iota(jnp.int32, (SUBLANES, LANES), 0)
        turn = step * lax.broadcasted_iota(jnp.int32, (SUBLANES, LANES), 1).astype(jnp.float32)
        mine = [row == i // 2 if i % 2 == 0 else jnp.logical_and(row == i // 2, cycle == 1) for i in range(SUBLANES)]
        second = down % 2 == 1
        start = at_wave() * here

        def body(g, carry):
            lens = [
                len_ref[start + jnp.minimum(g * SUBLANES + i, here - 1)] for i in range(SUBLANES)
            ]
            length = jnp.full((SUBLANES, LANES), lens[0], jnp.int32)
            length_down, before, before_down = length, length, length
            for i in range(1, SUBLANES):
                length = jnp.where(mine[i], lens[i], length)
                length_down = jnp.where(down == i, lens[i], length_down)
            for r in range(1, per):
                before = jnp.where(row == r, lens[2 * r], before)
                before_down = jnp.where(down // 2 == r, lens[2 * r], before_down)
            length = length.astype(jnp.float32)
            offset = jnp.where(cycle == 1, before, 0).astype(jnp.float32)
            split = (before >> (LANES.bit_length() - 1)).astype(jnp.float32)
            marks = jnp.where(second, before_down + length_down, before_down & (LANES - 1))
            length_down = length_down.astype(jnp.float32)
            inverse = 1.0 / length
            cos, sin = circle(order * (first - offset), length, inverse)
            o_ref[g, 0] = jnp.where(imag, sin, cos)
            o_ref[g, 1] = jnp.where(imag, cos, -sin)
            cos, sin = circle(stride, length, inverse)
            turns = jnp.where(down == 0, cos, sin)
            o_ref[g, 2] = jnp.where(down < 2, turns, way * split)
            cos, sin = circle(turn, length_down, 1.0 / length_down)
            o_ref[g, 3] = cos
            o_ref[g, 4] = -sin
            o_ref[g, 5] = 1.0 - 2.0 * sin * sin
            o_ref[g, 6] = -2.0 * sin * cos
            o_ref[g, 7] = marks.astype(jnp.float32)
            return carry

        lax.fori_loop(0, groups, body, 0, unroll=19)
        copy.wait()

    flat = jax.ShapeDtypeStruct((SUBLANES, LANES), jnp.float32)
    return pl.pallas_call(
        kernel,
        out_shape=(
            jax.ShapeDtypeStruct((rows, degrees_all), jnp.float32),
            jax.ShapeDtypeStruct((rows, degrees_all), jnp.float32),
            jax.ShapeDtypeStruct((2, rows, own), jnp.float32),
            jax.ShapeDtypeStruct(panel.shape, panel.dtype),
            jax.ShapeDtypeStruct((groups, 8, SUBLANES, LANES), jnp.float32),
            flat,
            flat,
            jax.ShapeDtypeStruct((slot_count, slot_count, LANES), jnp.float32),
        ),
        in_specs=[smem()] * 2 + [vmem()] * 3 + [pl.BlockSpec(memory_space=pl.ANY), vmem()],
        out_specs=(vmem(),) * 8,
        scratch_shapes=[pltpu.SemaphoreType.DMA],
        compiler_params=params(),
        cost_estimate=cost(3 * 10**9, 10**6),
        name="prepare",
    )(cycle_len, wave_map, cycle_len, gauss_w, spec, panel, signs)


def grid_values(fourier, tables, span, slot_count, rows_out, tiles):
    groups = tables.shape[0]
    per = SUBLANES // 2
    block = groups // STEPS
    blocks = -(-(span + SUBLANES // 2) // SUBLANES)
    size = 4 * slot_count
    kinds = 4 * slot_count
    around = LANES // SUBLANES

    total = rows_out * span
    tail = total % (2 * SUBLANES)
    tail_group, tail_at = divmod(total - tail, per * span)

    def kernel(fourier_ref, table_ref, o_hbm, rows_ref, wave_ref, part_ref, tail_ref, sems):
        wave, _, row, cycle = lane_facts(slot_count)
        way = (1 - 2 * cycle).astype(jnp.float32)
        point = lax.broadcasted_iota(jnp.int32, (SUBLANES, LANES), 1).astype(jnp.float32)
        down = lax.broadcasted_iota(jnp.int32, (SUBLANES, LANES), 0)
        second = down % 2 == 1
        unit = jnp.where(down < 2, 1.0, 0.0)
        beside = jnp.where(down < 6, -1.0, 1.0)
        for c in range(2):
            for h in range(2):
                for t in range(tiles):
                    at = (c * 2 + h) * slot_count
                    k = c * SUBLANES + h * (SUBLANES // 2) + t
                    rows_ref[t, at : at + slot_count, :] = fourier_ref[
                        pl.ds(k, slot_count, stride=2 * SUBLANES), :
                    ]
        pick = lax.broadcasted_iota(jnp.int32, (LANES, LANES), 0)
        lane = lax.broadcasted_iota(jnp.int32, (LANES, LANES), 1)
        pick = jnp.where(pick == lane // size * 2 + lane % 2, 1.0, 0.0).astype(jnp.bfloat16)

        turned = []
        for g in range(groups):
            shift = -g % around * SUBLANES
            value = rows_ref[g // around]
            turned.append(pltpu.roll(value, shift, 1) if shift else value)
        spread = jnp.dot(
            jnp.concatenate(turned, axis=0).astype(jnp.bfloat16), pick, preferred_element_type=jnp.float32
        )
        for g in range(groups):
            sums = []
            for k in range(4):
                at = g * kinds + k * slot_count
                value = jnp.where(down == wave, spread[at : at + SUBLANES], 0.0)
                sums.append(jnp.sum(value, axis=0, keepdims=True))
            for c in range(2):
                wave_ref[g, c] = jnp.where(down % 2 == 0, sums[2 * c], sums[2 * c + 1])

        def one_group(base, i, g):
            real, imag = wave_ref[g, 0], wave_ref[g, 1]
            x = real * table_ref[g, 0] + imag * table_ref[g, 1]
            y = real * table_ref[g, 1] - imag * table_ref[g, 0]
            turn_cos, turn_sin = table_ref[g, 2, 0:1], table_ref[g, 2, 1:2]
            split = table_ref[g, 2, 2:3]
            main, mixed = [], []
            for k in range(blocks):
                if k:
                    x, y = x * turn_cos + y * turn_sin, y * turn_cos - x * turn_sin
                tile, inside = tile_of_row(k, span, slot_count)
                apart = tile.astype(jnp.float32) * way - split
                value = jnp.where(inside, x, 0.0) if k in (0, blocks - 1) else x
                main.append(jnp.where(apart < 0.0, value, 0.0))
                mixed.append(jnp.where(apart == 0.0, value, 0.0))
            main, mixed = jnp.concatenate(main, axis=0), jnp.concatenate(mixed, axis=0)
            left = jnp.concatenate([main, mixed], axis=1).astype(jnp.bfloat16)

            columns, ends = [], []
            for r in range(per):
                ends.append(table_ref[g, 7, 2 * r + 1 : 2 * r + 2])
                cos1, sin1, cos2, sin2 = [
                    jnp.where(
                        second,
                        table_ref[g, i, 2 * r + 1 : 2 * r + 2],
                        table_ref[g, i, 2 * r : 2 * r + 1],
                    )
                    for i in range(3, 7)
                ]
                twice = 2.0 * cos2
                series = [jnp.where(down < 4, unit, jnp.where(down < 6, cos1, sin1))]
                third = series[0] * (twice + beside)
                series.append(jnp.where(down < 2, cos2, jnp.where(down < 4, sin2, third)))
                here = jnp.logical_xor(point < table_ref[g, 7, 2 * r : 2 * r + 1], second)
                for _ in range(2, size // SUBLANES):
                    series.append(twice * series[-1] - series[-2])
                full = jnp.concatenate(series, axis=0).astype(jnp.bfloat16)
                part = jnp.concatenate([jnp.where(here, v, 0.0) for v in series], axis=0).astype(jnp.bfloat16)
                before = [jnp.zeros((r * size, LANES), jnp.bfloat16)] if r else []
                after = [jnp.zeros((LANES - (r + 1) * size, LANES), jnp.bfloat16)] if r < per - 1 else []
                columns.append(jnp.concatenate(before + [full] + after + before + [part] + after, axis=0))
            right = jnp.concatenate(columns, axis=1)
            product = jnp.dot(left, right, preferred_element_type=jnp.float32)
            places = {}
            for r in range(per):
                shift = r * span % SUBLANES
                for k in range(blocks):
                    if k * SUBLANES >= shift + span:
                        continue
                    value = product[k * SUBLANES : (k + 1) * SUBLANES, r * LANES : (r + 1) * LANES]
                    if k == blocks - 1:
                        position = ((down + k * SUBLANES - shift) // 2 * LANES).astype(jnp.float32) + point
                        value = jnp.where(position < ends[r], value, 0.0)
                    places.setdefault((r * span - shift) // SUBLANES + k, []).append(value)
            whole = [functools.reduce(lambda a, b: a + b, places[k]) for k in sorted(places)]
            size_out = per * span
            part_ref[base, i * size_out : (i + 1) * size_out, :] = jnp.concatenate(
                whole, axis=0
            ).astype(jnp.bfloat16)
            if tail and i == tail_group % block:
                tail_ref[...] = whole[tail_at // SUBLANES].astype(jnp.bfloat16)

        size_out = per * span
        cuts = [piece * block // PIECES for piece in range(PIECES + 1)]

        def copy(i, piece):
            start, end = cuts[piece] * size_out, cuts[piece + 1] * size_out
            place = i * block * size_out
            size = min(end, total - tail - place) - start
            return pltpu.make_async_copy(
                part_ref.at[i, pl.ds(start, size), :],
                o_hbm.at[pl.ds(place + start, size), :],
                sems.at[PIECES * i + piece],
            )

        def step(base, carry):
            for piece in range(PIECES):
                for i in range(cuts[piece], cuts[piece + 1]):
                    one_group(base, i, base * block + i)
                for i in range(STEPS):

                    @pl.when(base == i)
                    def _(i=i, piece=piece):
                        copy(i, piece).start()

            return carry

        lax.fori_loop(0, STEPS, step, 0)
        if tail:
            rest = pltpu.make_async_copy(
                tail_ref, o_hbm.at[pl.ds(total - tail, tail), :], sems.at[PIECES * STEPS]
            )
            rest.start()
        for i in range(STEPS):
            for piece in range(PIECES):
                copy(i, piece).wait()
        if tail:
            rest.wait()

    return pl.pallas_call(
        kernel,
        out_shape=jax.ShapeDtypeStruct((rows_out * span, LANES), jnp.bfloat16),
        in_specs=[vmem()] * 2,
        out_specs=pl.BlockSpec(memory_space=pl.ANY),
        scratch_shapes=[
            pltpu.VMEM((tiles, kinds, LANES), jnp.float32),
            pltpu.VMEM((groups, 2, SUBLANES, LANES), jnp.float32),
            pltpu.VMEM((STEPS, block * per * span, LANES), jnp.bfloat16),
            pltpu.VMEM((SUBLANES, LANES), jnp.bfloat16),
            pltpu.SemaphoreType.DMA((PIECES * STEPS + 1,)),
        ],
        compiler_params=params(16 * 1024 * 1024),
        cost_estimate=cost(8 * 10**9, 3 * 10**6),
        name="grid_values",
    )(fourier, tables)


def direct(returned, factors, panels):
    waves, tall, _ = returned.shape
    depth, lats = panels[0].shape
    own, here = factors.shape[2], lats // waves
    slots, half = depth // own, factors.shape[1] // 2
    chips = tall // (2 * half)

    def kernel(x_ref, factor_ref, own_ref, other_ref, *refs):
        o_refs, left_ref, all_ref = refs[:chips], refs[chips], refs[chips + 1]
        for place, j in enumerate(from_middle(waves)):
            left_ref[:, j * here : (j + 1) * here] = x_ref[place, :, 0:here].astype(jnp.float32)
        left = left_ref[...].astype(jnp.bfloat16)
        shape = (chips, half, own)
        slot_of = lax.broadcasted_iota(jnp.int32, shape, 1) // 2
        for e, panel_ref in enumerate((own_ref, other_ref)):
            total = lax.dot_general(
                left, panel_ref[...], (((1,), (1,)), ((), ())), preferred_element_type=jnp.float32
            ).reshape(chips, 2 * half, depth)
            result = jnp.zeros(shape, jnp.float32)
            for s in range(slots):
                mine = total[:, :, s * own : (s + 1) * own] * factor_ref[e][None]
                result = jnp.where(slot_of == s, mine[:, :half] + mine[:, half:], result)
            all_ref[:, e * half : (e + 1) * half, :] = result
        for i in range(chips):
            o_refs[i][...] = all_ref[(at_level() // 2) ^ i ^ turned(chips)]

    return pl.pallas_call(
        kernel,
        out_shape=(jax.ShapeDtypeStruct((2 * half, own), jnp.float32),) * chips,
        in_specs=[vmem()] * 4,
        out_specs=(vmem(),) * chips,
        scratch_shapes=[
            pltpu.VMEM((tall, lats), jnp.float32),
            pltpu.VMEM((chips, 2 * half, own), jnp.float32),
        ],
        compiler_params=params(),
        cost_estimate=cost(10**9, 2 * 10**6),
        name="direct",
    )(returned, factors, *panels)


def join_degrees(pieces, slots):
    chips = len(pieces)
    rows, own = pieces[0].shape
    half = rows // 2

    def kernel(*refs):
        piece_refs, o_ref, all_ref = refs[:chips], refs[chips], refs[chips + 1]
        for i in range(chips):
            for e in range(2):
                all_ref[at_level() ^ (2 * i + e)] = piece_refs[i][e * half : (e + 1) * half, :]
        whole = jnp.concatenate([all_ref[v] for v in range(2 * chips)], axis=1)
        for s in range(slots):
            o_ref[s] = whole[2 * s : 2 * s + 2]

    return pl.pallas_call(
        kernel,
        out_shape=jax.ShapeDtypeStruct((slots, 2, 2 * chips * own), jnp.float32),
        in_specs=[vmem()] * chips,
        out_specs=vmem(),
        scratch_shapes=[pltpu.VMEM((2 * chips, half, own), jnp.float32)],
        compiler_params=params(),
        name="join_degrees",
    )(*pieces)


def evenly_spaced(levels, spec, legendre, gauss_w, cycle_len, wave_map):
    slots = spec.shape[0]
    degrees_all = spec.shape[3]
    own = legendre.shape[1]
    lats = legendre.shape[2]
    slot_count = wave_map.shape[0]
    step = degrees_all // slot_count
    waves = slot_count // slots
    chips = levels // 2

    def across(x, bits):
        return lax.ppermute(x, "lev", [(j, j ^ bits) for j in range(levels)])

    def same_core(x):
        groups = [
            [
                wave * levels + 2 * (chip ^ turned(chips)) + core
                for wave in from_middle(waves)
                for chip in range(chips)
            ]
            for core in range(2)
        ]
        return lax.all_to_all(x, ("wave", "lev"), 0, 0, tiled=True, axis_index_groups=groups)

    mine = spec.reshape(slots, 2, degrees_all)
    others = [across(mine, 2 * i) for i in range(1, chips)]
    panel = legendre.reshape(slots * own, lats)
    signs = parity_signs(2 * slots * 2, degrees_all)
    here = lats // waves
    wide = -(-here // LANES) * LANES
    tiles = wide // LANES
    per = SUBLANES // 2
    rows_out = here // 2
    groups = -(-rows_out // (per * STEPS)) * STEPS
    span = 2 * (LPAD // LANES)
    rows_here = 2 * slots * 2
    first, factor, factors, near, tables, lens, weights, held = prepare(
        cycle_len, gauss_w, wave_map, mine, panel, signs, span, step, waves, groups, wide
    )
    panels = (near, across(panel, 1))

    part = partial_fourier(first, factor, others, panels, slots, waves, wide)
    part = same_core(part.reshape(waves * chips, rows_here, wide))
    fourier, returned = quadratic(held, part, lens, weights, waves, step)
    returned = same_core(returned)

    values = grid_values(fourier, tables, span, slot_count, rows_out, tiles)
    values = values.reshape(rows_out, span // 2, 2, LANES)
    values = with_layout_constraint(values, Layout(major_to_minor=(0, 1, 2, 3)))
    values = values.transpose(0, 2, 1, 3)
    values = with_layout_constraint(values, Layout(major_to_minor=(0, 2, 1, 3)))
    values = values.reshape(rows_out, 2, LPAD)
    values = with_layout_constraint(values, Layout(major_to_minor=(0, 1, 2)))
    grid = values.transpose(1, 0, 2).reshape(2, rows_out, 1, LPAD)

    returned = returned.reshape(waves, chips * rows_here, wide)
    pieces = direct(returned, factors, (panel, panels[1]))
    pieces = [pieces[0]] + [across(pieces[i], 2 * i) for i in range(1, chips)]
    spec_out = join_degrees(pieces, slots).reshape(slots, 1, 2, degrees_all)
    return (grid, spec_out)


def per_device(levels, spec, legendre, gauss_w, cycle_len, wave_map):
    slot_count = wave_map.shape[0]
    fits = (
        spec.shape[3] % slot_count == 0
        and 2 * slot_count * SUBLANES == LANES
        and spec.shape[1] == 1
        and 4 * spec.shape[0] == SUBLANES
        and levels > 1
        and levels & (levels - 1) == 0
    )
    if fits:
        return evenly_spaced(levels, spec, legendre, gauss_w, cycle_len, wave_map)
    return general(spec, legendre, gauss_w, cycle_len, wave_map)


def solution(mesh):
    placed = (P("wave", "lev", None, None), P("wave", "lev", None), P(), P(), P())
    return jax.shard_map(
        functools.partial(per_device, mesh.shape["lev"]),
        mesh=mesh,
        in_specs=placed,
        out_specs=(P(None, "wave", "lev", None), P("wave", "lev", None, None)),
        check_vma=False,
    )
```

```python
import functools
import math

import jax
import jax.numpy as jnp
from jax import lax
from jax.experimental import pallas as pl
from jax.experimental.layout import Layout, with_layout_constraint
from jax.experimental.pallas import tpu as pltpu
from jax.sharding import PartitionSpec as P

LPAD = 4864


def block_rows():
    for candidate in (10, 8, 6, 5, 4, 3, 2):
        return candidate
    return 1


def cycle_tables(lens_pair, orders, padded):
    position = jnp.arange(padded, dtype=jnp.int32)[None, :]
    first_len = lens_pair[:, 0:1]
    second = lens_pair[:, 1:2]
    upper_half = position >= first_len
    occupied = position < first_len + second
    offset = jnp.where(upper_half, position - first_len, position)
    length = jnp.where(upper_half, second, first_len)
    turn_count = orders[None, :, None] * offset[:, None, :] % length[:, None, :]
    angles = 2.0 * math.pi * turn_count.astype(jnp.float32) / length[:, None, :].astype(jnp.float32)
    cosine = jnp.where(occupied[:, None, :], jnp.cos(angles), 0.0).astype(jnp.bfloat16)
    minus_sine = jnp.where(occupied[:, None, :], -jnp.sin(angles), 0.0).astype(jnp.bfloat16)
    return (jnp.concatenate([cosine, minus_sine], 1), upper_half, occupied)


def cycle_block(waves, lens_pair, weights, orders, padded):
    row_count = waves.shape[0]
    fields = waves.shape[3]
    slot_count = orders.shape[0]
    tables, upper_half, occupied = cycle_tables(lens_pair, orders, padded)
    double = jnp.where(orders == 0, 1.0, 2.0)
    resolved = 2 * orders[None, None, :] < lens_pair[:, :, None]
    widening = jnp.where(resolved, double[None, None, :], 0.0)
    scaled = (waves.astype(jnp.float32) * widening[:, None, :, None, None, :]).astype(jnp.bfloat16)
    scaled = scaled.reshape(row_count, 4 * fields, 2 * slot_count)
    images = jnp.einsum("rak,rkp->rap", scaled, tables, preferred_element_type=jnp.float32)
    images = images.reshape(row_count, 2, 2, fields, padded)
    values = jnp.where(upper_half[:, None, None, :], images[:, :, 1], images[:, :, 0])
    values = jnp.where(occupied[:, None, None, :], values, 0.0).astype(jnp.bfloat16)
    squared = (values.astype(jnp.float32) * values.astype(jnp.float32)).astype(jnp.bfloat16)
    selector = jnp.stack([jnp.logical_not(upper_half), upper_half], 1)
    by_cycle = jnp.where(
        selector[:, None, :, None, :], squared[:, :, None, :, :], jnp.zeros((), jnp.bfloat16)
    )
    by_cycle = by_cycle.reshape(row_count, 4 * fields, padded)
    returned = jnp.einsum("rap,rkp->rak", by_cycle, tables, preferred_element_type=jnp.float32)
    returned = returned.reshape(row_count, 2, 2, fields, 2, slot_count)
    factor = jnp.where(
        resolved, weights[:, :, None] / lens_pair[:, :, None].astype(jnp.float32), 0.0
    )
    returned = (returned * factor[:, None, :, None, None, :]).astype(jnp.bfloat16)
    return (values, returned)


def parity_of(degree_ids, own_orders):
    return jnp.where((degree_ids[None, :] + own_orders[:, None]) % 2 == 0, 1.0, -1.0)


def general(spec, legendre, gauss_w, cycle_len, wave_map):
    slots_dev = spec.shape[0]
    fields = spec.shape[1]
    degrees_all = spec.shape[3]
    slot_count = wave_map.shape[0]
    orders = wave_map * degrees_all // slot_count
    wave_pos = lax.axis_index("wave")
    own_orders = lax.dynamic_slice_in_dim(orders, wave_pos * slots_dev, slots_dev)
    degrees = jnp.arange(degrees_all, dtype=jnp.int32)
    retained = degrees[None, :] >= own_orders[:, None]
    coefficients = jnp.where(retained[:, None, None, :], spec, jnp.zeros((), jnp.bfloat16))
    panels = lax.all_gather(legendre, "lev", axis=1, tiled=True)
    sign_flip = parity_of(degrees, own_orders)
    flipped = (coefficients.astype(jnp.float32) * sign_flip[:, None, None, :]).astype(jnp.bfloat16)
    stacked = jnp.stack([coefficients, flipped], 1)
    fourier = jnp.einsum(
        "shfcn,snq->shfcq", stacked, panels, preferred_element_type=jnp.float32
    ).astype(jnp.bfloat16)
    cycle_waves = lax.all_to_all(fourier, "wave", split_axis=4, concat_axis=0, tiled=True)
    local_lats = cycle_waves.shape[4]
    row_total = local_lats // 2
    lat_start = wave_pos * local_lats
    lens_here = lax.dynamic_slice_in_dim(cycle_len, lat_start, local_lats)
    weights_here = lax.dynamic_slice_in_dim(gauss_w, lat_start, local_lats)
    row_block = block_rows()
    blocks = row_total // row_block
    ordered = cycle_waves.reshape(slot_count, 2, fields, 2, row_total, 2).transpose(
        4, 1, 5, 2, 3, 0
    )
    ordered = ordered.reshape(blocks, row_block, 2, 2, fields, 2, slot_count)

    def run_block(operands):
        return cycle_block(operands[0], operands[1], operands[2], orders, LPAD)

    values, returned = lax.map(
        run_block,
        (
            ordered,
            lens_here.reshape(blocks, row_block, 2),
            weights_here.reshape(blocks, row_block, 2),
        ),
    )
    grid = values.reshape(row_total, 2, fields, LPAD).transpose(1, 0, 2, 3)
    returned = returned.reshape(row_total, 2, 2, fields, 2, slot_count).transpose(5, 1, 3, 4, 0, 2)
    returned = returned.reshape(slot_count, 2, fields, 2, local_lats)
    spectral = lax.all_to_all(returned, "wave", split_axis=0, concat_axis=4, tiled=True)
    both = jnp.einsum("shfcq,snq->shfcn", spectral, panels, preferred_element_type=jnp.float32)
    total = both[:, 0] + sign_flip[:, None, None, :] * both[:, 1]
    spec_out = jnp.where(retained[:, None, None, :], total, 0.0)
    return (grid, spec_out)


LANES = 128
SUBLANES = 8
STEPS = 2
PIECES = 4
VMEM = 8 * 1024 * 1024
SINE = (6.28318516, -41.34165503, 81.60100407, -76.54978222, 39.53670553)


def circle(x, period, inverse):
    turn = (x - period * jnp.floor(x * inverse + 0.5)) * inverse
    away = jnp.abs(turn)
    values = []
    for v in (0.25 - away, 0.25 - jnp.abs(away - 0.25)):
        y = v * v
        series = SINE[4]
        for coefficient in SINE[3::-1]:
            series = series * y + coefficient
        values.append(v * series)
    return values[0], jnp.where(turn < 0.0, -values[1], values[1])


def params(memory=VMEM):
    return pltpu.CompilerParams(vmem_limit_bytes=memory)


def cost(flops, nbytes):
    return pl.CostEstimate(flops=flops, bytes_accessed=nbytes, transcendentals=0)


def at_wave():
    return lax.axis_index("wave")


def at_level():
    return lax.axis_index("lev")


def from_middle(count):
    return sorted(range(count), key=lambda i: (abs(2 * i - count + 1), -i))


def turned(chips):
    return chips // 2


def smem():
    return pl.BlockSpec(memory_space=pltpu.SMEM)


def vmem():
    return pl.BlockSpec(memory_space=pltpu.VMEM)


def parity_signs(rows, degrees_all):
    def kernel(o_ref):
        row = lax.broadcasted_iota(jnp.int32, (rows, degrees_all), 0)
        degree = lax.broadcasted_iota(jnp.int32, (rows, degrees_all), 1)
        odd = jnp.logical_and(row >= rows // 2, (degree & 1) == 1)
        o_ref[...] = jnp.where(odd, -1.0, 1.0)

    return pl.pallas_call(
        kernel,
        out_shape=jax.ShapeDtypeStruct((rows, degrees_all), jnp.float32),
        out_specs=vmem(),
        compiler_params=params(),
        cost_estimate=cost(4 * 10**9, 10**6),
        name="parity_signs",
    )()


def partial_fourier(first, factor, others, panels, slots, waves):
    chips = len(others) + 1
    rows, degrees_all = first.shape
    parts = rows // (2 * slots)
    depth, lats = panels[0].shape
    own, here = depth // slots, lats // waves

    def kernel(first_ref, factor_ref, *refs):
        spec_refs, panel_refs = refs[: chips - 1], refs[chips - 1 : chips + 1]
        o_ref, left_ref = refs[chips + 1 :]
        factor = factor_ref[...]
        whole = [first_ref[...]]
        for ref in spec_refs:
            x = [ref[s].astype(jnp.float32) for s in range(slots)]
            whole.append(jnp.concatenate(x + x, axis=0) * factor)
        whole = jnp.concatenate(whole, axis=0)
        slot_of = lax.broadcasted_iota(jnp.int32, (chips * rows, own), 0) // parts % slots
        for level in range(2 * chips):

            @pl.when(at_level() == level)
            def _(level=level):
                for e in range(2):
                    start = (level ^ e) * own
                    piece = whole[:, start : start + own]
                    left = [jnp.where(slot_of == s, piece, 0.0) for s in range(slots)]
                    left_ref[e] = jnp.concatenate(left, axis=1).astype(jnp.bfloat16)

        total = jnp.dot(left_ref[0], panel_refs[0][...], preferred_element_type=jnp.float32)
        total += jnp.dot(left_ref[1], panel_refs[1][...], preferred_element_type=jnp.float32)
        chip = at_level() // 2
        places = [from_middle(waves).index(j) for j in range(waves)]
        half, full = rows // 2, here // LANES
        fill = jnp.zeros((half, LANES // 2 - here % LANES), jnp.float32)
        for i in range(chips):
            for j in range(waves):
                tiles = []
                for t in range(full + 1):
                    start = j * here + t * LANES
                    both = [
                        total[i * rows + h * half : i * rows + (h + 1) * half, start : min(start + LANES, (j + 1) * here)]
                        for h in range(2)
                    ]
                    if t == full:
                        both = [jnp.concatenate([both[0], fill, both[1], fill], axis=1)]
                    tiles += both
                for k, tile in enumerate(tiles):
                    o_ref[places[j], chip ^ i ^ turned(chips), k] = tile.astype(jnp.bfloat16)

    return pl.pallas_call(
        kernel,
        out_shape=jax.ShapeDtypeStruct(
            (waves, chips, 2 * (here // LANES) + 1, rows // 2, LANES), jnp.bfloat16
        ),
        in_specs=[vmem()] * (chips + 3),
        out_specs=vmem(),
        scratch_shapes=[pltpu.VMEM((2, chips * rows, depth), jnp.bfloat16)],
        compiler_params=params(),
        cost_estimate=cost(10**9, 2 * 10**6),
        name="partial_fourier",
    )(first, factor, *others, *panels)


def quadratic(held, parts_sum, lens, weights, waves, step):
    sources, packs, half, _ = parts_sum.shape
    slot_count = held.shape[0]
    levels = sources // waves
    slots = slot_count // waves
    full = packs // 2
    top = 2 * (slot_count - 1)
    shape = (SUBLANES, LANES)

    def kernel(held_ref, x_ref, len_ref, weight_ref, g_ref, o_ref, z_ref, r_ref):
        z_ref[...] = jnp.zeros(z_ref.shape, jnp.float32)
        for place, i in enumerate(from_middle(waves)):
            total = x_ref[place * levels].astype(jnp.float32)
            for j in range(1, levels):
                total = total + x_ref[place * levels + j].astype(jnp.float32)
            total = total.astype(jnp.bfloat16).astype(jnp.float32)
            for t in range(full + 1):
                for h in range(2):
                    at = i * half * SUBLANES + h * (SUBLANES // 2) + t
                    if t < full:
                        value = total[2 * t + h]
                    else:
                        value = pltpu.roll(total[2 * t], LANES // 2, 1) if h else total[2 * t]
                    z_ref[pl.ds(at, half, stride=SUBLANES), :] = value
        lens_here = len_ref[...]
        kept = [
            jnp.where(lens_here > 2.0 * step * w, 1.0, 0.0) for w in range(slot_count)
        ]
        held = [
            [held_ref[w, i : i + 1, :] > 0.5 for i in range(slot_count)] for w in range(slot_count)
        ]
        real, imag = [], []
        for w in range(slot_count):
            re, im = jnp.zeros(shape, jnp.float32), jnp.zeros(shape, jnp.float32)
            for i in range(slot_count):
                at = i * 2 * SUBLANES
                re = jnp.where(held[w][i], z_ref[at : at + SUBLANES, :], re)
                im = jnp.where(held[w][i], z_ref[at + SUBLANES : at + 2 * SUBLANES, :], im)
            real.append(re * kept[w])
            imag.append(im * kept[w])
        for w in range(slot_count):
            double = 1.0 if w == 0 else 2.0
            at = 2 * w * SUBLANES
            g_ref[at : at + SUBLANES, :] = real[w] * double
            g_ref[at + SUBLANES : at + 2 * SUBLANES, :] = imag[w] * double
        imag[0] = jnp.zeros(shape, jnp.float32)
        square_real, square_imag = [], []
        for n in range(top + 1):
            re, im = jnp.zeros(shape, jnp.float32), jnp.zeros(shape, jnp.float32)
            for a in range(max(0, n - slot_count + 1), (n + 1) // 2):
                b = n - a
                re = re + (real[a] * real[b] - imag[a] * imag[b])
                im = im + (real[a] * imag[b] + imag[a] * real[b])
            for b in range(1, slot_count - n):
                a = n + b
                re = re + (real[a] * real[b] + imag[a] * imag[b])
                im = im + (imag[a] * real[b] - real[a] * imag[b])
            re, im = 2.0 * re, 2.0 * im
            if n % 2 == 0:
                a = n // 2
                re = re + (real[a] * real[a] - imag[a] * imag[a])
                im = im + 2.0 * (real[a] * imag[a])
            square_real.append(re)
            square_imag.append(im)
        whole = {
            d: jnp.where(lens_here == 1.0 * step * d, 1.0, 0.0)
            for d in range(3, top + slot_count)
        }
        weights_here = weight_ref[...]
        result = []
        for w in range(slot_count):
            re, im = square_real[w], square_imag[w]
            if w == 0:
                im = jnp.zeros(shape, jnp.float32)
            else:
                for n in range(w + 1, top + 1):
                    re = re + whole[w + n] * square_real[n]
                    im = im - whole[w + n] * square_imag[n]
            factor = kept[w] * weights_here
            result.append((re * factor, im * factor))
        for i in range(slot_count):
            re, im = result[0]
            for w in range(1, slot_count):
                re = jnp.where(held[w][i], result[w][0], re)
                im = jnp.where(held[w][i], result[w][1], im)
            at = i * 2 * SUBLANES
            r_ref[at : at + SUBLANES, :] = re
            r_ref[at + SUBLANES : at + 2 * SUBLANES, :] = im
        for place, i in enumerate(from_middle(waves)):
            for t in range(full + 1):
                both = [
                    r_ref[pl.ds(i * half * SUBLANES + h * (SUBLANES // 2) + t, half, stride=SUBLANES), :]
                    for h in range(2)
                ]
                if t == full:
                    both = [both[0] + pltpu.roll(both[1], LANES // 2, 1)]
                for h, value in enumerate(both):
                    packed = value.astype(jnp.bfloat16)
                    for j in range(levels):
                        o_ref[place * levels + j, 2 * t + h] = packed

    return pl.pallas_call(
        kernel,
        out_shape=(
            jax.ShapeDtypeStruct((2 * slot_count * SUBLANES, LANES), jnp.float32),
            jax.ShapeDtypeStruct(parts_sum.shape, jnp.bfloat16),
        ),
        in_specs=[vmem()] * 4,
        out_specs=(vmem(), vmem()),
        scratch_shapes=[
            pltpu.VMEM((2 * slot_count * SUBLANES, LANES), jnp.float32),
            pltpu.VMEM((2 * slot_count * SUBLANES, LANES), jnp.float32),
        ],
        compiler_params=params(),
        name="quadratic",
    )(held, parts_sum, lens, weights)


def lane_facts(slot_count):
    lane = lax.broadcasted_iota(jnp.int32, (SUBLANES, LANES), 1)
    return (lane % (4 * slot_count) // 4, lane % 4 // 2, lane // (4 * slot_count), lane % 2)


def tile_of_row(block, span, slot_count):
    at = lax.broadcasted_iota(jnp.int32, (SUBLANES, LANES), 0) + block * SUBLANES
    at = at - lane_facts(slot_count)[2] * span % SUBLANES
    return at // 2, jnp.logical_and(at >= 0, at < span)


def prepare(cycle_len, gauss_w, wave_map, spec, panel, signs, span, step, waves, groups, wide):
    slot_count = wave_map.shape[0]
    slots, parts, degrees_all = spec.shape
    own = panel.shape[0] // slots
    levels = degrees_all // own
    rows = 2 * slots * parts
    here = cycle_len.shape[0] // waves
    tiles = wide // LANES
    per = SUBLANES // 2

    def kernel(
        len_ref, map_ref, len_row_ref, weight_row_ref, x_ref, panel_ref, sign_ref,
        first_ref, factor_ref, factors_ref, near_ref, o_ref, lens_ref, weights_ref, held_ref, sem,
    ):
        copy = pltpu.make_async_copy(panel_ref, near_ref, sem)
        copy.start()
        row_of = lax.broadcasted_iota(jnp.int32, (rows, degrees_all), 0)
        degree = lax.broadcasted_iota(jnp.int32, (rows, degrees_all), 1)
        bound = jnp.zeros((rows, degrees_all), jnp.int32)
        for s in range(slots):
            mine = row_of // parts % slots == s
            bound = jnp.where(mine, map_ref[at_wave() * slots + s] * step, bound)
        turned = jnp.logical_and(row_of >= rows // 2, (bound & 1) == 1)
        sign = sign_ref[...]
        factor = jnp.where(degree >= bound, jnp.where(turned, -sign, sign), 0.0)
        factor_ref[...] = factor
        x = [x_ref[s].astype(jnp.float32) for s in range(slots)]
        first_ref[...] = jnp.concatenate(x + x, axis=0) * factor
        for level in range(levels):

            @pl.when(at_level() == level)
            def _(level=level):
                for e in range(2):
                    start = (level ^ e) * own
                    factors_ref[e] = factor[:, start : start + own]

        for i in range(slot_count):
            for w in range(slot_count):
                held = jnp.where(map_ref[i] == w, 1.0, 0.0)
                held_ref[w, i : i + 1, :] = jnp.full((1, LANES), held, jnp.float32)

        lens_ref[...] = jnp.full((SUBLANES, LANES), 4.0, jnp.float32)
        weights_ref[...] = jnp.zeros((SUBLANES, LANES), jnp.float32)
        for v in range(waves):

            @pl.when(at_wave() == v)
            def _(v=v):
                for t in range(tiles):
                    size = min(LANES, here - t * LANES)
                    at = v * here + t * LANES
                    lens = len_row_ref[at : at + size].astype(jnp.float32).reshape(1, size)
                    weights = weight_row_ref[at : at + size].reshape(1, size)
                    for h in range(2):
                        k = h * (SUBLANES // 2) + t
                        lens_ref[k : k + 1, 0:size] = lens
                        weights_ref[k : k + 1, 0:size] = weights

        wave, part, row, cycle = lane_facts(slot_count)
        tile, _ = tile_of_row(0, span, slot_count)
        first = (tile * LANES).astype(jnp.float32)
        order = (step * wave).astype(jnp.float32)
        stride = order * (LANES * SUBLANES / 2.0)
        imag = part == 1
        way = (1 - 2 * cycle).astype(jnp.float32)
        down = lax.broadcasted_iota(jnp.int32, (SUBLANES, LANES), 0)
        turn = step * lax.broadcasted_iota(jnp.int32, (SUBLANES, LANES), 1).astype(jnp.float32)
        mine = [row == i // 2 if i % 2 == 0 else jnp.logical_and(row == i // 2, cycle == 1) for i in range(SUBLANES)]
        second = down % 2 == 1
        start = at_wave() * here

        def body(g, carry):
            lens = [
                len_ref[start + jnp.minimum(g * SUBLANES + i, here - 1)] for i in range(SUBLANES)
            ]
            length = jnp.full((SUBLANES, LANES), lens[0], jnp.int32)
            length_down, before, before_down = length, length, length
            for i in range(1, SUBLANES):
                length = jnp.where(mine[i], lens[i], length)
                length_down = jnp.where(down == i, lens[i], length_down)
            for r in range(1, per):
                before = jnp.where(row == r, lens[2 * r], before)
                before_down = jnp.where(down // 2 == r, lens[2 * r], before_down)
            length = length.astype(jnp.float32)
            offset = jnp.where(cycle == 1, before, 0).astype(jnp.float32)
            split = (before >> (LANES.bit_length() - 1)).astype(jnp.float32)
            marks = jnp.where(second, before_down + length_down, before_down & (LANES - 1))
            length_down = length_down.astype(jnp.float32)
            inverse = 1.0 / length
            cos, sin = circle(order * (first - offset), length, inverse)
            o_ref[g, 0] = jnp.where(imag, sin, cos)
            o_ref[g, 1] = jnp.where(imag, cos, -sin)
            cos, sin = circle(stride, length, inverse)
            turns = jnp.where(down == 0, cos, sin)
            o_ref[g, 2] = jnp.where(down < 2, turns, way * split)
            cos, sin = circle(turn, length_down, 1.0 / length_down)
            o_ref[g, 3] = cos
            o_ref[g, 4] = -sin
            o_ref[g, 5] = 1.0 - 2.0 * sin * sin
            o_ref[g, 6] = -2.0 * sin * cos
            o_ref[g, 7] = marks.astype(jnp.float32)
            return carry

        lax.fori_loop(0, groups, body, 0, unroll=19)
        copy.wait()

    flat = jax.ShapeDtypeStruct((SUBLANES, LANES), jnp.float32)
    return pl.pallas_call(
        kernel,
        out_shape=(
            jax.ShapeDtypeStruct((rows, degrees_all), jnp.float32),
            jax.ShapeDtypeStruct((rows, degrees_all), jnp.float32),
            jax.ShapeDtypeStruct((2, rows, own), jnp.float32),
            jax.ShapeDtypeStruct(panel.shape, panel.dtype),
            jax.ShapeDtypeStruct((groups, 8, SUBLANES, LANES), jnp.float32),
            flat,
            flat,
            jax.ShapeDtypeStruct((slot_count, slot_count, LANES), jnp.float32),
        ),
        in_specs=[smem()] * 2 + [vmem()] * 3 + [pl.BlockSpec(memory_space=pl.ANY), vmem()],
        out_specs=(vmem(),) * 8,
        scratch_shapes=[pltpu.SemaphoreType.DMA],
        compiler_params=params(),
        cost_estimate=cost(3 * 10**9, 10**6),
        name="prepare",
    )(cycle_len, wave_map, cycle_len, gauss_w, spec, panel, signs)


def grid_values(fourier, tables, span, slot_count, rows_out, tiles):
    groups = tables.shape[0]
    per = SUBLANES // 2
    block = groups // STEPS
    blocks = -(-(span + SUBLANES // 2) // SUBLANES)
    size = 4 * slot_count
    kinds = 4 * slot_count
    around = LANES // SUBLANES

    total = rows_out * span
    tail = total % (2 * SUBLANES)
    tail_group, tail_at = divmod(total - tail, per * span)

    def kernel(fourier_ref, table_ref, o_hbm, rows_ref, wave_ref, part_ref, tail_ref, sems):
        wave, _, row, cycle = lane_facts(slot_count)
        way = (1 - 2 * cycle).astype(jnp.float32)
        point = lax.broadcasted_iota(jnp.int32, (SUBLANES, LANES), 1).astype(jnp.float32)
        down = lax.broadcasted_iota(jnp.int32, (SUBLANES, LANES), 0)
        second = down % 2 == 1
        unit = jnp.where(down < 2, 1.0, 0.0)
        beside = jnp.where(down < 6, -1.0, 1.0)
        for c in range(2):
            for h in range(2):
                for t in range(tiles):
                    at = (c * 2 + h) * slot_count
                    k = c * SUBLANES + h * (SUBLANES // 2) + t
                    rows_ref[t, at : at + slot_count, :] = fourier_ref[
                        pl.ds(k, slot_count, stride=2 * SUBLANES), :
                    ]
        pick = lax.broadcasted_iota(jnp.int32, (LANES, LANES), 0)
        lane = lax.broadcasted_iota(jnp.int32, (LANES, LANES), 1)
        pick = jnp.where(pick == lane // size * 2 + lane % 2, 1.0, 0.0).astype(jnp.bfloat16)

        turned = []
        for g in range(groups):
            shift = -g % around * SUBLANES
            value = rows_ref[g // around]
            turned.append(pltpu.roll(value, shift, 1) if shift else value)
        spread = jnp.dot(
            jnp.concatenate(turned, axis=0).astype(jnp.bfloat16), pick, preferred_element_type=jnp.float32
        )
        for g in range(groups):
            sums = []
            for k in range(4):
                at = g * kinds + k * slot_count
                value = jnp.where(down == wave, spread[at : at + SUBLANES], 0.0)
                sums.append(jnp.sum(value, axis=0, keepdims=True))
            for c in range(2):
                wave_ref[g, c] = jnp.where(down % 2 == 0, sums[2 * c], sums[2 * c + 1])

        def one_group(base, i, g):
            real, imag = wave_ref[g, 0], wave_ref[g, 1]
            x = real * table_ref[g, 0] + imag * table_ref[g, 1]
            y = real * table_ref[g, 1] - imag * table_ref[g, 0]
            turn_cos, turn_sin = table_ref[g, 2, 0:1], table_ref[g, 2, 1:2]
            split = table_ref[g, 2, 2:3]
            main, mixed = [], []
            for k in range(blocks):
                if k:
                    x, y = x * turn_cos + y * turn_sin, y * turn_cos - x * turn_sin
                tile, inside = tile_of_row(k, span, slot_count)
                apart = tile.astype(jnp.float32) * way - split
                value = jnp.where(inside, x, 0.0) if k in (0, blocks - 1) else x
                main.append(jnp.where(apart < 0.0, value, 0.0))
                mixed.append(jnp.where(apart == 0.0, value, 0.0))
            main, mixed = jnp.concatenate(main, axis=0), jnp.concatenate(mixed, axis=0)
            left = jnp.concatenate([main, mixed], axis=1).astype(jnp.bfloat16)

            columns, ends = [], []
            for r in range(per):
                ends.append(table_ref[g, 7, 2 * r + 1 : 2 * r + 2])
                cos1, sin1, cos2, sin2 = [
                    jnp.where(
                        second,
                        table_ref[g, i, 2 * r + 1 : 2 * r + 2],
                        table_ref[g, i, 2 * r : 2 * r + 1],
                    )
                    for i in range(3, 7)
                ]
                twice = 2.0 * cos2
                series = [jnp.where(down < 4, unit, jnp.where(down < 6, cos1, sin1))]
                third = series[0] * (twice + beside)
                series.append(jnp.where(down < 2, cos2, jnp.where(down < 4, sin2, third)))
                here = jnp.logical_xor(point < table_ref[g, 7, 2 * r : 2 * r + 1], second)
                for _ in range(2, size // SUBLANES):
                    series.append(twice * series[-1] - series[-2])
                full = jnp.concatenate(series, axis=0).astype(jnp.bfloat16)
                part = jnp.concatenate([jnp.where(here, v, 0.0) for v in series], axis=0).astype(jnp.bfloat16)
                before = [jnp.zeros((r * size, LANES), jnp.bfloat16)] if r else []
                after = [jnp.zeros((LANES - (r + 1) * size, LANES), jnp.bfloat16)] if r < per - 1 else []
                columns.append(jnp.concatenate(before + [full] + after + before + [part] + after, axis=0))
            right = jnp.concatenate(columns, axis=1)
            product = jnp.dot(left, right, preferred_element_type=jnp.float32)
            places = {}
            for r in range(per):
                shift = r * span % SUBLANES
                for k in range(blocks):
                    if k * SUBLANES >= shift + span:
                        continue
                    value = product[k * SUBLANES : (k + 1) * SUBLANES, r * LANES : (r + 1) * LANES]
                    if k == blocks - 1:
                        position = ((down + k * SUBLANES - shift) // 2 * LANES).astype(jnp.float32) + point
                        value = jnp.where(position < ends[r], value, 0.0)
                    places.setdefault((r * span - shift) // SUBLANES + k, []).append(value)
            whole = [functools.reduce(lambda a, b: a + b, places[k]) for k in sorted(places)]
            size_out = per * span
            part_ref[base, i * size_out : (i + 1) * size_out, :] = jnp.concatenate(
                whole, axis=0
            ).astype(jnp.bfloat16)
            if tail and i == tail_group % block:
                tail_ref[...] = whole[tail_at // SUBLANES].astype(jnp.bfloat16)

        size_out = per * span
        cuts = [piece * block // PIECES for piece in range(PIECES + 1)]

        def copy(i, piece):
            start, end = cuts[piece] * size_out, cuts[piece + 1] * size_out
            place = i * block * size_out
            size = min(end, total - tail - place) - start
            return pltpu.make_async_copy(
                part_ref.at[i, pl.ds(start, size), :],
                o_hbm.at[pl.ds(place + start, size), :],
                sems.at[PIECES * i + piece],
            )

        def step(base, carry):
            for piece in range(PIECES):
                for i in range(cuts[piece], cuts[piece + 1]):
                    one_group(base, i, base * block + i)
                for i in range(STEPS):

                    @pl.when(base == i)
                    def _(i=i, piece=piece):
                        copy(i, piece).start()

            return carry

        lax.fori_loop(0, STEPS, step, 0)
        if tail:
            rest = pltpu.make_async_copy(
                tail_ref, o_hbm.at[pl.ds(total - tail, tail), :], sems.at[PIECES * STEPS]
            )
            rest.start()
        for i in range(STEPS):
            for piece in range(PIECES):
                copy(i, piece).wait()
        if tail:
            rest.wait()

    return pl.pallas_call(
        kernel,
        out_shape=jax.ShapeDtypeStruct((rows_out * span, LANES), jnp.bfloat16),
        in_specs=[vmem()] * 2,
        out_specs=pl.BlockSpec(memory_space=pl.ANY),
        scratch_shapes=[
            pltpu.VMEM((tiles, kinds, LANES), jnp.float32),
            pltpu.VMEM((groups, 2, SUBLANES, LANES), jnp.float32),
            pltpu.VMEM((STEPS, block * per * span, LANES), jnp.bfloat16),
            pltpu.VMEM((SUBLANES, LANES), jnp.bfloat16),
            pltpu.SemaphoreType.DMA((PIECES * STEPS + 1,)),
        ],
        compiler_params=params(16 * 1024 * 1024),
        cost_estimate=cost(8 * 10**9, 3 * 10**6),
        name="grid_values",
    )(fourier, tables)


def direct(returned, factors, panels):
    waves, chips, packs, half, _ = returned.shape
    depth, lats = panels[0].shape
    own, here = factors.shape[2], lats // waves
    slots, full = depth // own, packs // 2
    tall = chips * 2 * half

    def kernel(x_ref, factor_ref, own_ref, other_ref, *refs):
        o_refs, left_ref, all_ref, wide_ref = refs[:chips], refs[chips], refs[chips + 1], refs[chips + 2]
        for place, j in enumerate(from_middle(waves)):
            for i in range(chips):
                for t in range(full + 1):
                    for h in range(2):
                        if t < full:
                            value = x_ref[place, i, 2 * t + h].astype(jnp.float32)
                        elif h == 0:
                            value = x_ref[place, i, 2 * t].astype(jnp.float32)
                        else:
                            value = pltpu.roll(value, LANES // 2, 1)
                        at = (2 * i + h) * half
                        wide_ref[j, at : at + half, t * LANES : (t + 1) * LANES] = value
            left_ref[:, j * here : (j + 1) * here] = wide_ref[j, :, 0:here]
        left = left_ref[...].astype(jnp.bfloat16)
        shape = (chips, half, own)
        slot_of = lax.broadcasted_iota(jnp.int32, shape, 1) // 2
        for e, panel_ref in enumerate((own_ref, other_ref)):
            total = lax.dot_general(
                left, panel_ref[...], (((1,), (1,)), ((), ())), preferred_element_type=jnp.float32
            ).reshape(chips, 2 * half, depth)
            result = jnp.zeros(shape, jnp.float32)
            for s in range(slots):
                mine = total[:, :, s * own : (s + 1) * own] * factor_ref[e][None]
                result = jnp.where(slot_of == s, mine[:, :half] + mine[:, half:], result)
            all_ref[:, e * half : (e + 1) * half, :] = result
        for i in range(chips):
            o_refs[i][...] = all_ref[(at_level() // 2) ^ i ^ turned(chips)]

    return pl.pallas_call(
        kernel,
        out_shape=(jax.ShapeDtypeStruct((2 * half, own), jnp.float32),) * chips,
        in_specs=[vmem()] * 4,
        out_specs=(vmem(),) * chips,
        scratch_shapes=[
            pltpu.VMEM((tall, lats), jnp.float32),
            pltpu.VMEM((chips, 2 * half, own), jnp.float32),
            pltpu.VMEM((waves, tall, (full + 1) * LANES), jnp.float32),
        ],
        compiler_params=params(),
        cost_estimate=cost(10**9, 2 * 10**6),
        name="direct",
    )(returned, factors, *panels)


def join_degrees(pieces, slots):
    chips = len(pieces)
    rows, own = pieces[0].shape
    half = rows // 2

    def kernel(*refs):
        piece_refs, o_ref, all_ref = refs[:chips], refs[chips], refs[chips + 1]
        for i in range(chips):
            for e in range(2):
                all_ref[at_level() ^ (2 * i + e)] = piece_refs[i][e * half : (e + 1) * half, :]
        whole = jnp.concatenate([all_ref[v] for v in range(2 * chips)], axis=1)
        for s in range(slots):
            o_ref[s] = whole[2 * s : 2 * s + 2]

    return pl.pallas_call(
        kernel,
        out_shape=jax.ShapeDtypeStruct((slots, 2, 2 * chips * own), jnp.float32),
        in_specs=[vmem()] * chips,
        out_specs=vmem(),
        scratch_shapes=[pltpu.VMEM((2 * chips, half, own), jnp.float32)],
        compiler_params=params(),
        name="join_degrees",
    )(*pieces)


def evenly_spaced(levels, spec, legendre, gauss_w, cycle_len, wave_map):
    slots = spec.shape[0]
    degrees_all = spec.shape[3]
    own = legendre.shape[1]
    lats = legendre.shape[2]
    slot_count = wave_map.shape[0]
    step = degrees_all // slot_count
    waves = slot_count // slots
    chips = levels // 2

    def across(x, bits):
        return lax.ppermute(x, "lev", [(j, j ^ bits) for j in range(levels)])

    def same_core(x):
        groups = [
            [
                wave * levels + 2 * (chip ^ turned(chips)) + core
                for wave in from_middle(waves)
                for chip in range(chips)
            ]
            for core in range(2)
        ]
        return lax.all_to_all(x, ("wave", "lev"), 0, 0, tiled=True, axis_index_groups=groups)

    mine = spec.reshape(slots, 2, degrees_all)
    others = [across(mine, 2 * i) for i in range(1, chips)]
    panel = legendre.reshape(slots * own, lats)
    signs = parity_signs(2 * slots * 2, degrees_all)
    here = lats // waves
    wide = -(-here // LANES) * LANES
    tiles = wide // LANES
    per = SUBLANES // 2
    rows_out = here // 2
    groups = -(-rows_out // (per * STEPS)) * STEPS
    span = 2 * (LPAD // LANES)
    first, factor, factors, near, tables, lens, weights, held = prepare(
        cycle_len, gauss_w, wave_map, mine, panel, signs, span, step, waves, groups, wide
    )
    panels = (near, across(panel, 1))

    part = partial_fourier(first, factor, others, panels, slots, waves)
    part = same_core(part.reshape((waves * chips,) + part.shape[2:]))
    fourier, returned = quadratic(held, part, lens, weights, waves, step)
    returned = same_core(returned)

    values = grid_values(fourier, tables, span, slot_count, rows_out, tiles)
    values = values.reshape(rows_out, span // 2, 2, LANES)
    values = with_layout_constraint(values, Layout(major_to_minor=(0, 1, 2, 3)))
    values = values.transpose(0, 2, 1, 3)
    values = with_layout_constraint(values, Layout(major_to_minor=(0, 2, 1, 3)))
    values = values.reshape(rows_out, 2, LPAD)
    values = with_layout_constraint(values, Layout(major_to_minor=(0, 1, 2)))
    grid = values.transpose(1, 0, 2).reshape(2, rows_out, 1, LPAD)

    returned = returned.reshape((waves, chips) + returned.shape[1:])
    pieces = direct(returned, factors, (panel, panels[1]))
    pieces = [pieces[0]] + [across(pieces[i], 2 * i) for i in range(1, chips)]
    spec_out = join_degrees(pieces, slots).reshape(slots, 1, 2, degrees_all)
    return (grid, spec_out)


def per_device(levels, spec, legendre, gauss_w, cycle_len, wave_map):
    slot_count = wave_map.shape[0]
    fits = (
        spec.shape[3] % slot_count == 0
        and 2 * slot_count * SUBLANES == LANES
        and spec.shape[1] == 1
        and 4 * spec.shape[0] == SUBLANES
        and levels > 1
        and 0 < legendre.shape[2] * spec.shape[0] // slot_count % LANES <= LANES // 2
        and levels & (levels - 1) == 0
    )
    if fits:
        return evenly_spaced(levels, spec, legendre, gauss_w, cycle_len, wave_map)
    return general(spec, legendre, gauss_w, cycle_len, wave_map)


def solution(mesh):
    placed = (P("wave", "lev", None, None), P("wave", "lev", None), P(), P(), P())
    return jax.shard_map(
        functools.partial(per_device, mesh.shape["lev"]),
        mesh=mesh,
        in_specs=placed,
        out_specs=(P(None, "wave", "lev", None), P("wave", "lev", None, None)),
        check_vma=False,
    )
```
